32 devices in a mesh: dp: 16 (over z, y, x), sub: 2 (over core).
Axes of the slice: x: 2, y: 2, z: 4, core: 2. Of those that a mesh axis runs over, the one named last changes fastest.
Arguments:
- inputs: bfloat16 [32768, 576], P(('dp', 'sub')), may hold values from -6 to 6
- out_grad: bfloat16 [32768, 576], P(('dp', 'sub')), may hold values from -6 to 6
- lang_tags: int32 [32], P(('dp', 'sub')), may hold values from 0 to 7
- attn_master: float32 [1536, 576], P(('dp', 'sub')), may hold values from -0.5 to 0.5
- gate_up_master: float32 [3072, 576], P(('dp', 'sub')), may hold values from -0.25 to 0.25
- down_master: float32 [1536, 576], P(('dp', 'sub')), may hold values from -0.15625 to 0.15625
- attn_momentum: float32 [1536, 576], P(('dp', 'sub')), may hold values from -2 to 2
- gate_up_momentum: float32 [3072, 576], P(('dp', 'sub')), may hold values from -2 to 2
- down_momentum: float32 [1536, 576], P(('dp', 'sub')), may hold values from -2 to 2
- norm_gains: float32 [2, 576], replicated, may hold values from 0.5 to 1.6
- gain_first: float32 [2, 576], replicated, may hold values from -0.5 to 0.5
- gain_second: float32 [2, 576], replicated, may hold values from 0.02752512 to 0.1114112
Outputs:
- outputs: bfloat16 [32768, 576], P(('dp', 'sub'))
- input_grad: bfloat16 [32768, 576], P(('dp', 'sub'))
- attn_grad: float32 [1536, 576], P(('dp', 'sub'))
- gate_up_grad: float32 [3072, 576], P(('dp', 'sub'))
- down_grad: float32 [1536, 576], P(('dp', 'sub'))
- grad_norm: float32 [], replicated
- attn_momentum_new: float32 [1536, 576], P(('dp', 'sub'))
- gate_up_momentum_new: float32 [3072, 576], P(('dp', 'sub'))
- down_momentum_new: float32 [1536, 576], P(('dp', 'sub'))
- attn_new: float32 [1536, 576], P(('dp', 'sub'))
- gate_up_new: float32 [3072, 576], P(('dp', 'sub'))
- down_new: float32 [1536, 576], P(('dp', 'sub'))
- gain_grad: float32 [2, 576], replicated
- gain_first_new: float32 [2, 576], replicated
- gain_second_new: float32 [2, 576], replicated
- norm_gains_new: float32 [2, 576], replicated
The draws below stay inside these ranges and needn't reach their ends.
All inputs are finite; a program needn't handle non-finite values.
Results may differ from the reference program's by a relative error of at most 0.015.
The reference program's roundings to bfloat16 on the way count: a program that leaves them out, or rounds other values in their place, can miss the bound.
Values may be sent and summed in bfloat16 or wider, within the bound.
No kernel may reach another device: no remote copies, remote signals or barrier semaphores. Data moves between devices by JAX's collectives and lax.ppermute only.
A program may use at most 320 MiB of HBM per device.

```python
import math
import jax
import jax.numpy as jnp
from jax import lax

D = 576
HEADS = 9
KV_HEADS = 3
HEAD_DIM = 64
FF = 1536
TOK_DEV = 1024
NUM_TAGS = 8
ORTHO_STEPS = 5
STEP_NUMBER = 10
SEQS = 32
TOKENS = 32768
ATT_ROWS = 1536
PARAMS = 3540096


def draw_lang_tags(key, part):
    key = jax.random.fold_in(key, 5)
    position = jnp.arange(SEQS, dtype=jnp.int32)
    base_tag = NUM_TAGS * position * position // (SEQS * SEQS)
    jitter = jax.random.randint(key, (SEQS,), 0, 2, dtype=jnp.int32)
    return jnp.minimum(base_tag + jitter, NUM_TAGS - 1).astype(jnp.int32)


def draw_attn_master(key, part):
    key = jax.random.fold_in(key, 11)
    q_rows = HEADS * HEAD_DIM
    kv_rows = KV_HEADS * HEAD_DIM
    row_index = jnp.arange(ATT_ROWS)
    row_scale = jnp.where(row_index < q_rows + kv_rows, 1.6 / D ** 0.5, 1.0 / D ** 0.5)
    row_scale = jnp.where(row_index >= q_rows + 2 * kv_rows, 3.0 / q_rows ** 0.5, row_scale)
    base_values = jnp.clip(jax.random.normal(key, (ATT_ROWS, D), jnp.float32), -4.0, 4.0)
    return (base_values * row_scale[:, None]).astype(jnp.float32)


def draw_norm_gains(key, part):
    key = jax.random.fold_in(key, 7)
    ramp = jnp.arange(D, dtype=jnp.float32) / (D - 1)
    base_gain = 0.75 + 0.55 * ramp
    jitter = jax.random.uniform(key, (2, D), jnp.float32, 0.9, 1.1)
    return (base_gain[None, :] * jitter).astype(jnp.float32)


def levels(rng, extent, cuts, smallest, high):
    factor_of = 1.0
    for axis_at, blocks in cuts:
        draws = jax.random.uniform(jax.random.fold_in(jax.random.fold_in(rng, 6), axis_at), (blocks,), jnp.float32, smallest / len(cuts), high / len(cuts))
        factor_of = factor_of * jnp.repeat(jnp.exp(draws), extent[axis_at] // blocks).reshape((-1,) + (1,) * (len(extent) - 1 - axis_at))
    return factor_of


def centred(key, extent, spread, bound, split=(), kind=jnp.bfloat16):
    entries = jax.random.normal(key, extent, jnp.float32) * spread
    if len(split) > 0:
        entries = levels(key, extent, split, -0.22, 0.18) * entries
    return jnp.clip(entries, min=-bound, max=bound).astype(kind)


def setup_inputs(seed: int = 0) -> dict:
    key_list = jax.random.split(jax.random.key(seed), 13)
    inputs = centred(key_list[0], (TOKENS, D), 1.0, 6.0, ((0, 32),))
    out_grad = centred(key_list[1], (TOKENS, D), 1.0, 6.0, ((0, 32),))
    lang_tags = draw_lang_tags(jax.random.fold_in(key_list[12], 71), 0)
    attn_master = draw_attn_master(jax.random.fold_in(key_list[12], 71), 0)
    gate_up_master = centred(key_list[4], (2 * FF, D), D ** -0.5, 0.25, ((0, 32),), jnp.float32)
    down_master = centred(key_list[5], (FF, D), FF ** -0.5, 0.15625, ((0, 32),), jnp.float32)
    attn_momentum = centred(key_list[6], (ATT_ROWS, D), (0.002 * TOKENS ** 0.5), 2.0, ((0, 32),), jnp.float32)
    gate_up_momentum = centred(key_list[7], (2 * FF, D), (0.002 * TOKENS ** 0.5), 2.0, ((0, 32),), jnp.float32)
    down_momentum = centred(key_list[8], (FF, D), (0.002 * TOKENS ** 0.5), 2.0, ((0, 32),), jnp.float32)
    norm_gains = draw_norm_gains(jax.random.fold_in(key_list[12], 71), 0)
    gain_first = centred(key_list[10], (2, D), (0.00044 * TOKENS ** 0.5), 0.5, (), jnp.float32)
    gain_second = jnp.clip(jnp.exp(jax.random.uniform(key_list[11], (2, D), jnp.float32, math.log(0.02752512), math.log(0.1114112))), 0.02752512, 0.1114112)
    return dict(inputs=inputs, out_grad=out_grad, lang_tags=lang_tags, attn_master=attn_master, gate_up_master=gate_up_master, down_master=down_master, attn_momentum=attn_momentum, gate_up_momentum=gate_up_momentum, down_momentum=down_momentum, norm_gains=norm_gains, gain_first=gain_first, gain_second=gain_second)


NORM_EPS = 1e-05
ROPE_BASE = 100000.0
POLY_ONE = 3.4445
POLY_TWO = -4.775
POLY_THREE = 2.0315
MOMENTUM_DECAY = 0.95
MATRIX_RATE = 0.2
MATRIX_DECAY = 0.1
GAIN_RATE = 1.0
BETA_FIRST = 0.9
BETA_SECOND = 0.95
ADAM_EPS = 1e-08
CLIP_SCALE = 0.002
HIGHEST_PRECISION = lax.Precision.HIGHEST

@jax.custom_vjp
def low(v):
    return lax.optimization_barrier(v.astype(jnp.bfloat16)).astype(jnp.float32)

@jax.custom_vjp
def low_back(v):
    return v

def low_keep(v):
    return (low(v), None)

def low_pass(kept, grad):
    return (grad,)

def back_keep(v):
    return (v, None)

def back_low(kept, grad):
    return (low(grad),)
low.defvjp(low_keep, low_pass)
low_back.defvjp(back_keep, back_low)

def settle(values):
    return lax.optimization_barrier(values.astype(jnp.bfloat16)).astype(jnp.float32)

def rms_scale(values, gain):
    return values * lax.rsqrt(lax.optimization_barrier(jnp.mean(values * values, axis=-1, keepdims=True)) + NORM_EPS) * gain

def rotary_tables(length):
    half_dim = HEAD_DIM // 2
    frequency = ROPE_BASE ** (-(jnp.arange(half_dim, dtype=jnp.float32) * 2.0 / HEAD_DIM))
    angles = jnp.arange(length, dtype=jnp.float32)[:, None] * frequency[None, :]
    return (jnp.cos(angles), jnp.sin(angles))

def rotate(tensor, cosine, sine_table):
    half_dim = tensor.shape[-1] // 2
    first_half = tensor[..., :half_dim]
    second_half = tensor[..., half_dim:]
    return jnp.concatenate([first_half * cosine - second_half * sine_table, second_half * cosine + first_half * sine_table], axis=-1)

def attend_sequence(items):
    queries, keys, values = items
    group_size = HEADS // KV_HEADS
    key_full = jnp.repeat(keys, group_size, axis=1)
    value_full = jnp.repeat(values, group_size, axis=1)
    scores = low_back(jnp.einsum('qhd,khd->hqk', queries, key_full, precision=HIGHEST_PRECISION) * HEAD_DIM ** (-0.5))
    length = queries.shape[0]
    query_pos = jnp.arange(length)[:, None]
    key_pos = jnp.arange(length)[None, :]
    scores = jnp.where(key_pos <= query_pos, scores, -1e+30)
    weights = low(jax.nn.softmax(scores, axis=-1))
    return jnp.einsum('hqk,khd->qhd', weights, value_full, precision=HIGHEST_PRECISION)

def layer(hidden_in, attn_weights, gate_up_weights, down_weights, norm_gains):
    q_rows = HEADS * HEAD_DIM
    kv_rows = KV_HEADS * HEAD_DIM
    batch_seqs = hidden_in.shape[0]
    length = hidden_in.shape[1]
    normed_one = low(rms_scale(hidden_in, norm_gains[0]))
    proj_q = low_back(jnp.einsum('nld,cd->nlc', normed_one, attn_weights[:q_rows], precision=HIGHEST_PRECISION))
    proj_k = low_back(jnp.einsum('nld,cd->nlc', normed_one, attn_weights[q_rows:q_rows + kv_rows], precision=HIGHEST_PRECISION))
    proj_v = low(low_back(jnp.einsum('nld,cd->nlc', normed_one, attn_weights[q_rows + kv_rows:q_rows + 2 * kv_rows], precision=HIGHEST_PRECISION)))
    cosine, sine_table = rotary_tables(length)
    cosine = cosine[:, None, :]
    sine_table = sine_table[:, None, :]
    queries = low(rotate(proj_q.reshape(batch_seqs, length, HEADS, HEAD_DIM), cosine, sine_table))
    keys = low(rotate(proj_k.reshape(batch_seqs, length, KV_HEADS, HEAD_DIM), cosine, sine_table))
    values = proj_v.reshape(batch_seqs, length, KV_HEADS, HEAD_DIM)
    attended = lax.map(jax.checkpoint(attend_sequence), (queries, keys, values))
    attended = low(low_back(attended.reshape(batch_seqs, length, q_rows)))
    residual = hidden_in + low_back(jnp.einsum('nlc,cd->nld', attended, attn_weights[q_rows + 2 * kv_rows:], precision=HIGHEST_PRECISION))
    normed_two = low(rms_scale(residual, norm_gains[1]))
    gate_values = low_back(jnp.einsum('nld,fd->nlf', normed_two, gate_up_weights[:FF], precision=HIGHEST_PRECISION))
    up_values = low_back(jnp.einsum('nld,fd->nlf', normed_two, gate_up_weights[FF:], precision=HIGHEST_PRECISION))
    activation = low(jax.nn.silu(gate_values) * up_values)
    return residual + low_back(jnp.einsum('nlf,fd->nld', activation, down_weights, precision=HIGHEST_PRECISION))

def block_list():
    q_rows = HEADS * HEAD_DIM
    kv_rows = KV_HEADS * HEAD_DIM
    return ((0, 0, q_rows), (0, q_rows, kv_rows), (0, q_rows + kv_rows, kv_rows), (0, q_rows + 2 * kv_rows, q_rows), (1, 0, FF), (1, FF, FF), (2, 0, FF))

def orthogonalize(block):
    scaled = block / (jnp.sqrt(jnp.sum(block * block)) + 1e-07)
    for sweep_index in range(ORTHO_STEPS):
        if block.shape[0] <= block.shape[1]:
            gram = jnp.dot(scaled, scaled.T, precision=HIGHEST_PRECISION, preferred_element_type=jnp.float32)
            poly = POLY_TWO * gram + POLY_THREE * jnp.dot(gram, gram, precision=HIGHEST_PRECISION, preferred_element_type=jnp.float32)
            scaled = POLY_ONE * scaled + jnp.dot(poly, scaled, precision=HIGHEST_PRECISION, preferred_element_type=jnp.float32)
        else:
            gram = jnp.dot(scaled.T, scaled, precision=HIGHEST_PRECISION, preferred_element_type=jnp.float32)
            poly = POLY_TWO * gram + POLY_THREE * jnp.dot(gram, gram, precision=HIGHEST_PRECISION, preferred_element_type=jnp.float32)
            scaled = POLY_ONE * scaled + jnp.dot(scaled, poly, precision=HIGHEST_PRECISION, preferred_element_type=jnp.float32)
    return scaled

def update_arrays(masters, moments):
    results = []
    for array_id in range(3):
        pieces = []
        for owner_id, row_start, row_count in block_list():
            if owner_id == array_id:
                block = settle(moments[array_id][row_start:row_start + row_count])
                ortho = settle(orthogonalize(block))
                pieces.append(0.2 * math.sqrt(max(row_count, D)) * ortho)
        step_rows = jnp.concatenate(pieces, axis=0)
        results.append(masters[array_id] - MATRIX_RATE * (step_rows + MATRIX_DECAY * masters[array_id]))
    return tuple(results)

def reference(inputs, out_grad, lang_tags, attn_master, gate_up_master, down_master, attn_momentum, gate_up_momentum, down_momentum, norm_gains, gain_first, gain_second):
    seq_total = lang_tags.shape[0]
    tag_hot = (lang_tags[:, None] == jnp.arange(NUM_TAGS, dtype=jnp.int32)[None, :]).astype(jnp.float32)
    tag_count = lax.optimization_barrier(jnp.sum(tag_hot, axis=0))
    seq_weight = seq_total / (NUM_TAGS * lax.optimization_barrier(jnp.sum(tag_hot * tag_count[None, :], axis=1)))
    masters = (attn_master, gate_up_master, down_master)
    rounded = tuple((settle(master) for master in masters))
    round_seqs = min(seq_total, max(1, 4096 // TOK_DEV))
    round_count = seq_total // round_seqs
    hidden_all = inputs.astype(jnp.float32).reshape(round_count, round_seqs, TOK_DEV, D)
    upstream = out_grad.astype(jnp.float32).reshape(seq_total, TOK_DEV, D) * seq_weight[:, None, None]
    upstream = upstream.reshape(round_count, round_seqs, TOK_DEV, D)

    def one_round(carry, item):
        hidden_part, upstream_part = item
        result, pull = jax.vjp(layer, hidden_part, rounded[0], rounded[1], rounded[2], norm_gains)
        input_part, attn_part, gate_up_part, down_part, gain_part = pull(upstream_part)
        carry = (carry[0] + attn_part, carry[1] + gate_up_part, carry[2] + down_part, carry[3] + gain_part)
        return (carry, (result.astype(jnp.bfloat16), input_part.astype(jnp.bfloat16)))
    start_sums = (jnp.zeros(attn_master.shape, jnp.float32), jnp.zeros(gate_up_master.shape, jnp.float32), jnp.zeros(down_master.shape, jnp.float32), jnp.zeros(norm_gains.shape, jnp.float32))
    sums, (results, input_parts) = lax.scan(one_round, start_sums, (hidden_all, upstream))
    outputs = results.reshape(TOKENS, D)
    input_grad = input_parts.reshape(TOKENS, D)
    square_total = jnp.sum(sums[0] * sums[0]) + jnp.sum(sums[1] * sums[1]) + jnp.sum(sums[2] * sums[2]) + jnp.sum(sums[3] * sums[3])
    grad_norm = jnp.sqrt(square_total)
    factor = jnp.minimum(1.0, CLIP_SCALE * math.sqrt(TOKENS * PARAMS) / grad_norm)
    attn_grad = sums[0] * factor
    gate_up_grad = sums[1] * factor
    down_grad = sums[2] * factor
    gain_grad = sums[3] * factor
    moments_new = (MOMENTUM_DECAY * attn_momentum + attn_grad, MOMENTUM_DECAY * gate_up_momentum + gate_up_grad, MOMENTUM_DECAY * down_momentum + down_grad)
    attn_new, gate_up_new, down_new = update_arrays(masters, moments_new)
    first_new = BETA_FIRST * gain_first + (1.0 - BETA_FIRST) * gain_grad
    second_new = BETA_SECOND * gain_second + (1.0 - BETA_SECOND) * gain_grad * gain_grad
    gains_new = norm_gains - GAIN_RATE * (first_new / (1.0 - BETA_FIRST ** STEP_NUMBER)) / (jnp.sqrt(second_new / (1.0 - BETA_SECOND ** STEP_NUMBER)) + ADAM_EPS)
    return (outputs, input_grad, attn_grad, gate_up_grad, down_grad, grad_norm, moments_new[0], moments_new[1], moments_new[2], attn_new, gate_up_new, down_new, gain_grad, first_new, second_new, gains_new)
```

```python
from functools import partial
import math

import jax
import jax.numpy as jnp
from jax import lax
from jax.sharding import PartitionSpec as P

D = 576
HEADS = 9
KV_HEADS = 3
HEAD_DIM = 64
FF = 1536
NUM_TAGS = 8
ORTHO_STEPS = 5
STEP_NUMBER = 10


NORM_EPS = 1e-05
ROPE_BASE = 100000.0
POLY_ONE = 3.4445
POLY_TWO = -4.775
POLY_THREE = 2.0315
MOMENTUM_DECAY = 0.95
MATRIX_RATE = 0.2
MATRIX_DECAY = 0.1
GAIN_RATE = 1.0
BETA_FIRST = 0.9
BETA_SECOND = 0.95
ADAM_EPS = 1e-08
CLIP_SCALE = 0.002
HIGHEST_PRECISION = lax.Precision.HIGHEST


AXES = ("dp", "sub")


def bit_of(place, bit):
    return (place >> bit) & 1


def swap(array, bit, devices, only=None):
    pairs = [(i, i ^ (1 << bit)) for i in range(devices) if only is None or only(i)]
    return lax.ppermute(array, AXES, pairs)


def ordered(mine, own, other, axis):
    first = jnp.where(mine == 0, own, other)
    second = jnp.where(mine == 0, other, own)
    return jnp.stack([first, second], axis=axis)


def gather_rows(rows, place, devices):
    blocks = rows[None]
    for bit in reversed(range(devices.bit_length() - 1)):
        other = swap(blocks, bit, devices)
        blocks = ordered(bit_of(place, bit), blocks, other, 1)
        blocks = blocks.reshape((-1,) + rows.shape)
    return blocks


def pick(array, axis, index):
    return lax.dynamic_index_in_dim(array, index, axis, keepdims=False)


def scatter_sums(parts, place, devices, extra=None):
    width = parts[0].shape[-1]
    sizes = [part.shape[0] // devices for part in parts]
    kept = [part.reshape(devices, size, width) for part, size in zip(parts, sizes)]
    for bit in range(devices.bit_length() - 1):
        mine = bit_of(place, bit)
        halves = [part.reshape(part.shape[0] // 2, 2, part.shape[1], width) for part in kept]
        message = [pick(half, 1, 1 - mine).astype(jnp.bfloat16) for half in halves]
        message = jnp.concatenate(message, axis=1).reshape(-1, width)
        if extra is not None:
            high = lax.reduce_precision(extra, 8, 7)
            message = jnp.concatenate(
                [message, high.astype(jnp.bfloat16), (extra - high).astype(jnp.bfloat16)], axis=0
            )
        message = swap(message, bit, devices).astype(jnp.float32)
        if extra is not None:
            count = extra.shape[0]
            extra = extra + (message[-2 * count : -count] + message[-count:])
            message = message[: -2 * count]
        message = message.reshape(halves[0].shape[0], sum(sizes), width)
        start = 0
        kept = []
        for half, size in zip(halves, sizes):
            kept.append(pick(half, 1, mine) + message[:, start : start + size])
            start += size
    return [part[0] for part in kept], extra


def sum_small(value, devices):
    for bit in reversed(range(devices.bit_length() - 1)):
        value = value + swap(value, bit, devices)
    return value


def rotary_tables(length):
    half_dim = HEAD_DIM // 2
    frequency = ROPE_BASE ** (-(jnp.arange(half_dim, dtype=jnp.float32) * 2.0 / HEAD_DIM))
    angles = jnp.arange(length, dtype=jnp.float32)[:, None] * frequency[None, :]
    return (jnp.cos(angles), jnp.sin(angles))


def rotate(tensor, cosine, sine_table):
    half_dim = tensor.shape[-1] // 2
    first_half = tensor[..., :half_dim]
    second_half = tensor[..., half_dim:]
    return jnp.concatenate(
        [
            first_half * cosine - second_half * sine_table,
            second_half * cosine + first_half * sine_table,
        ],
        axis=-1,
    )


def rotate_back(tensor, cosine, sine_table):
    half_dim = tensor.shape[-1] // 2
    first_half = tensor[..., :half_dim]
    second_half = tensor[..., half_dim:]
    return jnp.concatenate(
        [
            first_half * cosine + second_half * sine_table,
            second_half * cosine - first_half * sine_table,
        ],
        axis=-1,
    )


def norm_forward(values, gain):
    inverse = lax.rsqrt(jnp.mean(values * values, axis=-1, keepdims=True) + NORM_EPS)
    return (values * inverse * gain, inverse)


def norm_backward(values, inverse, gain, grad_in):
    scaled = grad_in * gain
    gain_part = jnp.sum(grad_in * values * inverse, axis=0)
    back = inverse * scaled - values * (inverse * inverse * inverse) * jnp.mean(
        scaled * values, axis=-1, keepdims=True
    )
    return (back, gain_part)


def dot_rows(left, right):
    return lax.dot_general(
        left, right, (((1,), (1,)), ((), ())), preferred_element_type=jnp.float32
    )


def dot_cols(left, right):
    return lax.dot_general(
        left, right, (((0,), (0,)), ((), ())), preferred_element_type=jnp.float32
    )


def masked_scores(query_part, key_part, block_start):
    raw = jnp.einsum(
        "qgd,td->gqt", query_part, key_part, preferred_element_type=jnp.float32
    ) * HEAD_DIM ** (-0.5)
    query_pos = block_start + jnp.arange(query_part.shape[0])[:, None]
    key_pos = jnp.arange(key_part.shape[0])[None, :]
    return jnp.where(key_pos <= query_pos, raw, -1e30)


def attention_forward(queries, keys, values):
    length = queries.shape[0]
    block_rows = min(512, length)
    group_size = HEADS // KV_HEADS
    query_heads = queries.reshape(length, KV_HEADS, group_size, HEAD_DIM)
    key_heads = keys.reshape(length, KV_HEADS, HEAD_DIM)
    value_heads = values.reshape(length, KV_HEADS, HEAD_DIM)
    block_outs = []
    row_stats = []
    for block_start in range(0, length, block_rows):
        block_end = block_start + block_rows
        per_head = []
        for head_index in range(KV_HEADS):
            scores = masked_scores(
                query_heads[block_start:block_end, head_index],
                key_heads[:block_end, head_index],
                block_start,
            )
            row_peak = jnp.max(scores, axis=-1, keepdims=True)
            shifted = jnp.exp(scores - row_peak)
            row_total = jnp.sum(shifted, axis=-1, keepdims=True)
            prob_low = (shifted / row_total).astype(jnp.bfloat16)
            per_head.append(
                jnp.einsum(
                    "gqt,td->qgd",
                    prob_low,
                    value_heads[:block_end, head_index],
                    preferred_element_type=jnp.float32,
                )
            )
            row_stats.append((row_peak, row_total))
        block_outs.append(jnp.stack(per_head, axis=1))
    return (jnp.concatenate(block_outs, axis=0).reshape(length, HEADS * HEAD_DIM), row_stats)


def attention_backward(queries, keys, values, attended_grad, row_stats):
    length = queries.shape[0]
    block_rows = min(512, length)
    group_size = HEADS // KV_HEADS
    score_scale = HEAD_DIM ** (-0.5)
    query_heads = queries.reshape(length, KV_HEADS, group_size, HEAD_DIM)
    key_heads = keys.reshape(length, KV_HEADS, HEAD_DIM)
    value_heads = values.reshape(length, KV_HEADS, HEAD_DIM)
    grad_heads = attended_grad.reshape(length, KV_HEADS, group_size, HEAD_DIM)
    key_grad = jnp.zeros((length, KV_HEADS, HEAD_DIM), jnp.float32)
    value_grad = jnp.zeros((length, KV_HEADS, HEAD_DIM), jnp.float32)
    query_blocks = []
    counter = 0
    for block_start in range(0, length, block_rows):
        block_end = block_start + block_rows
        per_head = []
        for head_index in range(KV_HEADS):
            query_part = query_heads[block_start:block_end, head_index]
            key_part = key_heads[:block_end, head_index]
            value_part = value_heads[:block_end, head_index]
            grad_part = grad_heads[block_start:block_end, head_index]
            row_peak, row_total = row_stats[counter]
            counter += 1
            scores = masked_scores(query_part, key_part, block_start)
            prob_values = jnp.exp(scores - row_peak) / row_total
            prob_low = prob_values.astype(jnp.bfloat16)
            prob_grad = jnp.einsum(
                "qgd,td->gqt", grad_part, value_part, preferred_element_type=jnp.float32
            )
            score_grad = (
                prob_values * (prob_grad - jnp.sum(prob_values * prob_grad, axis=-1, keepdims=True))
            ).astype(jnp.bfloat16)
            per_head.append(
                jnp.einsum("gqt,td->qgd", score_grad, key_part, preferred_element_type=jnp.float32)
                * score_scale
            )
            key_grad = key_grad.at[:block_end, head_index].add(
                jnp.einsum(
                    "gqt,qgd->td", score_grad, query_part, preferred_element_type=jnp.float32
                )
                * score_scale
            )
            value_grad = value_grad.at[:block_end, head_index].add(
                jnp.einsum("gqt,qgd->td", prob_low, grad_part, preferred_element_type=jnp.float32)
            )
        query_blocks.append(jnp.stack(per_head, axis=1))
    query_grad = jnp.concatenate(query_blocks, axis=0).reshape(length, HEADS, HEAD_DIM)
    return (query_grad, key_grad, value_grad.reshape(length, KV_HEADS * HEAD_DIM))


def block_list():
    q_rows = HEADS * HEAD_DIM
    kv_rows = KV_HEADS * HEAD_DIM
    return (
        (0, 0, q_rows),
        (0, q_rows, kv_rows),
        (0, q_rows + kv_rows, kv_rows),
        (0, q_rows + 2 * kv_rows, q_rows),
        (1, 0, FF),
        (1, FF, FF),
        (2, 0, FF),
    )


def row_scales(array_id):
    pieces = [
        jnp.full((row_count,), 0.2 * math.sqrt(max(row_count, D)), jnp.float32)
        for owner_id, row_start, row_count in block_list()
        if owner_id == array_id
    ]
    return jnp.concatenate(pieces, axis=0)


def bf16_dot(left, right, dims):
    return lax.dot_general(
        left.astype(jnp.bfloat16),
        right.astype(jnp.bfloat16),
        (dims, ((), ())),
        preferred_element_type=jnp.float32,
    )


def orthogonalize(block):
    size = min(block.shape)
    left = block.shape[0] < block.shape[1]
    eye = jnp.eye(size, dtype=jnp.float32)
    scaled = block / (jnp.sqrt(jnp.sum(block * block)) + 1e-07)
    for sweep_index in range(ORTHO_STEPS):
        side = ((1,), (1,)) if left else ((0,), (0,))
        gram = bf16_dot(scaled, scaled, side)
        mean = jnp.sum(gram * eye) / size
        rest = gram - mean * eye
        poly = (POLY_TWO + 2.0 * POLY_THREE * mean) * rest + POLY_THREE * bf16_dot(
            rest, rest, ((1,), (0,))
        )
        turned = (
            bf16_dot(poly, scaled, ((1,), (0,))) if left else bf16_dot(scaled, poly, ((1,), (0,)))
        )
        scaled = (POLY_ONE + POLY_TWO * mean + POLY_THREE * mean * mean) * scaled + turned
    return scaled.astype(jnp.bfloat16)


def orthogonal_rows(attn_low, gate_up_low, down_low, place, devices):
    q_rows = HEADS * HEAD_DIM
    kv_rows = KV_HEADS * HEAD_DIM
    bits = devices.bit_length() - 1
    top_bit = bits - 1
    core, across, top = bit_of(place, 0), bit_of(place, 1), bit_of(place, top_bit)
    rows = attn_low.shape[0]
    other = swap(jnp.where(top == 0, attn_low, down_low), top_bit, devices)
    third = ordered(top, jnp.where(top == 0, down_low, attn_low), other, 0).reshape(2 * rows, D)
    other = swap(jnp.where(across == 0, third, gate_up_low), 1, devices)
    blocks = ordered(across, jnp.where(across == 0, gate_up_low, third), other, 0)
    middle = list(range(2, top_bit))
    for bit in middle + [0]:
        other = swap(blocks, bit, devices)
        blocks = ordered(bit_of(place, bit), blocks, other, 0)
    spot = core * (devices // 8) + ((place >> 2) & (devices // 8 - 1))

    def whole(blocks):
        result = orthogonalize(blocks.reshape(-1, D).astype(jnp.float32))
        return pick(result.reshape(devices // 4, 2, 2 * rows, D), 0, spot)

    def natural(blocks, half):
        lead = blocks.reshape(2, devices // 8, 2, 2, rows, D)[:, :, :, half]
        return lead.transpose(1, 2, 0, 3, 4).reshape(-1, D).astype(jnp.float32)

    def placed(first, second):
        result = jnp.concatenate([first, second], axis=0)
        result = pick(result.reshape(devices // 8, 2, 2, rows, D), 0, (place >> 2) & (devices // 8 - 1))
        return result.reshape(2, 2 * rows, D)

    def query_key(blocks):
        block = natural(blocks, 0)
        return placed(orthogonalize(block[:q_rows]), orthogonalize(block[q_rows:]))

    def value_out(blocks):
        block = natural(blocks, 1)
        return placed(orthogonalize(block[:kv_rows]), orthogonalize(block[kv_rows:]))

    is_attn = (top == 1) & (across == 1)
    result = lax.switch(
        jnp.where(is_attn, 1 + core, 0), [whole, query_key, value_out], blocks
    )
    by_core = result.reshape(2, 2, rows, D)
    other = swap(
        pick(by_core, 1, 1 - core), 0, devices, lambda i: (i >> 1) & 1 == 1 and i >> top_bit == 1
    )
    joined = ordered(core, pick(by_core, 1, core), other, 1)
    by_top = jnp.where(is_attn, joined, by_core)
    other = swap(pick(by_top, 1, 1 - top), top_bit, devices, lambda i: (i >> 1) & 1 == 1)
    own = pick(by_top, 1, top)
    down_rows = jnp.where(top == 0, own, other)
    attn_rows = jnp.where(top == 0, other, own)
    result = by_top.reshape(2, 2 * rows, D)
    other = swap(
        jnp.where(across == 0, result[1], jnp.concatenate([down_rows[0], attn_rows[0]], axis=0)),
        1,
        devices,
    )
    return (
        jnp.where(across == 0, other[rows:], attn_rows[1]),
        jnp.where(across == 0, result[0], other),
        jnp.where(across == 0, other[:rows], down_rows[1]),
    )


def per_device(
    inputs,
    out_grad,
    lang_tags,
    attn_master,
    gate_up_master,
    down_master,
    attn_momentum,
    gate_up_momentum,
    down_momentum,
    norm_gains,
    gain_first,
    gain_second,
):
    devices = lax.axis_size(("dp", "sub"))
    device_place = lax.axis_index(("dp", "sub"))
    q_rows = HEADS * HEAD_DIM
    kv_rows = KV_HEADS * HEAD_DIM
    qkv_rows = q_rows + 2 * kv_rows
    tag_hot = (lang_tags[:, None] == jnp.arange(NUM_TAGS, dtype=jnp.int32)[None, :]).astype(
        jnp.float32
    )
    masters = (attn_master, gate_up_master, down_master)
    attn_low = attn_master.astype(jnp.bfloat16)
    gate_up_low = gate_up_master.astype(jnp.bfloat16)
    down_low = down_master.astype(jnp.bfloat16)
    tag_rows = jnp.pad(jnp.sum(tag_hot, axis=0)[None], ((0, 15), (0, D - NUM_TAGS)))
    attn_weights = gather_rows(attn_low, device_place, devices).reshape(-1, D)
    ffn_low = jnp.concatenate([gate_up_low, down_low, tag_rows.astype(jnp.bfloat16)], axis=0)
    ffn_weights = lax.all_gather(ffn_low, AXES, axis=0)
    ffn_rows = gate_up_low.shape[0] + down_low.shape[0]
    gate_up_weights = ffn_weights[:, : gate_up_low.shape[0]].reshape(-1, D)
    down_weights = ffn_weights[:, gate_up_low.shape[0] : ffn_rows].reshape(-1, D)
    tag_count = jnp.sum(ffn_weights[:, ffn_rows, :NUM_TAGS].astype(jnp.float32), axis=0)
    seq_weight = (
        devices * lang_tags.shape[0] / (NUM_TAGS * jnp.sum(tag_hot * tag_count[None, :], axis=1))
    )
    hidden_in = inputs.astype(jnp.float32)
    length = hidden_in.shape[0]
    norm_one, inverse_one = norm_forward(hidden_in, norm_gains[0])
    normed_one = norm_one.astype(jnp.bfloat16)
    projected = dot_rows(normed_one, attn_weights[:qkv_rows])
    cosine, sine_table = rotary_tables(length)
    cosine = cosine[:, None, :]
    sine_table = sine_table[:, None, :]
    queries = (
        rotate(projected[:, :q_rows].reshape(length, HEADS, HEAD_DIM), cosine, sine_table)
        .reshape(length, q_rows)
        .astype(jnp.bfloat16)
    )
    keys_rot = (
        rotate(
            projected[:, q_rows : q_rows + kv_rows].reshape(length, KV_HEADS, HEAD_DIM),
            cosine,
            sine_table,
        )
        .reshape(length, kv_rows)
        .astype(jnp.bfloat16)
    )
    values_low = projected[:, q_rows + kv_rows :].astype(jnp.bfloat16)
    attended, row_stats = attention_forward(queries, keys_rot, values_low)
    attended_low = attended.astype(jnp.bfloat16)
    residual = hidden_in + jnp.dot(
        attended_low, attn_weights[qkv_rows:], preferred_element_type=jnp.float32
    )
    norm_two, inverse_two = norm_forward(residual, norm_gains[1])
    normed_two = norm_two.astype(jnp.bfloat16)
    gate_up_values = dot_rows(normed_two, gate_up_weights)
    gate_values = gate_up_values[:, :FF]
    up_values = gate_up_values[:, FF:]
    sigmoid_gate = jax.nn.sigmoid(gate_values)
    silu_gate = gate_values * sigmoid_gate
    activation = (silu_gate * up_values).astype(jnp.bfloat16)
    result = residual + jnp.dot(activation, down_weights, preferred_element_type=jnp.float32)
    outputs = result.astype(jnp.bfloat16)
    upstream = out_grad.astype(jnp.float32) * seq_weight[0]
    upstream_low = upstream.astype(jnp.bfloat16)
    down_part = dot_cols(activation, upstream_low)
    act_grad = dot_rows(upstream_low, down_weights)
    gate_grad = act_grad * up_values * (sigmoid_gate * (1.0 + gate_values * (1.0 - sigmoid_gate)))
    up_grad = act_grad * silu_gate
    gate_up_low_grad = jnp.concatenate([gate_grad, up_grad], axis=1).astype(jnp.bfloat16)
    gate_up_part = dot_cols(gate_up_low_grad, normed_two)
    normed_two_grad = jnp.dot(gate_up_low_grad, gate_up_weights, preferred_element_type=jnp.float32)
    (gate_up_sum, down_sum), _ = scatter_sums([gate_up_part, down_part], device_place, devices)
    norm_two_back, gain_two = norm_backward(residual, inverse_two, norm_gains[1], normed_two_grad)
    residual_grad = upstream + norm_two_back
    branch_low = residual_grad.astype(jnp.bfloat16)
    o_part = dot_cols(attended_low, branch_low)
    attended_grad = dot_rows(branch_low, attn_weights[qkv_rows:]).astype(jnp.bfloat16)
    query_grad, key_grad, value_grad = attention_backward(
        queries, keys_rot, values_low, attended_grad, row_stats
    )
    query_back = rotate_back(query_grad, cosine, sine_table).reshape(length, q_rows)
    key_back = rotate_back(key_grad, cosine, sine_table).reshape(length, kv_rows)
    proj_grad = jnp.concatenate([query_back, key_back, value_grad], axis=1).astype(jnp.bfloat16)
    qkv_part = dot_cols(proj_grad, normed_one)
    normed_one_grad = jnp.dot(
        proj_grad, attn_weights[:qkv_rows], preferred_element_type=jnp.float32
    )
    norm_one_back, gain_one = norm_backward(hidden_in, inverse_one, norm_gains[0], normed_one_grad)
    input_grad = (residual_grad + norm_one_back).astype(jnp.bfloat16)
    gain_part = jnp.stack([gain_one, gain_two], axis=0)
    attn_term = jnp.concatenate([qkv_part, o_part], axis=0)
    (attn_sum,), gain_total = scatter_sums([attn_term], device_place, devices, gain_part)
    squares = (
        jnp.sum(attn_sum * attn_sum)
        + jnp.sum(gate_up_sum * gate_up_sum)
        + jnp.sum(down_sum * down_sum)
    )
    squares = sum_small(jnp.full((8, 128), squares), devices)[0, 0]
    square_total = squares + jnp.sum(gain_total * gain_total)
    grad_norm = jnp.sqrt(square_total)
    param_count = (qkv_rows + q_rows + 3 * FF) * D + 2 * D
    factor = jnp.minimum(1.0, CLIP_SCALE * math.sqrt(devices * length * param_count) / grad_norm)
    attn_grad = attn_sum * factor
    gate_up_grad = gate_up_sum * factor
    down_grad = down_sum * factor
    gain_grad = gain_total * factor
    attn_moment = MOMENTUM_DECAY * attn_momentum + attn_grad
    gate_up_moment = MOMENTUM_DECAY * gate_up_momentum + gate_up_grad
    down_moment = MOMENTUM_DECAY * down_momentum + down_grad
    ortho_shards = orthogonal_rows(
        attn_moment.astype(jnp.bfloat16),
        gate_up_moment.astype(jnp.bfloat16),
        down_moment.astype(jnp.bfloat16),
        device_place,
        devices,
    )
    new_masters = []
    for array_id in range(3):
        shard_rows = masters[array_id].shape[0]
        scale_rows = lax.dynamic_slice_in_dim(
            row_scales(array_id), device_place * shard_rows, shard_rows, 0
        )
        new_masters.append(
            masters[array_id]
            - MATRIX_RATE
            * (scale_rows[:, None] * ortho_shards[array_id] + MATRIX_DECAY * masters[array_id])
        )
    first_new = BETA_FIRST * gain_first + (1.0 - BETA_FIRST) * gain_grad
    second_new = BETA_SECOND * gain_second + (1.0 - BETA_SECOND) * gain_grad * gain_grad
    gains_new = norm_gains - GAIN_RATE * (first_new / (1.0 - BETA_FIRST**STEP_NUMBER)) / (
        jnp.sqrt(second_new / (1.0 - BETA_SECOND**STEP_NUMBER)) + ADAM_EPS
    )
    return (
        outputs,
        input_grad,
        attn_grad,
        gate_up_grad,
        down_grad,
        grad_norm,
        attn_moment,
        gate_up_moment,
        down_moment,
        new_masters[0],
        new_masters[1],
        new_masters[2],
        gain_grad,
        first_new,
        second_new,
        gains_new,
    )


def solution(mesh):
    placed = (
        P(("dp", "sub"), None),
        P(("dp", "sub"), None),
        P(("dp", "sub")),
        P(("dp", "sub"), None),
        P(("dp", "sub"), None),
        P(("dp", "sub"), None),
        P(("dp", "sub"), None),
        P(("dp", "sub"), None),
        P(("dp", "sub"), None),
        P(),
        P(),
        P(),
    )
    return jax.shard_map(
        per_device,
        mesh=mesh,
        in_specs=placed,
        out_specs=(
            P(("dp", "sub"), None),
            P(("dp", "sub"), None),
            P(("dp", "sub"), None),
            P(("dp", "sub"), None),
            P(("dp", "sub"), None),
            P(),
            P(("dp", "sub"), None),
            P(("dp", "sub"), None),
            P(("dp", "sub"), None),
            P(("dp", "sub"), None),
            P(("dp", "sub"), None),
            P(("dp", "sub"), None),
            P(),
            P(),
            P(),
            P(),
        ),
        check_vma=False,
    )
```

```python
from functools import partial
import math

import jax
import jax.numpy as jnp
import numpy as np
from jax import lax
from jax.experimental import pallas as pl
from jax.experimental.pallas import tpu as pltpu
from jax.sharding import PartitionSpec as P

D = 576
HEADS = 9
KV_HEADS = 3
HEAD_DIM = 64
FF = 1536
NUM_TAGS = 8
ORTHO_STEPS = 5
STEP_NUMBER = 10


NORM_EPS = 1e-05
ROPE_BASE = 100000.0
POLY_ONE = 3.4445
POLY_TWO = -4.775
POLY_THREE = 2.0315
MOMENTUM_DECAY = 0.95
MATRIX_RATE = 0.2
MATRIX_DECAY = 0.1
GAIN_RATE = 1.0
BETA_FIRST = 0.9
BETA_SECOND = 0.95
ADAM_EPS = 1e-08
CLIP_SCALE = 0.002
VMEM_BYTES = 56 * 2**20


AXES = ("dp", "sub")


def bit_of(place, bit):
    return (place >> bit) & 1


def swap(array, bit, devices, only=None):
    pairs = [(i, i ^ (1 << bit)) for i in range(devices) if only is None or only(i)]
    return lax.ppermute(array, AXES, pairs)


def ordered(mine, own, other, axis):
    first = jnp.where(mine == 0, own, other)
    second = jnp.where(mine == 0, other, own)
    return jnp.stack([first, second], axis=axis)


def gather_rows(rows, place, devices):
    blocks = rows[None]
    for bit in reversed(range(devices.bit_length() - 1)):
        other = swap(blocks, bit, devices)
        blocks = ordered(bit_of(place, bit), blocks, other, 1)
        blocks = blocks.reshape((-1,) + rows.shape)
    return blocks


def pick(array, axis, index):
    return lax.dynamic_index_in_dim(array, index, axis, keepdims=False)


def halve(held, came, axis, mine):
    if came is None:
        return pick(held, axis, mine), pick(held, axis, 1 - mine).astype(jnp.bfloat16)
    came = came.reshape(held.shape)
    kept = pick(held, axis, mine) + pick(came, axis, mine).astype(jnp.float32)
    sent = pick(held, axis, 1 - mine) + pick(came, axis, 1 - mine).astype(jnp.float32)
    return kept, sent.astype(jnp.bfloat16)


class Sums:
    def __init__(self, held, place, devices, bits, came=None):
        self.place, self.devices, self.bits = place, devices, list(bits)
        self.shape = held.shape[-2:]
        self.held = held.reshape((2,) * len(self.bits) + self.shape)
        self.came = came

    def hop(self, bit):
        axis = len(self.bits) - 1 - self.bits.index(bit)
        self.held, sent = halve(self.held, self.came, axis, bit_of(self.place, bit))
        self.bits.remove(bit)
        self.came = swap(sent.reshape((-1,) + self.shape), bit, self.devices)

    def total(self):
        return self.held + self.came.reshape(self.held.shape).astype(jnp.float32)


def after(value, sums):
    value, *came = lax.optimization_barrier((value, *[s.came for s in sums]))
    for s, c in zip(sums, came):
        s.came = c
    return value


def sum_small(value, devices):
    for bit in reversed(range(devices.bit_length() - 1)):
        value = value + swap(value, bit, devices)
    return value


SCORE_SCALE = HEAD_DIM ** (-0.5)
MASKED = -1e30


def product(left, right, left_dim, right_dim):
    return lax.dot_general(
        left, right, (((left_dim,), (right_dim,)), ((), ())), preferred_element_type=jnp.float32
    )


def call(kernel, outs, args, flops, grid=(), in_specs=None, out_specs=None, scratch=()):
    specs = {} if in_specs is None else dict(in_specs=in_specs, out_specs=out_specs)
    listed = tuple(outs) if isinstance(outs, (tuple, list)) else (outs,)
    moved = sum(math.prod(a.shape) * a.dtype.itemsize for a in tuple(args) + listed)
    return pl.pallas_call(
        kernel,
        out_shape=outs,
        grid=grid,
        scratch_shapes=scratch,
        compiler_params=pltpu.CompilerParams(vmem_limit_bytes=VMEM_BYTES),
        cost_estimate=pl.CostEstimate(flops=int(flops), bytes_accessed=moved, transcendentals=0),
        **specs,
    )(*args)


def shape_of(shape, dtype):
    return jax.ShapeDtypeStruct(shape, dtype)


def rotary_rows(length):
    half_dim = HEAD_DIM // 2
    frequency = np.float32(ROPE_BASE) ** (
        -(np.arange(half_dim, dtype=np.float32) * np.float32(2.0 / HEAD_DIM))
    )
    angles = np.arange(length, dtype=np.float32)[:, None] * frequency[None, :].astype(np.float32)
    cosine, sine = np.cos(angles), np.sin(angles)
    wide_cosine = np.concatenate([cosine] * 4, axis=1)
    wide_sine = np.concatenate([-sine, sine, -sine, sine], axis=1)
    return wide_cosine, wide_sine, cosine.T.copy(), sine.T.copy()


def causal_mask(size):
    key_pos = lax.broadcasted_iota(jnp.int32, (size, size), 0)
    query_pos = lax.broadcasted_iota(jnp.int32, (size, size), 1)
    return key_pos <= query_pos


def scores_by_key(keys, queries, mask):
    size = queries.shape[0]
    before = keys.shape[0] - size
    raw = product(keys, queries, 1, 1)
    last = jnp.where(mask, raw[before:], MASKED)
    return last if before == 0 else jnp.concatenate([raw[:before], last], axis=0)


def scaled_norm(values, gain):
    inverse = lax.rsqrt(jnp.mean(values * values, axis=-1, keepdims=True) + NORM_EPS)
    return values * inverse * gain, inverse


def attention_kernel(
    x_ref, w_ref, gain_ref, cos_ref, sin_ref,
    q_ref, k_ref, v_ref, normed_ref, low_ref, peak_ref, total_ref, res_ref, two_ref,
):
    length = x_ref.shape[0]
    q_rows = HEADS * HEAD_DIM
    kv_rows = KV_HEADS * HEAD_DIM
    turned = q_rows + kv_rows
    size = min(256, length)
    lane = lax.broadcasted_iota(jnp.int32, (size, turned), 1)
    first = lane % HEAD_DIM < HEAD_DIM // 2
    for start in range(0, length, size):
        rows = slice(start, start + size)
        hidden = x_ref[rows].astype(jnp.float32)
        normed = scaled_norm(hidden, gain_ref[0:1])[0].astype(jnp.bfloat16)
        normed_ref[rows] = normed
        raw = product(normed, w_ref[: turned + kv_rows], 1, 1)
        both = raw[:, :turned]
        swapped = jnp.where(
            first,
            pltpu.roll(both, turned - HEAD_DIM // 2, 1),
            pltpu.roll(both, HEAD_DIM // 2, 1),
        )
        cosine = jnp.concatenate([cos_ref[rows]] * (turned // 128), axis=1)
        sine = jnp.concatenate([sin_ref[rows]] * (turned // 128), axis=1)
        both = both * cosine + swapped * sine
        q_ref[rows] = both[:, :q_rows].astype(jnp.bfloat16)
        k_ref[rows] = both[:, q_rows:].astype(jnp.bfloat16)
        v_ref[rows] = raw[:, turned:].astype(jnp.bfloat16)
    size = min(512, length)
    mask = causal_mask(size)
    group = HEADS // KV_HEADS
    for head in range(HEADS):
        place = slice(head * HEAD_DIM, (head + 1) * HEAD_DIM)
        shared = slice(head // group * HEAD_DIM, (head // group + 1) * HEAD_DIM)
        for start in range(0, length, size):
            end = start + size
            queries = q_ref[start:end, place] * jnp.bfloat16(SCORE_SCALE)
            scores = scores_by_key(k_ref[:end, shared], queries, mask)
            peak = jnp.max(scores, axis=0, keepdims=True)
            shifted = jnp.exp(scores - peak)
            inverse = 1.0 / jnp.sum(shifted, axis=0, keepdims=True)
            prob_low = (shifted * inverse).astype(jnp.bfloat16)
            out = product(v_ref[:end, shared], prob_low, 0, 0)
            low_ref[start:end, place] = out.T.astype(jnp.bfloat16)
            peak_ref[head : head + 1, start:end] = peak
            total_ref[head : head + 1, start:end] = inverse
    size = min(256, length)
    for start in range(0, length, size):
        rows = slice(start, start + size)
        residual = x_ref[rows].astype(jnp.float32) + product(
            low_ref[rows], w_ref[turned + kv_rows :], 1, 0
        )
        res_ref[rows] = residual
        two_ref[rows] = scaled_norm(residual, gain_ref[1:2])[0].astype(jnp.bfloat16)


def feed_kernel(
    weight_ref, core_ref, two_ref, res_ref, grad_ref, low_ref, gate_ref, up_ref, down_ref, o_ref,
    gain_ref, out_ref, back_ref, att_ref, do_ref, dgain_ref, *refs,
):
    *grad_refs, sum_ref, inner_ref, coming_ref = refs
    step = pl.program_id(0)
    length = two_ref.shape[0]
    size = min(256, length)
    weight = weight_ref[0, 0]
    core = core_ref[0, 0]
    gate_w = gate_ref[...].reshape(-1, D)
    up_w = up_ref[...].reshape(-1, D)
    down_w = down_ref[...].reshape(-1, D)

    @pl.when(step == 0)
    def _():
        coming_ref[...] = (grad_ref[...].astype(jnp.float32) * weight).astype(jnp.bfloat16)
        sum_ref[...] = jnp.zeros_like(sum_ref)
        inner_ref[...] = jnp.zeros_like(inner_ref)

    two = two_ref[...]
    coming = coming_ref[...]
    gate = product(two, gate_w, 1, 1)
    up = product(two, up_w, 1, 1)
    sigmoid = 0.5 * jnp.tanh(0.5 * gate) + 0.5
    silu = gate * sigmoid
    activation = (silu * up).astype(jnp.bfloat16)
    act_grad = product(coming, down_w, 1, 1)
    gate_low = (act_grad * up * (sigmoid * (1.0 + gate * (1.0 - sigmoid)))).astype(jnp.bfloat16)
    up_low = (act_grad * silu).astype(jnp.bfloat16)
    sum_ref[...] += product(activation, down_w, 1, 0)
    inner_ref[...] += product(gate_low, gate_w, 1, 0) + product(up_low, up_w, 1, 0)
    down_grad = product(activation, coming, 0, 0)
    gate_grad = product(gate_low, two, 0, 0)
    up_grad = product(up_low, two, 0, 0)
    if len(grad_refs) == 3:
        for ref, grad in zip(grad_refs, (gate_grad, up_grad, down_grad)):
            ref[...] = grad.reshape(ref.shape)
    else:
        first_held, first_sent, second_held, second_sent = grad_refs
        cut = first_held.shape[1]
        pairs = first_held.shape[0]
        for kind, grad in enumerate((gate_grad, up_grad, down_grad)):
            blocks, rows = (down_ref if kind == 2 else gate_ref).shape[:2]
            grad = grad.reshape(blocks // 2, 2, rows, D)
            kept = jnp.where(core == 0, grad[:, 0], grad[:, 1])
            sent = jnp.where(core == 0, grad[:, 1], grad[:, 0]).astype(jnp.bfloat16)
            start = step * (blocks // 2) + (pairs // 2 if kind == 1 else 0)
            spot = pl.ds(start, blocks // 2)
            if kind == 2:
                second_held[spot, gate_ref.shape[1] - cut :, :] = kept
                second_sent[spot, gate_ref.shape[1] - cut :, :] = sent
            else:
                first_held[spot] = kept[:, :cut]
                first_sent[spot] = sent[:, :cut]
                second_held[spot, : rows - cut, :] = kept[:, cut:]
                second_sent[spot, : rows - cut, :] = sent[:, cut:]

    @pl.when(step == pl.num_programs(0) - 1)
    def _():
        dgain_ref[...] = jnp.zeros_like(dgain_ref)
        for start in range(0, length, size):
            rows = slice(start, start + size)
            residual = res_ref[rows]
            out_ref[rows] = (residual + sum_ref[rows]).astype(jnp.bfloat16)
            inner = inner_ref[rows]
            inverse = scaled_norm(residual, 1.0)[1]
            scaled = inner * gain_ref[1:2]
            dgain_ref[...] += jnp.sum(inner * residual * inverse, axis=0, keepdims=True)
            back = (
                grad_ref[rows].astype(jnp.float32) * weight
                + inverse * scaled
                - residual
                * (inverse * inverse * inverse)
                * jnp.mean(scaled * residual, axis=-1, keepdims=True)
            )
            back_ref[rows] = back
            coming_ref[rows] = back.astype(jnp.bfloat16)
        do_ref[...] = product(low_ref[...], coming_ref[...], 0, 0)
        att_ref[...] = product(coming_ref[...], o_ref[...], 1, 1).astype(jnp.bfloat16)


def head_kernel(
    head, q_ref, k_ref, v_ref, grad_ref, peak_ref, total_ref, cos_ref, sin_ref,
    dq_ref, dk_ref, dv_ref, key_sum, value_sum,
):
    length = q_ref.shape[0]
    size = min(256, length)
    half_dim = HEAD_DIM // 2
    mask = causal_mask(size)
    group = HEADS // KV_HEADS
    shared = slice(head * HEAD_DIM, (head + 1) * HEAD_DIM)
    key_sum[...] = jnp.zeros_like(key_sum)
    value_sum[...] = jnp.zeros_like(value_sum)

    def turn_back(grad, columns):
        first, second = grad[:half_dim], grad[half_dim:]
        cosine, sine = cos_ref[:, columns], sin_ref[:, columns]
        turned = [first * cosine + second * sine, second * cosine - first * sine]
        return jnp.concatenate(turned, axis=0).T

    for member in range(group):
        row = head * group + member
        place = slice(row * HEAD_DIM, (row + 1) * HEAD_DIM)
        for start in range(0, length, size):
            end = start + size
            queries = q_ref[start:end, place] * jnp.bfloat16(SCORE_SCALE)
            grad = grad_ref[start:end, place]
            keys, values = k_ref[:end, shared], v_ref[:end, shared]
            scores = scores_by_key(keys, queries, mask)
            probs = (
                jnp.exp(scores - peak_ref[row : row + 1, start:end])
                * total_ref[row : row + 1, start:end]
            )
            moved = probs * product(values, grad, 1, 1)
            score_grad = (moved - probs * jnp.sum(moved, axis=0, keepdims=True)).astype(
                jnp.bfloat16
            )
            value_sum[:end] += product(probs.astype(jnp.bfloat16), grad, 1, 0)
            key_sum[:end] += product(score_grad, queries, 1, 0)
            back = turn_back(product(keys, score_grad, 0, 0) * SCORE_SCALE, slice(start, end))
            dq_ref[start:end, member * HEAD_DIM : (member + 1) * HEAD_DIM] = back.astype(
                jnp.bfloat16
            )
    dk_ref[...] = turn_back(key_sum[...].T, slice(0, length)).astype(jnp.bfloat16)
    dv_ref[...] = value_sum[...].astype(jnp.bfloat16)


def qkv_kernel(core_ref, *refs):
    parts, (normed_ref, o_ref, joined_ref), out_refs = refs[:9], refs[9:12], refs[12:]
    start = 0
    for part in parts:
        joined_ref[:, start : start + part.shape[1]] = part[...]
        start += part.shape[1]
    grad = product(joined_ref[...], normed_ref[...], 0, 0)
    if len(out_refs) == 1:
        out_refs[0][:start] = grad
        out_refs[0][start:] = o_ref[...]
        return
    held_ref, sent_ref = out_refs
    rows = held_ref.shape[1]
    spot = 0
    for value in (grad, o_ref[...]):
        value = value.reshape(-1, 2, rows, D)
        end = spot + value.shape[0]
        held_ref[spot:end] = jnp.where(core_ref[0, 0] == 0, value[:, 0], value[:, 1])
        sent = jnp.where(core_ref[0, 0] == 0, value[:, 1], value[:, 0])
        sent_ref[spot:end] = sent.astype(jnp.bfloat16)
        spot = end


def input_kernel(joined_ref, w_ref, x_ref, back_ref, gain_ref, out_ref, dgain_ref):
    length = x_ref.shape[0]
    size = min(256, length)
    count = joined_ref.shape[1]
    dgain_ref[...] = jnp.zeros_like(dgain_ref)
    for start in range(0, length, size):
        rows = slice(start, start + size)
        inner = product(joined_ref[rows], w_ref[:count], 1, 0)
        hidden = x_ref[rows].astype(jnp.float32)
        inverse = scaled_norm(hidden, 1.0)[1]
        scaled = inner * gain_ref[0:1]
        dgain_ref[...] += jnp.sum(inner * hidden * inverse, axis=0, keepdims=True)
        out_ref[rows] = (
            back_ref[rows]
            + inverse * scaled
            - hidden
            * (inverse * inverse * inverse)
            * jnp.mean(scaled * hidden, axis=-1, keepdims=True)
        ).astype(jnp.bfloat16)


def ortho_kernel(block_ref, out_ref, held_ref):
    size = min(block_ref.shape)
    left = block_ref.shape[0] < block_ref.shape[1]
    block = block_ref[...].astype(jnp.float32)
    held_ref[...] = block * (1.0 / (jnp.sqrt(jnp.sum(block * block)) + 1e-07))
    row = lax.broadcasted_iota(jnp.int32, (size, size), 0)
    diagonal = row == lax.broadcasted_iota(jnp.int32, (size, size), 1)

    def sweep(index, carry):
        held = held_ref[...]
        scaled = held.astype(jnp.bfloat16)
        side = 1 if left else 0
        gram = product(scaled, scaled, side, side)
        mean = jnp.sum(jnp.where(diagonal, gram, 0.0)) / size
        rest = jnp.where(diagonal, gram - mean, gram)
        rest_low = rest.astype(jnp.bfloat16)
        poly = (POLY_TWO + 2.0 * POLY_THREE * mean) * rest + POLY_THREE * product(
            rest_low, rest_low, 1, 0
        )
        poly_low = poly.astype(jnp.bfloat16)
        turned = product(poly_low, scaled, 1, 0) if left else product(scaled, poly_low, 1, 0)
        held_ref[...] = (POLY_ONE + POLY_TWO * mean + POLY_THREE * mean * mean) * held + turned
        return carry

    lax.fori_loop(0, ORTHO_STEPS, sweep, 0)
    out_ref[...] = held_ref[...].astype(jnp.bfloat16)


def orthogonalize(block):
    rows, columns = block.shape
    small, large = min(block.shape), max(block.shape)
    return call(
        ortho_kernel,
        shape_of(block.shape, jnp.bfloat16),
        (block,),
        2 * ORTHO_STEPS * small * small * (2 * large + small),
        scratch=(pltpu.VMEM((rows, columns), jnp.float32),),
    )


def block_list():
    q_rows = HEADS * HEAD_DIM
    kv_rows = KV_HEADS * HEAD_DIM
    return (
        (0, 0, q_rows),
        (0, q_rows, kv_rows),
        (0, q_rows + kv_rows, kv_rows),
        (0, q_rows + 2 * kv_rows, q_rows),
        (1, 0, FF),
        (1, FF, FF),
        (2, 0, FF),
    )


def row_scales(array_id):
    pieces = [
        jnp.full((row_count,), 0.2 * math.sqrt(max(row_count, D)), jnp.float32)
        for owner_id, row_start, row_count in block_list()
        if owner_id == array_id
    ]
    return jnp.concatenate(pieces, axis=0)


def orthogonal_rows(attn_low, gate_up_low, down_low, place, devices):
    q_rows = HEADS * HEAD_DIM
    kv_rows = KV_HEADS * HEAD_DIM
    bits = devices.bit_length() - 1
    top_bit = bits - 1
    core, across, top = bit_of(place, 0), bit_of(place, 1), bit_of(place, top_bit)
    rows = attn_low.shape[0]
    other = swap(jnp.where(top == 0, attn_low, down_low), top_bit, devices)
    third = ordered(top, jnp.where(top == 0, down_low, attn_low), other, 0).reshape(2 * rows, D)
    other = swap(jnp.where(across == 0, third, gate_up_low), 1, devices)
    blocks = ordered(across, jnp.where(across == 0, gate_up_low, third), other, 0)
    middle = list(range(2, top_bit))
    for bit in middle + [0]:
        other = swap(blocks, bit, devices)
        blocks = ordered(bit_of(place, bit), blocks, other, 0)
    spot = core * (devices // 8) + ((place >> 2) & (devices // 8 - 1))

    def whole(blocks):
        result = orthogonalize(blocks.reshape(-1, D))
        return pick(result.reshape(devices // 4, 2, 2 * rows, D), 0, spot)

    def natural(blocks, half):
        lead = blocks.reshape(2, devices // 8, 2, 2, rows, D)[:, :, :, half]
        return lead.transpose(1, 2, 0, 3, 4).reshape(-1, D)

    def placed(first, second):
        result = jnp.concatenate([first, second], axis=0)
        result = pick(result.reshape(devices // 8, 2, 2, rows, D), 0, (place >> 2) & (devices // 8 - 1))
        return result.reshape(2, 2 * rows, D)

    def query_key(blocks):
        block = natural(blocks, 0)
        return placed(orthogonalize(block[:q_rows]), orthogonalize(block[q_rows:]))

    def value_out(blocks):
        block = natural(blocks, 1)
        return placed(orthogonalize(block[:kv_rows]), orthogonalize(block[kv_rows:]))

    is_attn = (top == 1) & (across == 1)
    result = lax.switch(
        jnp.where(is_attn, 1 + core, 0), [whole, query_key, value_out], blocks
    )
    by_core = result.reshape(2, 2, rows, D)
    other = swap(
        pick(by_core, 1, 1 - core), 0, devices, lambda i: (i >> 1) & 1 == 1 and i >> top_bit == 1
    )
    joined = ordered(core, pick(by_core, 1, core), other, 1)
    by_top = jnp.where(is_attn, joined, by_core)
    other = swap(pick(by_top, 1, 1 - top), top_bit, devices, lambda i: (i >> 1) & 1 == 1)
    own = pick(by_top, 1, top)
    down_rows = jnp.where(top == 0, own, other)
    attn_rows = jnp.where(top == 0, other, own)
    result = by_top.reshape(2, 2 * rows, D)
    other = swap(
        jnp.where(across == 0, result[1], jnp.concatenate([down_rows[0], attn_rows[0]], axis=0)),
        1,
        devices,
    )
    return (
        jnp.where(across == 0, other[rows:], attn_rows[1]),
        jnp.where(across == 0, result[0], other),
        jnp.where(across == 0, other[:rows], down_rows[1]),
    )


def per_device(
    inputs,
    out_grad,
    lang_tags,
    attn_master,
    gate_up_master,
    down_master,
    attn_momentum,
    gate_up_momentum,
    down_momentum,
    norm_gains,
    gain_first,
    gain_second,
):
    devices = lax.axis_size(("dp", "sub"))
    device_place = lax.axis_index(("dp", "sub"))
    q_rows = HEADS * HEAD_DIM
    kv_rows = KV_HEADS * HEAD_DIM
    qkv_rows = q_rows + 2 * kv_rows
    tag_hot = (lang_tags[:, None] == jnp.arange(NUM_TAGS, dtype=jnp.int32)[None, :]).astype(
        jnp.float32
    )
    masters = (attn_master, gate_up_master, down_master)
    attn_low = attn_master.astype(jnp.bfloat16)
    gate_up_low = gate_up_master.astype(jnp.bfloat16)
    down_low = down_master.astype(jnp.bfloat16)
    tag_rows = jnp.pad(jnp.sum(tag_hot, axis=0)[None], ((0, 15), (0, D - NUM_TAGS)))
    attn_weights = gather_rows(attn_low, device_place, devices).reshape(-1, D)
    ffn_low = jnp.concatenate([gate_up_low, down_low, tag_rows.astype(jnp.bfloat16)], axis=0)
    ffn_weights = lax.all_gather(ffn_low, AXES, axis=0)
    ffn_rows = gate_up_low.shape[0] + down_low.shape[0]
    gate_up_rows, down_rows = gate_up_low.shape[0], down_low.shape[0]
    even = down_rows % 16 == 0
    if even:
        gate_up_weights = down_weights = ffn_weights
        down_skip = gate_up_rows // down_rows
    else:
        gate_up_weights = ffn_weights[:, :gate_up_rows].reshape(32, -1, D)
        down_weights = ffn_weights[:, gate_up_rows:ffn_rows].reshape(32, -1, D)
        gate_up_rows, down_rows = gate_up_weights.shape[1], down_weights.shape[1]
        down_skip = 0
    tag_count = jnp.sum(ffn_weights[:, ffn_rows, :NUM_TAGS].astype(jnp.float32), axis=0)
    seq_weight = (
        devices * lang_tags.shape[0] / (NUM_TAGS * jnp.sum(tag_hot * tag_count[None, :], axis=1))
    )
    length = inputs.shape[0]
    wide_cos, wide_sin, tall_cos, tall_sin = [jnp.asarray(t) for t in rotary_rows(length)]
    low, single = jnp.bfloat16, jnp.float32
    queries, keys, values, normed_one, attended_low, peaks, totals, residual, normed_two = call(
        attention_kernel,
        (
            shape_of((length, q_rows), low),
            shape_of((length, kv_rows), low),
            shape_of((length, kv_rows), low),
            shape_of((length, D), low),
            shape_of((length, q_rows), low),
            shape_of((HEADS, length), single),
            shape_of((HEADS, length), single),
            shape_of((length, D), single),
            shape_of((length, D), low),
        ),
        (inputs, attn_weights, norm_gains, wide_cos, wide_sin),
        2 * length * D * 3 * (qkv_rows + q_rows),
    )
    chunk = 768 if even else 384
    steps = FF // chunk
    place = device_place
    core = bit_of(place, 0)[None, None]
    held_once = dict(pipeline_mode=pl.Buffered(1))
    whole = lambda *shape: pl.BlockSpec(shape, lambda c: (0,) * len(shape), **held_once)
    gate_blocks, down_blocks = chunk // gate_up_rows, chunk // down_rows
    part = lambda skip: pl.BlockSpec((gate_blocks, gate_up_rows, D), lambda c: (c + skip, 0, 0))
    down_part = pl.BlockSpec((down_blocks, down_rows, D), lambda c: (c, down_skip, 0))
    if even:
        cut = (gate_up_rows + down_rows) * 9 // 16 // 16 * 16
        other_cut = gate_up_rows + down_rows - cut
        pairs = devices // 2
        grad_outs = tuple(
            shape_of((pairs, size, D), kind) for size in (cut, other_cut) for kind in (single, low)
        )
        grad_specs = tuple(whole(*out.shape) for out in grad_outs)
    else:
        grad_outs = (
            shape_of((16, gate_up_rows, D), single),
            shape_of((16, gate_up_rows, D), single),
            shape_of((32, down_rows, D), single),
        )
        grad_specs = (part(0), part(0), pl.BlockSpec((down_blocks, down_rows, D), lambda c: (c, 0, 0)))
    outputs, residual_grad, attended_grad, o_part, gain_two, *ffn_grads = call(
        feed_kernel,
        (
            shape_of((length, D), low),
            shape_of((length, D), single),
            shape_of((length, q_rows), low),
            shape_of((q_rows, D), single),
            shape_of((1, D), single),
            *grad_outs,
        ),
        (
            seq_weight[:1, None],
            core,
            normed_two,
            residual,
            out_grad,
            attended_low,
            gate_up_weights,
            gate_up_weights,
            down_weights,
            attn_weights[qkv_rows:],
            norm_gains,
        ),
        2 * 3 * length * D * (3 * FF + q_rows),
        grid=(steps,),
        in_specs=[
            pl.BlockSpec(memory_space=pltpu.SMEM),
            pl.BlockSpec(memory_space=pltpu.SMEM),
            whole(length, D),
            whole(length, D),
            whole(length, D),
            whole(length, q_rows),
            part(0),
            part(steps),
            down_part,
            whole(q_rows, D),
            whole(2, D),
        ],
        out_specs=(
            whole(length, D),
            whole(length, D),
            whole(length, q_rows),
            whole(q_rows, D),
            whole(1, D),
            *grad_specs,
        ),
        scratch=(
            pltpu.VMEM((length, D), single),
            pltpu.VMEM((length, D), single),
            pltpu.VMEM((length, D), low),
        ),
    )
    bits = range(devices.bit_length() - 1)
    if even:
        first_held, first_sent, second_held, second_sent = ffn_grads
        sums = [
            Sums(first_held, place, devices, bits[1:], swap(first_sent, 0, devices)),
            Sums(second_held, place, devices, bits[1:], swap(second_sent, 0, devices)),
        ]
    else:
        gate_up_part = jnp.concatenate([g.reshape(-1, D) for g in ffn_grads[:2]], axis=0)
        sums = [
            Sums(gate_up_part.reshape(devices, -1, D), place, devices, bits),
            Sums(ffn_grads[2].reshape(devices, -1, D), place, devices, bits),
        ]
        for s in sums:
            s.hop(0)
    head_grads = []
    for head in range(KV_HEADS):
        head_grads.append(
            call(
                partial(head_kernel, head),
                (
                    shape_of((length, q_rows // KV_HEADS), low),
                    shape_of((length, HEAD_DIM), low),
                    shape_of((length, HEAD_DIM), low),
                ),
                (queries, keys, values, attended_grad, peaks, totals, tall_cos, tall_sin),
                2 * 2 * length * length * q_rows,
                scratch=(
                    pltpu.VMEM((length, HEAD_DIM), single),
                    pltpu.VMEM((length, HEAD_DIM), single),
                ),
            )
        )
        if head == 0:
            attended_grad = after(attended_grad, sums)
            sums[0].hop(1)
            sums[1].hop(2)
    proj_parts = [head_grads[head][kind] for kind in range(3) for head in range(KV_HEADS)]
    normed_one = after(normed_one, sums)
    sums[0].hop(2)
    sums[1].hop(1)
    if even:
        grad_outs = (
            shape_of((pairs, attn_low.shape[0], D), single),
            shape_of((pairs, attn_low.shape[0], D), low),
        )
    else:
        grad_outs = (shape_of((qkv_rows + q_rows, D), single),)
    in_smem = pl.BlockSpec(memory_space=pltpu.SMEM)
    in_vmem = pl.BlockSpec(memory_space=pltpu.VMEM)
    joined, *attn_grads = call(
        qkv_kernel,
        (shape_of((length, qkv_rows), low), *grad_outs),
        (core, *proj_parts, normed_one, o_part),
        2 * length * D * qkv_rows,
        in_specs=[in_smem] + [in_vmem] * 11,
        out_specs=(in_vmem,) * (1 + len(grad_outs)),
    )
    if even:
        cut = attn_low.shape[0] // 2
        held, sent = attn_grads
        came = swap(sent, 0, devices)
        late = [
            Sums(held[:, :cut], place, devices, bits[1:], came[:, :cut]),
            Sums(held[:, cut:], place, devices, bits[1:], came[:, cut:]),
        ]
    else:
        late = [Sums(attn_grads[0].reshape(devices, -1, D), place, devices, bits)]
        late[0].hop(0)
    residual_grad = after(residual_grad, late)
    input_grad, gain_one = call(
        input_kernel,
        (shape_of((length, D), low), shape_of((1, D), single)),
        (joined, attn_weights, inputs, residual_grad, norm_gains),
        2 * length * D * qkv_rows,
    )
    for index, order in enumerate(((1, 2), (2, 1))[: len(late)]):
        for bit in order:
            late[index].hop(bit)
    for bit in bits[3:]:
        for s in sums:
            s.hop(bit)
    for bit in bits[3:]:
        for s in late:
            s.hop(bit)
    attn_sum = jnp.concatenate([s.total() for s in late], axis=0)
    if even:
        cut = first_held.shape[1]
        first, second = [s.total() for s in sums]
        gate_up_sum = jnp.concatenate([first, second[: gate_up_rows - cut]], axis=0)
        down_sum = second[gate_up_rows - cut :]
    else:
        gate_up_sum, down_sum = [s.total() for s in sums]
    gain_total = sum_small(jnp.concatenate([gain_one, gain_two], axis=0), devices)
    squares = (
        jnp.sum(attn_sum * attn_sum)
        + jnp.sum(gate_up_sum * gate_up_sum)
        + jnp.sum(down_sum * down_sum)
    )
    squares = sum_small(jnp.full((8, 128), squares), devices)[0, 0]
    square_total = squares + jnp.sum(gain_total * gain_total)
    grad_norm = jnp.sqrt(square_total)
    param_count = (qkv_rows + q_rows + 3 * FF) * D + 2 * D
    factor = jnp.minimum(1.0, CLIP_SCALE * math.sqrt(devices * length * param_count) / grad_norm)
    attn_grad = attn_sum * factor
    gate_up_grad = gate_up_sum * factor
    down_grad = down_sum * factor
    gain_grad = gain_total * factor
    attn_moment = MOMENTUM_DECAY * attn_momentum + attn_grad
    gate_up_moment = MOMENTUM_DECAY * gate_up_momentum + gate_up_grad
    down_moment = MOMENTUM_DECAY * down_momentum + down_grad
    ortho_shards = orthogonal_rows(
        attn_moment.astype(jnp.bfloat16),
        gate_up_moment.astype(jnp.bfloat16),
        down_moment.astype(jnp.bfloat16),
        device_place,
        devices,
    )
    new_masters = []
    for array_id in range(3):
        shard_rows = masters[array_id].shape[0]
        scale_rows = lax.dynamic_slice_in_dim(
            row_scales(array_id), device_place * shard_rows, shard_rows, 0
        )
        new_masters.append(
            masters[array_id]
            - MATRIX_RATE
            * (scale_rows[:, None] * ortho_shards[array_id] + MATRIX_DECAY * masters[array_id])
        )
    first_new = BETA_FIRST * gain_first + (1.0 - BETA_FIRST) * gain_grad
    second_new = BETA_SECOND * gain_second + (1.0 - BETA_SECOND) * gain_grad * gain_grad
    gains_new = norm_gains - GAIN_RATE * (first_new / (1.0 - BETA_FIRST**STEP_NUMBER)) / (
        jnp.sqrt(second_new / (1.0 - BETA_SECOND**STEP_NUMBER)) + ADAM_EPS
    )
    return (
        outputs,
        input_grad,
        attn_grad,
        gate_up_grad,
        down_grad,
        grad_norm,
        attn_moment,
        gate_up_moment,
        down_moment,
        new_masters[0],
        new_masters[1],
        new_masters[2],
        gain_grad,
        first_new,
        second_new,
        gains_new,
    )


def solution(mesh):
    placed = (
        P(("dp", "sub"), None),
        P(("dp", "sub"), None),
        P(("dp", "sub")),
        P(("dp", "sub"), None),
        P(("dp", "sub"), None),
        P(("dp", "sub"), None),
        P(("dp", "sub"), None),
        P(("dp", "sub"), None),
        P(("dp", "sub"), None),
        P(),
        P(),
        P(),
    )
    return jax.shard_map(
        per_device,
        mesh=mesh,
        in_specs=placed,
        out_specs=(
            P(("dp", "sub"), None),
            P(("dp", "sub"), None),
            P(("dp", "sub"), None),
            P(("dp", "sub"), None),
            P(("dp", "sub"), None),
            P(),
            P(("dp", "sub"), None),
            P(("dp", "sub"), None),
            P(("dp", "sub"), None),
            P(("dp", "sub"), None),
            P(("dp", "sub"), None),
            P(("dp", "sub"), None),
            P(),
            P(),
            P(),
            P(),
        ),
        check_vma=False,
    )
```

```python
from functools import partial
import math

import jax
import jax.numpy as jnp
import numpy as np
from jax import lax
from jax.experimental import pallas as pl
from jax.experimental.pallas import tpu as pltpu
from jax.sharding import PartitionSpec as P

D = 576
HEADS = 9
KV_HEADS = 3
HEAD_DIM = 64
FF = 1536
NUM_TAGS = 8
ORTHO_STEPS = 5
STEP_NUMBER = 10


NORM_EPS = 1e-05
ROPE_BASE = 100000.0
POLY_ONE = 3.4445
POLY_TWO = -4.775
POLY_THREE = 2.0315
MOMENTUM_DECAY = 0.95
MATRIX_RATE = 0.2
MATRIX_DECAY = 0.1
GAIN_RATE = 1.0
BETA_FIRST = 0.9
BETA_SECOND = 0.95
ADAM_EPS = 1e-08
CLIP_SCALE = 0.002
VMEM_BYTES = 58 * 2**20


AXES = ("dp", "sub")


def bit_of(place, bit):
    return (place >> bit) & 1


def swap(array, bit, devices, only=None):
    pairs = [(i, i ^ (1 << bit)) for i in range(devices) if only is None or only(i)]
    return lax.ppermute(array, AXES, pairs)


def ordered(mine, own, other, axis):
    first = jnp.where(mine == 0, own, other)
    second = jnp.where(mine == 0, other, own)
    return jnp.stack([first, second], axis=axis)


def gather_rows(rows, place, devices, early):
    blocks = rows[None]
    for bit in reversed(range(1, devices.bit_length() - 1)):
        other = swap(blocks, bit, devices)
        blocks = ordered(bit_of(place, bit), blocks, other, 1)
        blocks = blocks.reshape((-1,) + rows.shape)
        if bit == 2:
            blocks, early = lax.optimization_barrier((blocks, early))
    return blocks, swap(blocks, 0, devices), early


def pick(array, axis, index):
    return lax.dynamic_index_in_dim(array, index, axis, keepdims=False)


def halve(held, came, axis, mine):
    if came is None:
        return pick(held, axis, mine), pick(held, axis, 1 - mine).astype(jnp.bfloat16)
    came = came.reshape(held.shape)
    kept = pick(held, axis, mine) + pick(came, axis, mine).astype(jnp.float32)
    sent = pick(held, axis, 1 - mine) + pick(came, axis, 1 - mine).astype(jnp.float32)
    return kept, sent.astype(jnp.bfloat16)


class Sums:
    def __init__(self, held, place, devices, bits, came=None):
        self.place, self.devices, self.bits = place, devices, list(bits)
        self.shape = held.shape[-2:]
        self.held = held.reshape((2,) * len(self.bits) + self.shape)
        self.came = came

    def hop(self, bit):
        axis = len(self.bits) - 1 - self.bits.index(bit)
        self.held, sent = halve(self.held, self.came, axis, bit_of(self.place, bit))
        self.bits.remove(bit)
        self.came = swap(sent.reshape((-1,) + self.shape), bit, self.devices)

    def total(self):
        return self.held + self.came.reshape(self.held.shape).astype(jnp.float32)


def after(value, sums):
    value, came = lax.optimization_barrier((value, [s.came for s in sums]))
    for s, c in zip(sums, came):
        s.came = c
    return value


def sum_small(value, devices):
    for bit in reversed(range(devices.bit_length() - 1)):
        value = value + swap(value, bit, devices)
    return value


SCORE_SCALE = HEAD_DIM ** (-0.5)
MASKED = -1e30


def product(left, right, left_dim, right_dim):
    return lax.dot_general(
        left, right, (((left_dim,), (right_dim,)), ((), ())), preferred_element_type=jnp.float32
    )


def call(kernel, outs, args, flops, grid=(), in_specs=None, out_specs=None, scratch=()):
    specs = {} if in_specs is None else dict(in_specs=in_specs, out_specs=out_specs)
    listed = tuple(outs) if isinstance(outs, (tuple, list)) else (outs,)
    moved = sum(math.prod(a.shape) * a.dtype.itemsize for a in tuple(args) + listed)
    return pl.pallas_call(
        kernel,
        out_shape=outs,
        grid=grid,
        scratch_shapes=scratch,
        compiler_params=pltpu.CompilerParams(vmem_limit_bytes=VMEM_BYTES),
        cost_estimate=pl.CostEstimate(flops=int(flops), bytes_accessed=moved, transcendentals=0),
        **specs,
    )(*args)


def shape_of(shape, dtype):
    return jax.ShapeDtypeStruct(shape, dtype)


def rotary_rows(length):
    half_dim = HEAD_DIM // 2
    frequency = np.float32(ROPE_BASE) ** (
        -(np.arange(half_dim, dtype=np.float32) * np.float32(2.0 / HEAD_DIM))
    )
    angles = np.arange(length, dtype=np.float32)[:, None] * frequency[None, :].astype(np.float32)
    cosine, sine = np.cos(angles), np.sin(angles)
    wide_cosine = np.concatenate([cosine] * 4, axis=1)
    wide_sine = np.concatenate([-sine, sine, -sine, sine], axis=1)
    return wide_cosine, wide_sine, cosine.T.copy(), sine.T.copy()


def causal_mask(size):
    key_pos = lax.broadcasted_iota(jnp.int32, (size, size), 0)
    query_pos = lax.broadcasted_iota(jnp.int32, (size, size), 1)
    return key_pos <= query_pos


def scores_by_key(keys, queries, mask):
    size = queries.shape[0]
    before = keys.shape[0] - size
    raw = product(keys, queries, 1, 1)
    last = jnp.where(mask, raw[before:], MASKED)
    return last if before == 0 else jnp.concatenate([raw[:before], last], axis=0)


def scaled_norm(values, gain):
    inverse = lax.rsqrt(jnp.mean(values * values, axis=-1, keepdims=True) + NORM_EPS)
    return values * inverse * gain, inverse


def attention_kernel(
    core_ref, x_ref, own_ref, other_ref, gain_ref, cos_ref, sin_ref,
    q_ref, k_ref, v_ref, normed_ref, low_ref, peak_ref, total_ref, res_ref, two_ref, joined_ref,
):
    length = x_ref.shape[0]
    q_rows = HEADS * HEAD_DIM
    kv_rows = KV_HEADS * HEAD_DIM
    turned = q_rows + kv_rows
    if other_ref is None:
        w_ref = own_ref
    else:
        core = core_ref[0, 0]
        joined_ref[:, core] = own_ref[...]
        joined_ref[:, 1 - core] = other_ref[...]
        w_ref = joined_ref
    weights = w_ref[...].reshape(-1, D)
    size = min(256, length)
    lane = lax.broadcasted_iota(jnp.int32, (size, turned), 1)
    first = lane % HEAD_DIM < HEAD_DIM // 2
    for start in range(0, length, size):
        rows = slice(start, start + size)
        normed = scaled_norm(x_ref[rows], gain_ref[0:1])[0].astype(jnp.bfloat16)
        normed_ref[rows] = normed
        raw = product(normed, weights[: turned + kv_rows], 1, 1)
        both = raw[:, :turned]
        swapped = jnp.where(
            first,
            pltpu.roll(both, turned - HEAD_DIM // 2, 1),
            pltpu.roll(both, HEAD_DIM // 2, 1),
        )
        cosine = jnp.concatenate([cos_ref[rows]] * (turned // 128), axis=1)
        sine = jnp.concatenate([sin_ref[rows]] * (turned // 128), axis=1)
        both = both * cosine + swapped * sine
        q_ref[rows] = both[:, :q_rows].astype(jnp.bfloat16)
        k_ref[rows] = both[:, q_rows:].astype(jnp.bfloat16)
        v_ref[rows] = raw[:, turned:].astype(jnp.bfloat16)
    size = min(512, length)
    mask = causal_mask(size)
    group = HEADS // KV_HEADS
    for head in range(HEADS):
        place = slice(head * HEAD_DIM, (head + 1) * HEAD_DIM)
        shared = slice(head // group * HEAD_DIM, (head // group + 1) * HEAD_DIM)
        for start in range(0, length, size):
            end = start + size
            queries = q_ref[start:end, place] * jnp.bfloat16(SCORE_SCALE)
            scores = scores_by_key(k_ref[:end, shared], queries, mask)
            peak = jnp.max(scores, axis=0, keepdims=True)
            shifted = jnp.exp(scores - peak)
            inverse = 1.0 / jnp.sum(shifted, axis=0, keepdims=True)
            prob_low = (shifted * inverse).astype(jnp.bfloat16)
            out = product(v_ref[:end, shared], prob_low, 0, 0)
            low_ref[start:end, place] = out.T.astype(jnp.bfloat16)
            peak_ref[head : head + 1, start:end] = peak
            total_ref[head : head + 1, start:end] = inverse
    size = min(256, length)
    for start in range(0, length, size):
        rows = slice(start, start + size)
        residual = x_ref[rows] + product(low_ref[rows], weights[turned + kv_rows :], 1, 0)
        res_ref[rows] = residual
        two_ref[rows] = scaled_norm(residual, gain_ref[1:2])[0].astype(jnp.bfloat16)


def whole_attention_kernel(core_ref, x_ref, own_ref, *refs):
    attention_kernel(core_ref, x_ref, own_ref, None, *refs, None)


def feed_kernel(
    core_ref, hot_ref, tags_ref, two_ref, res_ref, grad_ref, low_ref, gate_ref, up_ref, down_ref,
    attn_ref, gain_ref, out_ref, back_ref, att_ref, do_ref, dgain_ref, *refs,
):
    *grad_refs, sum_ref, inner_ref, coming_ref, hidden_ref = refs
    step = pl.program_id(0)
    length = two_ref.shape[0]
    size = min(256, length)
    core = core_ref[0, 0]
    counts = jnp.sum(tags_ref[:, 0].astype(jnp.float32), axis=0, keepdims=True)
    count = jnp.sum(hot_ref[...] * counts, axis=1, keepdims=True)
    weight = tags_ref.shape[0] / (NUM_TAGS * count)
    o_w = attn_ref[-(attn_ref.shape[0] * HEADS // (2 * (HEADS + KV_HEADS))) :].reshape(-1, D)
    gate_w = gate_ref[...].reshape(-1, D)
    up_w = up_ref[...].reshape(-1, D)
    down_w = down_ref[...].reshape(-1, D)

    @pl.when(step == 0)
    def _():
        for start in range(0, length, size):
            rows = slice(start, start + size)
            grad = grad_ref[:, rows].astype(jnp.float32).T
            coming_ref[rows] = (grad * weight).astype(jnp.bfloat16)
        sum_ref[...] = jnp.zeros_like(sum_ref)
        inner_ref[...] = jnp.zeros_like(inner_ref)

    for start in range(0, length, 2 * size):
        rows = slice(start, min(start + 2 * size, length))
        two = two_ref[rows]
        gate = product(two, gate_w, 1, 1)
        up = product(two, up_w, 1, 1)
        sigmoid = 0.5 * jnp.tanh(0.5 * gate) + 0.5
        silu = gate * sigmoid
        activation = (silu * up).astype(jnp.bfloat16)
        act_grad = product(coming_ref[rows], down_w, 1, 1)
        gate_low = act_grad * up * (sigmoid * (1.0 + gate * (1.0 - sigmoid)))
        gate_low = gate_low.astype(jnp.bfloat16)
        up_low = (act_grad * silu).astype(jnp.bfloat16)
        sum_ref[rows] += product(activation, down_w, 1, 0)
        inner_ref[rows] += product(gate_low, gate_w, 1, 0) + product(up_low, up_w, 1, 0)
        for kind, value in enumerate((gate_low, up_low, activation)):
            hidden_ref[kind, rows] = value
    gate_grad = product(hidden_ref[0], two_ref[...], 0, 0)
    up_grad = product(hidden_ref[1], two_ref[...], 0, 0)
    down_grad = product(hidden_ref[2], coming_ref[...], 0, 0)
    if len(grad_refs) == 3:
        for ref, grad in zip(grad_refs, (gate_grad, up_grad, down_grad)):
            ref[...] = grad.reshape(ref.shape)
    else:
        first_held, first_sent, second_held, second_sent = grad_refs
        cut = first_held.shape[1]
        pairs = first_held.shape[0]
        for kind, grad in enumerate((gate_grad, up_grad, down_grad)):
            blocks, rows = (down_ref if kind == 2 else gate_ref).shape[:2]
            grad = grad.reshape(blocks // 2, 2, rows, D)
            kept = jnp.where(core == 0, grad[:, 0], grad[:, 1])
            sent = jnp.where(core == 0, grad[:, 1], grad[:, 0]).astype(jnp.bfloat16)
            start = step * (blocks // 2) + (pairs // 2 if kind == 1 else 0)
            spot = pl.ds(start, blocks // 2)
            if kind == 2:
                second_held[spot, gate_ref.shape[1] - cut :, :] = kept
                second_sent[spot, gate_ref.shape[1] - cut :, :] = sent
            else:
                first_held[spot] = kept[:, :cut]
                first_sent[spot] = sent[:, :cut]
                second_held[spot, : rows - cut, :] = kept[:, cut:]
                second_sent[spot, : rows - cut, :] = sent[:, cut:]

    @pl.when(step == pl.num_programs(0) - 1)
    def _():
        dgain_ref[...] = jnp.zeros_like(dgain_ref)
        for start in range(0, length, size):
            rows = slice(start, start + size)
            residual = res_ref[rows]
            out_ref[:, rows] = (residual + sum_ref[rows]).T.astype(jnp.bfloat16)
            inner = inner_ref[rows]
            inverse = scaled_norm(residual, 1.0)[1]
            scaled = inner * gain_ref[1:2]
            dgain_ref[...] += jnp.sum(inner * residual * inverse, axis=0, keepdims=True)
            back = (
                grad_ref[:, rows].astype(jnp.float32).T * weight
                + inverse * scaled
                - residual
                * (inverse * inverse * inverse)
                * jnp.mean(scaled * residual, axis=-1, keepdims=True)
            )
            back_ref[rows] = back
            coming_ref[rows] = back.astype(jnp.bfloat16)
        do_ref[...] = product(low_ref[...], coming_ref[...], 0, 0)
        att_ref[...] = product(coming_ref[...], o_w, 1, 1).astype(jnp.bfloat16)


def head_kernel(
    head, q_ref, k_ref, v_ref, grad_ref, peak_ref, total_ref, cos_ref, sin_ref,
    dq_ref, dk_ref, dv_ref, key_sum, value_sum,
):
    length = q_ref.shape[0]
    size = min(256, length)
    half_dim = HEAD_DIM // 2
    mask = causal_mask(size)
    group = HEADS // KV_HEADS
    shared = slice(head * HEAD_DIM, (head + 1) * HEAD_DIM)
    key_sum[...] = jnp.zeros_like(key_sum)
    value_sum[...] = jnp.zeros_like(value_sum)

    def turn_back(grad, columns):
        first, second = grad[:half_dim], grad[half_dim:]
        cosine, sine = cos_ref[:, columns], sin_ref[:, columns]
        turned = [first * cosine + second * sine, second * cosine - first * sine]
        return jnp.concatenate(turned, axis=0).T

    for member in range(group):
        row = head * group + member
        place = slice(row * HEAD_DIM, (row + 1) * HEAD_DIM)
        for start in range(0, length, size):
            end = start + size
            queries = q_ref[start:end, place] * jnp.bfloat16(SCORE_SCALE)
            grad = grad_ref[start:end, place]
            keys, values = k_ref[:end, shared], v_ref[:end, shared]
            scores = scores_by_key(keys, queries, mask)
            probs = (
                jnp.exp(scores - peak_ref[row : row + 1, start:end])
                * total_ref[row : row + 1, start:end]
            )
            moved = probs * product(values, grad, 1, 1)
            score_grad = (moved - probs * jnp.sum(moved, axis=0, keepdims=True)).astype(
                jnp.bfloat16
            )
            value_sum[:end] += product(probs.astype(jnp.bfloat16), grad, 1, 0)
            key_sum[:end] += product(score_grad, queries, 1, 0)
            back = turn_back(product(keys, score_grad, 0, 0) * SCORE_SCALE, slice(start, end))
            dq_ref[start:end, member * HEAD_DIM : (member + 1) * HEAD_DIM] = back.astype(
                jnp.bfloat16
            )
    dk_ref[...] = turn_back(key_sum[...].T, slice(0, length)).astype(jnp.bfloat16)
    dv_ref[...] = value_sum[...].astype(jnp.bfloat16)


def qkv_kernel(core_ref, *refs):
    parts, (normed_ref, o_ref, joined_ref), out_refs = refs[:9], refs[9:12], refs[12:]
    start = 0
    for part in parts:
        joined_ref[:, start : start + part.shape[1]] = part[...]
        start += part.shape[1]
    grad = product(joined_ref[...], normed_ref[...], 0, 0)
    if len(out_refs) == 1:
        out_refs[0][:start] = grad
        out_refs[0][start:] = o_ref[...]
        return
    held_ref, sent_ref = out_refs
    rows = held_ref.shape[1]
    spot = 0
    for value in (grad, o_ref[...]):
        value = value.reshape(-1, 2, rows, D)
        end = spot + value.shape[0]
        held_ref[spot:end] = jnp.where(core_ref[0, 0] == 0, value[:, 0], value[:, 1])
        sent = jnp.where(core_ref[0, 0] == 0, value[:, 1], value[:, 0])
        sent_ref[spot:end] = sent.astype(jnp.bfloat16)
        spot = end


def input_kernel(joined_ref, w_ref, x_ref, back_ref, gain_ref, out_ref, dgain_ref):
    length = x_ref.shape[0]
    size = min(256, length)
    count = joined_ref.shape[1]
    weights = w_ref[...].reshape(-1, D)[:count]
    dgain_ref[...] = jnp.zeros_like(dgain_ref)
    for start in range(0, length, size):
        rows = slice(start, start + size)
        inner = product(joined_ref[rows], weights, 1, 0)
        hidden = x_ref[rows]
        inverse = scaled_norm(hidden, 1.0)[1]
        scaled = inner * gain_ref[0:1]
        dgain_ref[...] += jnp.sum(inner * hidden * inverse, axis=0, keepdims=True)
        grad = (
            back_ref[rows]
            + inverse * scaled
            - hidden
            * (inverse * inverse * inverse)
            * jnp.mean(scaled * hidden, axis=-1, keepdims=True)
        )
        out_ref[:, rows] = grad.T.astype(jnp.bfloat16)


def ortho_sweeps(block, held_ref):
    size = min(block.shape)
    left = block.shape[0] < block.shape[1]
    block = block.astype(jnp.float32)
    held_ref[...] = block * (1.0 / (jnp.sqrt(jnp.sum(block * block)) + 1e-07))
    row = lax.broadcasted_iota(jnp.int32, (size, size), 0)
    diagonal = row == lax.broadcasted_iota(jnp.int32, (size, size), 1)

    def sweep(index, carry):
        held = held_ref[...]
        scaled = held.astype(jnp.bfloat16)
        side = 1 if left else 0
        gram = product(scaled, scaled, side, side)
        mean = jnp.sum(jnp.where(diagonal, gram, 0.0)) / size
        rest = jnp.where(diagonal, gram - mean, gram)
        rest_low = rest.astype(jnp.bfloat16)
        poly = (POLY_TWO + 2.0 * POLY_THREE * mean) * rest + POLY_THREE * product(
            rest_low, rest_low, 1, 0
        )
        poly_low = poly.astype(jnp.bfloat16)
        turned = product(poly_low, scaled, 1, 0) if left else product(scaled, poly_low, 1, 0)
        held_ref[...] = (POLY_ONE + POLY_TWO * mean + POLY_THREE * mean * mean) * held + turned
        return carry

    lax.fori_loop(0, ORTHO_STEPS, sweep, 0)
    return held_ref[...].astype(jnp.bfloat16)


def ortho_kernel(block_ref, out_ref, held_ref):
    out_ref[...] = ortho_sweeps(block_ref[...], held_ref)


def solve_kernel(
    spot_ref, factor_ref, momenta_ref, feed_ref, attn_ref, out_ref, momentum_ref, block_ref, held_ref
):
    kind, top, around, core, start, count = [spot_ref[i] for i in range(6)]
    factor = factor_ref[0, 0]
    lead, size = block_ref.shape[:2]
    rows = size // 2

    def fetch(first, column, target, width):
        source = momenta_ref.at[pl.ds(first, lead), pl.ds(column, width)]
        pltpu.sync_copy(source, momentum_ref.at[:, pl.ds(target, width)])

    def mixed(spot, grad):
        momentum = momentum_ref[:, spot].astype(jnp.float32)
        return MOMENTUM_DECAY * momentum + factor * grad.astype(jnp.float32)

    @pl.when(kind == 0)
    def _():
        fetch(top * lead, 0, 0, size)

    @pl.when(kind == 1)
    def _():
        fetch(0, size, 0, rows)
        fetch(lead, size, rows, rows)

    @pl.when(kind < 2)
    def _():
        block_ref[...] = mixed(slice(None), feed_ref[...]).astype(jnp.bfloat16)

    @pl.when(kind >= 2)
    def _():
        fetch(top * lead, size + rows, 0, rows)
        index = lax.broadcasted_iota(jnp.int32, (lead, rows, D), 0) * rows
        index = index + lax.broadcasted_iota(jnp.int32, (lead, rows, D), 1)
        here = (index >= start) & (index < start + count)
        block = jnp.where(here, mixed(slice(0, rows), attn_ref[...]), 0.0)
        block_ref[:, :rows] = block.astype(jnp.bfloat16)
        block_ref[:, rows:] = jnp.zeros_like(block_ref[:, rows:])

    done = ortho_sweeps(block_ref[...].reshape(lead * size, D), held_ref)
    block_ref[...] = done.reshape(lead, size, D)
    second = (kind == 1) & (top == 1)
    for chip in range(4):
        found = block_ref[(around * 4 + chip) * 2 + core]
        out_ref[chip, :rows] = jnp.where(second, found[rows:], found[:rows])
        out_ref[chip, rows:] = found[rows:]


def solve(spots, factor, momenta, feed, attn):
    lead, size = feed.shape[:2]
    in_vmem = pl.BlockSpec(memory_space=pltpu.VMEM)
    in_smem = pl.BlockSpec(memory_space=pltpu.SMEM)
    return pl.pallas_call(
        solve_kernel,
        out_shape=shape_of((4, size, D), jnp.bfloat16),
        in_specs=[in_smem, in_smem, pl.BlockSpec(memory_space=pl.ANY), in_vmem, in_vmem],
        out_specs=in_vmem,
        scratch_shapes=[
            pltpu.VMEM((lead, size, D), jnp.bfloat16),
            pltpu.VMEM((lead, size, D), jnp.bfloat16),
            pltpu.VMEM((lead * size, D), jnp.float32),
        ],
        compiler_params=pltpu.CompilerParams(vmem_limit_bytes=VMEM_BYTES),
    )(spots, factor, momenta, feed, attn)


def orthogonalize(block):
    rows, columns = block.shape
    small, large = min(block.shape), max(block.shape)
    return call(
        ortho_kernel,
        shape_of(block.shape, jnp.bfloat16),
        (block,),
        2 * ORTHO_STEPS * small * small * (2 * large + small),
        scratch=(pltpu.VMEM((rows, columns), jnp.float32),),
    )


def block_list():
    q_rows = HEADS * HEAD_DIM
    kv_rows = KV_HEADS * HEAD_DIM
    return (
        (0, 0, q_rows),
        (0, q_rows, kv_rows),
        (0, q_rows + kv_rows, kv_rows),
        (0, q_rows + 2 * kv_rows, q_rows),
        (1, 0, FF),
        (1, FF, FF),
        (2, 0, FF),
    )


def row_scales(array_id):
    pieces = [
        jnp.full((row_count,), 0.2 * math.sqrt(max(row_count, D)), jnp.float32)
        for owner_id, row_start, row_count in block_list()
        if owner_id == array_id
    ]
    return jnp.concatenate(pieces, axis=0)


def split_rows(value):
    high = lax.reduce_precision(value, 8, 7)
    return jnp.concatenate([high.astype(jnp.bfloat16), (value - high).astype(jnp.bfloat16)], axis=0)


def joined_rows(rows):
    half = rows.shape[0] // 2
    return rows[:half].astype(jnp.float32) + rows[half:].astype(jnp.float32)


class Owners:
    def __init__(self, place, devices):
        self.place, self.devices = place, devices
        self.top_bit = devices.bit_length() - 2
        self.core, self.across, self.along = [bit_of(place, bit) for bit in range(3)]
        self.kind = 2 * self.along + self.across
        self.top = bit_of(place, self.top_bit)
        self.other_bits = list(range(3, self.top_bit)) + [0]

    def widen(self, blocks, other, bit):
        spread = ordered(bit_of(self.place, bit), blocks, other, 1 if bit == 0 else 0)
        return spread.reshape((-1,) + blocks.shape[1:])

    def attn_span(self, large):
        q_rows, kv_rows = HEADS * HEAD_DIM, KV_HEADS * HEAD_DIM
        large_start = jnp.where(self.top == 0, 0, kv_rows)
        small_start = jnp.where(self.top == 0, q_rows, 0)
        return jnp.where(large, large_start, small_start), jnp.where(large, q_rows, kv_rows)

    def solve(self, factor, feed, attn, momenta, rows):
        lead = self.devices // 2
        around = (self.place >> 3) & (self.devices // 16 - 1)
        start, count = self.attn_span(self.kind == 2)
        if rows % 16 == 0:
            spots = jnp.stack([self.kind, self.top, around, self.core, start, count])
            return solve(spots, factor[None, None], momenta, feed, attn)
        half = lax.dynamic_slice_in_dim(momenta, self.top * lead, lead, 0)
        wide = lambda array: jnp.pad(array, ((0, 0), (0, rows), (0, 0)))
        down = momenta[:, 2 * rows : 3 * rows].reshape(2, lead, rows, D)
        down = down.transpose(1, 0, 2, 3).reshape(lead, 2 * rows, D)
        attn_momentum = wide(half[:, 3 * rows :])
        momentum = jnp.where(self.kind == 0, half[:, : 2 * rows], down)
        momentum = jnp.where(self.kind >= 2, attn_momentum, momentum).astype(jnp.float32)
        grad = jnp.where(self.kind >= 2, wide(attn), feed).astype(jnp.float32)
        index = jnp.arange(lead)[:, None] * rows + jnp.arange(2 * rows)[None, :]
        here = (index >= start) & (index < start + count) & (jnp.arange(2 * rows) < rows)
        block = MOMENTUM_DECAY * momentum + factor * grad
        block = jnp.where((self.kind < 2) | here[..., None], block, 0.0).astype(jnp.bfloat16)
        done = orthogonalize(block.reshape(-1, D)).reshape(-1, 4, 2, 2 * rows, D)
        done = pick(pick(done, 0, around), 1, self.core)
        second = (self.kind == 1) & (self.top == 1)
        return jnp.where(second, jnp.roll(done, rows, axis=1), done)

    def spread(self, result, rows):
        came = {0: pick(result, 0, self.kind)}
        for flip in (1, 2, 3):
            pairs = [(i, i ^ (flip << 1)) for i in range(self.devices)]
            came[flip] = lax.ppermute(pick(result, 0, self.kind ^ flip), AXES, pairs)

        def from_chip(chip, count):
            found = came[0][:count]
            for flip in (1, 2, 3):
                found = jnp.where(self.kind ^ flip == chip, came[flip][:count], found)
            return found

        start, count = self.attn_span(True)
        row = (self.place & (self.devices // 2 - 1)) * rows
        large = (row >= start) & (row < start + count)
        attn = jnp.where(large, from_chip(2, rows), from_chip(3, rows))
        return attn, from_chip(0, 2 * rows), from_chip(1, rows)


class FeedGather:
    def __init__(self, owners, gate_up, down):
        self.owners = owners
        rows = down.shape[0]
        down = down.astype(jnp.bfloat16)
        other = swap(down, owners.top_bit, owners.devices)
        self.down = ordered(owners.top, down, other, 0).reshape(2 * rows, D)
        self.blocks = gate_up.astype(jnp.bfloat16)

    def hop(self, bit):
        owners = self.owners
        if bit == 1:
            sent = jnp.where(owners.across == 0, self.down, self.blocks)
            kept = jnp.where(owners.across == 0, self.blocks, self.down)
            self.blocks = owners.widen(kept[None], swap(sent, bit, owners.devices)[None], bit)
        else:
            other = swap(self.blocks, bit, owners.devices)
            self.blocks = owners.widen(self.blocks, other, bit)


class AttnGather:
    def __init__(self, owners, attn, sums):
        self.owners, self.sums = owners, sums
        self.blocks = attn.astype(jnp.bfloat16)[None]

    def hop(self, bit):
        owners = self.owners
        if bit == owners.top_bit:
            self.sums = self.sums + joined_rows(swap(split_rows(self.sums), bit, owners.devices))
            return
        shape = self.blocks.shape
        count = shape[0] * shape[1]
        message = jnp.concatenate(
            [self.blocks.reshape(count, D), split_rows(self.sums)], axis=0
        )
        other = swap(message, bit, owners.devices)
        self.sums = self.sums + joined_rows(other[count:])
        self.blocks = owners.widen(self.blocks, other[:count].reshape(shape), bit)


def meet(feed, attn):
    feed.blocks, attn.blocks, attn.sums = lax.optimization_barrier(
        (feed.blocks, attn.blocks, attn.sums)
    )


def per_device(
    inputs,
    out_grad,
    lang_tags,
    attn_master,
    gate_up_master,
    down_master,
    attn_momentum,
    gate_up_momentum,
    down_momentum,
    norm_gains,
    gain_first,
    gain_second,
):
    devices = lax.axis_size(("dp", "sub"))
    device_place = lax.axis_index(("dp", "sub"))
    q_rows = HEADS * HEAD_DIM
    kv_rows = KV_HEADS * HEAD_DIM
    qkv_rows = q_rows + 2 * kv_rows
    tag_hot = (lang_tags[:, None] == jnp.arange(NUM_TAGS, dtype=jnp.int32)[None, :]).astype(
        jnp.float32
    )
    masters = (attn_master, gate_up_master, down_master)
    attn_low = attn_master.astype(jnp.bfloat16)
    gate_up_low = gate_up_master.astype(jnp.bfloat16)
    down_low = down_master.astype(jnp.bfloat16)
    tag_rows = jnp.pad(jnp.sum(tag_hot, axis=0)[None], ((0, 15), (0, D - NUM_TAGS)))
    own_weights, other_weights, hidden_in = gather_rows(
        attn_low, device_place, devices, inputs.astype(jnp.float32)
    )
    ffn_low = jnp.concatenate([gate_up_low, down_low, tag_rows.astype(jnp.bfloat16)], axis=0)
    ffn_weights = lax.all_gather(ffn_low, AXES, axis=0)
    length = inputs.shape[0]
    wide_cos, wide_sin, tall_cos, tall_sin = [jnp.asarray(t) for t in rotary_rows(length)]
    low, single = jnp.bfloat16, jnp.float32
    place = device_place
    core = bit_of(place, 0)[None, None]
    in_smem = pl.BlockSpec(memory_space=pltpu.SMEM)
    in_vmem = pl.BlockSpec(memory_space=pltpu.VMEM)
    even = down_low.shape[0] % 16 == 0
    attn_outs = (
        shape_of((length, q_rows), low),
        shape_of((length, kv_rows), low),
        shape_of((length, kv_rows), low),
        shape_of((length, D), low),
        shape_of((length, q_rows), low),
        shape_of((HEADS, length), single),
        shape_of((HEADS, length), single),
        shape_of((length, D), single),
        shape_of((length, D), low),
    )
    if even:
        pieces = (own_weights, other_weights)
        attn_outs += (shape_of((devices // 2, 2) + attn_low.shape, low),)
    else:
        whole_weights = ordered(bit_of(place, 0), own_weights, other_weights, 1)
        pieces = (whole_weights.reshape(16, 2, -1, D),)
    queries, keys, values, normed_one, attended_low, peaks, totals, residual, normed_two, *attn_w = call(
        attention_kernel if even else whole_attention_kernel,
        attn_outs,
        (core, hidden_in, *pieces, norm_gains, wide_cos, wide_sin),
        2 * length * D * 3 * (qkv_rows + q_rows),
        in_specs=[in_smem] + [in_vmem] * (4 + len(pieces)),
        out_specs=(in_vmem,) * len(attn_outs),
    )
    attn_weights = attn_w[0] if even else pieces[0]
    momenta_low = jnp.concatenate(
        [part.astype(low) for part in (gate_up_momentum, down_momentum, attn_momentum)], axis=0
    )
    ffn_weights, normed_two, momenta_low = lax.optimization_barrier(
        (ffn_weights, normed_two, momenta_low)
    )
    momenta_low = lax.all_gather(momenta_low, AXES, axis=0)
    ffn_rows = gate_up_low.shape[0] + down_low.shape[0]
    gate_up_rows, down_rows = gate_up_low.shape[0], down_low.shape[0]
    if even:
        gate_up_weights = down_weights = ffn_weights
        down_skip = gate_up_rows // down_rows
    else:
        gate_up_weights = ffn_weights[:, :gate_up_rows].reshape(32, -1, D)
        down_weights = ffn_weights[:, gate_up_rows:ffn_rows].reshape(32, -1, D)
        gate_up_rows, down_rows = gate_up_weights.shape[1], down_weights.shape[1]
        down_skip = 0
    tag_hot_row = jnp.pad(tag_hot[:1], ((0, 0), (0, D - NUM_TAGS)))
    tags = ffn_weights if even else ffn_weights[:, ffn_rows:]
    chunk = 768 if even else 384
    steps = FF // chunk
    held_once = dict(pipeline_mode=pl.Buffered(1))
    whole = lambda *shape: pl.BlockSpec(shape, lambda c: (0,) * len(shape), **held_once)
    gate_blocks, down_blocks = chunk // gate_up_rows, chunk // down_rows
    part = lambda skip: pl.BlockSpec((gate_blocks, gate_up_rows, D), lambda c: (c + skip, 0, 0))
    down_part = pl.BlockSpec((down_blocks, down_rows, D), lambda c: (c, down_skip, 0))
    if even:
        cut = (gate_up_rows + down_rows) * 9 // 16 // 16 * 16
        other_cut = gate_up_rows + down_rows - cut
        pairs = devices // 2
        grad_outs = tuple(
            shape_of((pairs, size, D), kind) for size in (cut, other_cut) for kind in (single, low)
        )
        grad_specs = tuple(whole(*out.shape) for out in grad_outs)
    else:
        grad_outs = (
            shape_of((16, gate_up_rows, D), single),
            shape_of((16, gate_up_rows, D), single),
            shape_of((32, down_rows, D), single),
        )
        grad_specs = (part(0), part(0), pl.BlockSpec((down_blocks, down_rows, D), lambda c: (c, 0, 0)))
    outputs, residual_grad, attended_grad, o_part, gain_two, *ffn_grads = call(
        feed_kernel,
        (
            shape_of((D, length), low),
            shape_of((length, D), single),
            shape_of((length, q_rows), low),
            shape_of((q_rows, D), single),
            shape_of((1, D), single),
            *grad_outs,
        ),
        (
            core,
            tag_hot_row,
            tags,
            normed_two,
            residual,
            out_grad.T,
            attended_low,
            gate_up_weights,
            gate_up_weights,
            down_weights,
            attn_weights,
            norm_gains,
        ),
        2 * 3 * length * D * (3 * FF + q_rows),
        grid=(steps,),
        in_specs=[
            in_smem,
            whole(1, D),
            pl.BlockSpec((devices, 16, D), lambda c: (0, ffn_rows // 16 if even else 0, 0), **held_once),
            whole(length, D),
            whole(length, D),
            whole(D, length),
            whole(length, q_rows),
            part(0),
            part(steps),
            down_part,
            whole(*attn_weights.shape),
            whole(2, D),
        ],
        out_specs=(
            whole(D, length),
            whole(length, D),
            whole(length, q_rows),
            whole(q_rows, D),
            whole(1, D),
            *grad_specs,
        ),
        scratch=(
            pltpu.VMEM((length, D), single),
            pltpu.VMEM((length, D), single),
            pltpu.VMEM((length, D), low),
            pltpu.VMEM((3, length, chunk), low),
        ),
    )
    bits = range(devices.bit_length() - 1)
    if even:
        first_held, first_sent, second_held, second_sent = ffn_grads
        sums = [
            Sums(first_held, place, devices, bits[1:], swap(first_sent, 0, devices)),
            Sums(second_held, place, devices, bits[1:], swap(second_sent, 0, devices)),
        ]
    else:
        gate_up_part = jnp.concatenate([g.reshape(-1, D) for g in ffn_grads[:2]], axis=0)
        sums = [
            Sums(gate_up_part.reshape(devices, -1, D), place, devices, bits),
            Sums(ffn_grads[2].reshape(devices, -1, D), place, devices, bits),
        ]
        for s in sums:
            s.hop(0)
    head_grads = []
    for head in range(KV_HEADS):
        head_grads.append(
            call(
                partial(head_kernel, head),
                (
                    shape_of((length, q_rows // KV_HEADS), low),
                    shape_of((length, HEAD_DIM), low),
                    shape_of((length, HEAD_DIM), low),
                ),
                (queries, keys, values, attended_grad, peaks, totals, tall_cos, tall_sin),
                2 * 2 * length * length * q_rows,
                scratch=(
                    pltpu.VMEM((length, HEAD_DIM), single),
                    pltpu.VMEM((length, HEAD_DIM), single),
                ),
            )
        )
        if head == 0:
            attended_grad, head_grads[0] = after((attended_grad, head_grads[0]), sums)
            sums[0].hop(1)
            sums[1].hop(2)
    normed_one, momenta_low, head_grads = after((normed_one, momenta_low, head_grads), sums)
    proj_parts = [head_grads[head][kind] for kind in range(3) for head in range(KV_HEADS)]
    sums[0].hop(2)
    sums[1].hop(1)
    if even:
        grad_outs = (
            shape_of((pairs, attn_low.shape[0], D), single),
            shape_of((pairs, attn_low.shape[0], D), low),
        )
    else:
        grad_outs = (shape_of((qkv_rows + q_rows, D), single),)
    joined, *attn_grads = call(
        qkv_kernel,
        (shape_of((length, qkv_rows), low), *grad_outs),
        (core, *proj_parts, normed_one, o_part),
        2 * length * D * qkv_rows,
        in_specs=[in_smem] + [in_vmem] * 11,
        out_specs=(in_vmem,) * (1 + len(grad_outs)),
    )
    if even:
        held, sent = attn_grads
        sent = after(sent, sums)
        cut = attn_low.shape[0] // 2
        came = swap(sent, 0, devices)
        late = [
            Sums(held[:, :cut], place, devices, bits[1:], came[:, :cut]),
            Sums(held[:, cut:], place, devices, bits[1:], came[:, cut:]),
        ]
    else:
        late = [Sums(attn_grads[0].reshape(devices, -1, D), place, devices, bits)]
        late[0].hop(0)
    for s in sums:
        s.hop(3)
    residual_grad = after(residual_grad, late)
    for index, order in enumerate(((1, 2), (2, 1))[: len(late)]):
        late[index].hop(order[0])
    input_grad, gain_one = call(
        input_kernel,
        (shape_of((D, length), low), shape_of((1, D), single)),
        (joined, attn_weights, hidden_in, residual_grad, norm_gains),
        2 * length * D * qkv_rows,
    )
    input_grad = after(input_grad, late + sums)
    for index, order in enumerate(((1, 2), (2, 1))[: len(late)]):
        late[index].hop(order[1])
    for bit in bits[4:]:
        for s in sums:
            s.hop(bit)
    for s in late:
        s.hop(3)
    after(0, late + sums)
    if even:
        cut = first_held.shape[1]
        first, second = [s.total() for s in sums]
        gate_up_sum = jnp.concatenate([first, second[: gate_up_rows - cut]], axis=0)
        down_sum = second[gate_up_rows - cut :]
    else:
        gate_up_sum, down_sum = [s.total() for s in sums]
    owners = Owners(place, devices)
    feed = FeedGather(owners, gate_up_sum, down_sum)
    for bit in bits[4:]:
        for s in late:
            s.hop(bit)
    feed.down = after(feed.down, late)
    attn_sum = jnp.concatenate([s.total() for s in late], axis=0)
    squares = (
        jnp.sum(attn_sum * attn_sum)
        + jnp.sum(gate_up_sum * gate_up_sum)
        + jnp.sum(down_sum * down_sum)
    )
    small_sums = jnp.concatenate([gain_one, gain_two, jnp.full((1, D), squares)], axis=0)
    attn = AttnGather(owners, attn_sum, small_sums)
    others = owners.other_bits
    for attn_bit, feed_bit in zip([owners.top_bit, 1, 2], [1, 2, others[0]]):
        attn.hop(attn_bit)
        feed.hop(feed_bit)
        if feed_bit < 3:
            meet(feed, attn)
    for bit in others:
        attn.hop(bit)
    for bit in others[1:]:
        feed.hop(bit)
    gain_total, small_sums = attn.sums[:2], attn.sums
    square_total = small_sums[2, 0] + jnp.sum(gain_total * gain_total)
    grad_norm = jnp.sqrt(square_total)
    param_count = (qkv_rows + q_rows + 3 * FF) * D + 2 * D
    factor = jnp.minimum(1.0, CLIP_SCALE * math.sqrt(devices * length * param_count) / grad_norm)
    down_count = down_low.shape[0]
    solved = owners.solve(factor, feed.blocks, attn.blocks, momenta_low, down_count)
    factor, solved = lax.optimization_barrier((factor, solved))
    attn_grad = attn_sum * factor
    gate_up_grad = gate_up_sum * factor
    down_grad = down_sum * factor
    gain_grad = gain_total * factor
    attn_moment = MOMENTUM_DECAY * attn_momentum + attn_grad
    gate_up_moment = MOMENTUM_DECAY * gate_up_momentum + gate_up_grad
    down_moment = MOMENTUM_DECAY * down_momentum + down_grad
    ortho_shards = owners.spread(solved, down_count)
    new_masters = []
    for array_id in range(3):
        shard_rows = masters[array_id].shape[0]
        scale_rows = lax.dynamic_slice_in_dim(
            row_scales(array_id), device_place * shard_rows, shard_rows, 0
        )
        new_masters.append(
            masters[array_id]
            - MATRIX_RATE
            * (scale_rows[:, None] * ortho_shards[array_id] + MATRIX_DECAY * masters[array_id])
        )
    first_new = BETA_FIRST * gain_first + (1.0 - BETA_FIRST) * gain_grad
    second_new = BETA_SECOND * gain_second + (1.0 - BETA_SECOND) * gain_grad * gain_grad
    gains_new = norm_gains - GAIN_RATE * (first_new / (1.0 - BETA_FIRST**STEP_NUMBER)) / (
        jnp.sqrt(second_new / (1.0 - BETA_SECOND**STEP_NUMBER)) + ADAM_EPS
    )
    return (
        outputs.T,
        input_grad.T,
        attn_grad,
        gate_up_grad,
        down_grad,
        grad_norm,
        attn_moment,
        gate_up_moment,
        down_moment,
        new_masters[0],
        new_masters[1],
        new_masters[2],
        gain_grad,
        first_new,
        second_new,
        gains_new,
    )


def solution(mesh):
    placed = (
        P(("dp", "sub"), None),
        P(("dp", "sub"), None),
        P(("dp", "sub")),
        P(("dp", "sub"), None),
        P(("dp", "sub"), None),
        P(("dp", "sub"), None),
        P(("dp", "sub"), None),
        P(("dp", "sub"), None),
        P(("dp", "sub"), None),
        P(),
        P(),
        P(),
    )
    return jax.shard_map(
        per_device,
        mesh=mesh,
        in_specs=placed,
        out_specs=(
            P(("dp", "sub"), None),
            P(("dp", "sub"), None),
            P(("dp", "sub"), None),
            P(("dp", "sub"), None),
            P(("dp", "sub"), None),
            P(),
            P(("dp", "sub"), None),
            P(("dp", "sub"), None),
            P(("dp", "sub"), None),
            P(("dp", "sub"), None),
            P(("dp", "sub"), None),
            P(("dp", "sub"), None),
            P(),
            P(),
            P(),
            P(),
        ),
        check_vma=False,
    )
```

```python
from functools import partial
import math

import jax
import jax.numpy as jnp
import numpy as np
from jax import lax
from jax.experimental import pallas as pl
from jax.experimental.pallas import tpu as pltpu
from jax.sharding import PartitionSpec as P

D = 576
HEADS = 9
KV_HEADS = 3
HEAD_DIM = 64
FF = 1536
NUM_TAGS = 8
ORTHO_STEPS = 5
STEP_NUMBER = 10


NORM_EPS = 1e-05
ROPE_BASE = 100000.0
POLY_ONE = 3.4445
POLY_TWO = -4.775
POLY_THREE = 2.0315
MOMENTUM_DECAY = 0.95
MATRIX_RATE = 0.2
MATRIX_DECAY = 0.1
GAIN_RATE = 1.0
BETA_FIRST = 0.9
BETA_SECOND = 0.95
ADAM_EPS = 1e-08
CLIP_SCALE = 0.002


AXES = ("dp", "sub")


def bit_of(place, bit):
    return (place >> bit) & 1


def exchange(array, flip, devices, source=None):
    pairs = [(i, i ^ flip) for i in range(devices) if source is None or source(i)]
    return lax.ppermute(array, AXES, pairs)


def bit_groups(devices):
    bits = devices.bit_length() - 1
    return [(0,)] + [tuple(range(bit, min(bit + 2, bits))) for bit in range(1, bits, 2)]


def flips_of(group):
    return [part << group[0] for part in range(1, 1 << len(group))]


def pick(array, axis, index):
    return lax.dynamic_index_in_dim(array, index, axis, keepdims=False)


def gather_hop(blocks, group, devices, front=False, source=None):
    came = [exchange(blocks, flip, devices, source) for flip in flips_of(group)]
    stacked = jnp.stack([blocks] + came, axis=0 if front else 1)
    return stacked.reshape((-1,) + blocks.shape[1:])


def in_order(blocks, place):
    return jnp.take(blocks, jnp.arange(blocks.shape[0]) ^ place, axis=0)


class Sums:
    def __init__(self, held, place, devices, bits, came=()):
        self.place, self.devices, self.bits = place, devices, list(bits)
        self.shape = held.shape[-2:]
        self.held, self.came = held, list(came)

    def hop(self, *group):
        low, width = self.bits.index(group[0]), len(group)
        high = len(self.bits) - low - width
        terms = [
            term.reshape((1 << high, 1 << width, 1 << low) + self.shape)
            for term in [self.held] + self.came
        ]
        mine = (self.place >> group[0]) & ((1 << width) - 1)

        def part(index):
            chosen = [pick(term, 1, index).astype(jnp.float32) for term in terms]
            return sum(chosen[1:], chosen[0]).reshape((-1,) + self.shape)

        sent = [part(mine ^ flip).astype(jnp.bfloat16) for flip in range(1, 1 << width)]
        self.held = part(mine)
        self.came = [exchange(s, f, self.devices) for s, f in zip(sent, flips_of(group))]
        for bit in group:
            self.bits.remove(bit)

    def total(self):
        return sum([term.astype(jnp.float32) for term in self.came], self.held)


def after(value, sums):
    value, came = lax.optimization_barrier((value, [s.came for s in sums]))
    for s, c in zip(sums, came):
        s.came = c
    return value


SCORE_SCALE = HEAD_DIM ** (-0.5)
MASKED = -1e30


def product(left, right, left_dim, right_dim):
    return lax.dot_general(
        left, right, (((left_dim,), (right_dim,)), ((), ())), preferred_element_type=jnp.float32
    )


def call(kernel, outs, args, flops, mib, grid=(), in_specs=None, out_specs=None, scratch=()):
    specs = {} if in_specs is None else dict(in_specs=in_specs, out_specs=out_specs)
    listed = tuple(outs) if isinstance(outs, (tuple, list)) else (outs,)
    moved = sum(math.prod(a.shape) * a.dtype.itemsize for a in tuple(args) + listed)
    return pl.pallas_call(
        kernel,
        out_shape=outs,
        grid=grid,
        scratch_shapes=scratch,
        compiler_params=pltpu.CompilerParams(vmem_limit_bytes=mib * 2**20),
        cost_estimate=pl.CostEstimate(flops=int(flops), bytes_accessed=moved, transcendentals=0),
        **specs,
    )(*args)


def shape_of(shape, dtype):
    return jax.ShapeDtypeStruct(shape, dtype)


def rotary_rows(length):
    half_dim = HEAD_DIM // 2
    frequency = np.float32(ROPE_BASE) ** (
        -(np.arange(half_dim, dtype=np.float32) * np.float32(2.0 / HEAD_DIM))
    )
    angles = np.arange(length, dtype=np.float32)[:, None] * frequency[None, :].astype(np.float32)
    cosine, sine = np.cos(angles), np.sin(angles)
    wide_cosine = np.concatenate([cosine] * 4, axis=1)
    wide_sine = np.concatenate([-sine, sine, -sine, sine], axis=1)
    return wide_cosine, wide_sine, cosine.T.copy(), sine.T.copy()


def causal_mask(size):
    key_pos = lax.broadcasted_iota(jnp.int32, (size, size), 0)
    query_pos = lax.broadcasted_iota(jnp.int32, (size, size), 1)
    return key_pos <= query_pos


def scores_by_key(keys, queries, mask):
    size = queries.shape[0]
    before = keys.shape[0] - size
    raw = product(keys, queries, 1, 1)
    last = jnp.where(mask, raw[before:], MASKED)
    return last if before == 0 else jnp.concatenate([raw[:before], last], axis=0)


def scaled_norm(values, gain):
    inverse = lax.rsqrt(jnp.mean(values * values, axis=-1, keepdims=True) + NORM_EPS)
    return values * inverse * gain, inverse


def attention_kernel(
    place_ref, x_ref, own_ref, other_ref, gain_ref, cos_ref, sin_ref,
    q_ref, k_ref, v_ref, normed_ref, low_ref, peak_ref, total_ref, res_ref, two_ref, joined_ref,
    heads_ref,
):
    length = x_ref.shape[0]
    q_rows = HEADS * HEAD_DIM
    kv_rows = KV_HEADS * HEAD_DIM
    turned = q_rows + kv_rows
    if other_ref is None:
        w_ref = own_ref
    else:
        core, pair = place_ref[0, 0] & 1, place_ref[0, 0] >> 1
        for index in range(own_ref.shape[0]):
            joined_ref[index ^ pair, core] = own_ref[index]
            joined_ref[index ^ pair, 1 - core] = other_ref[index]
        w_ref = joined_ref
    weights = w_ref[...].reshape(-1, D)
    size = min(256, length)
    lane = lax.broadcasted_iota(jnp.int32, (size, turned), 1)
    first = lane % HEAD_DIM < HEAD_DIM // 2
    for start in range(0, length, size):
        rows = slice(start, start + size)
        normed = scaled_norm(x_ref[rows], gain_ref[0:1])[0].astype(jnp.bfloat16)
        normed_ref[rows] = normed
        raw = product(normed, weights[: turned + kv_rows], 1, 1)
        both = raw[:, :turned]
        swapped = jnp.where(
            first,
            pltpu.roll(both, turned - HEAD_DIM // 2, 1),
            pltpu.roll(both, HEAD_DIM // 2, 1),
        )
        cosine = jnp.concatenate([cos_ref[rows]] * (turned // 128), axis=1)
        sine = jnp.concatenate([sin_ref[rows]] * (turned // 128), axis=1)
        both = both * cosine + swapped * sine
        q_ref[rows] = both[:, :q_rows].astype(jnp.bfloat16)
        k_ref[rows] = both[:, q_rows:].astype(jnp.bfloat16)
        v_ref[rows] = raw[:, turned:].astype(jnp.bfloat16)
    size = min(512, length)
    mask = causal_mask(size)
    group = HEADS // KV_HEADS
    span = lambda head: slice(head * HEAD_DIM, (head + 1) * HEAD_DIM)
    for head in range(HEADS):
        heads_ref[head] = q_ref[:, span(head)] * jnp.bfloat16(SCORE_SCALE)
    for head in range(KV_HEADS):
        heads_ref[HEADS + head] = k_ref[:, span(head)]
        heads_ref[HEADS + KV_HEADS + head] = v_ref[:, span(head)]

    def attend(head, carry):
        keys_at = HEADS + head // group
        for start in range(0, length, size):
            end = start + size
            queries = heads_ref[head, start:end]
            scores = scores_by_key(heads_ref[keys_at, :end], queries, mask)
            peak = jnp.max(scores, axis=0, keepdims=True)
            shifted = jnp.exp(scores - peak)
            inverse = 1.0 / jnp.sum(shifted, axis=0, keepdims=True)
            prob_low = (shifted * inverse).astype(jnp.bfloat16)
            out = product(heads_ref[keys_at + KV_HEADS, :end], prob_low, 0, 0)
            heads_ref[head, start:end] = out.T.astype(jnp.bfloat16)
            peak_ref[head, :, start:end] = peak
            total_ref[head, :, start:end] = inverse
        return carry

    lax.fori_loop(0, HEADS, attend, 0)
    low_ref[...] = jnp.concatenate([heads_ref[head] for head in range(HEADS)], axis=1)
    size = min(256, length)
    for start in range(0, length, size):
        rows = slice(start, start + size)
        residual = x_ref[rows] + product(low_ref[rows], weights[turned + kv_rows :], 1, 0)
        res_ref[rows] = residual
        two_ref[rows] = scaled_norm(residual, gain_ref[1:2])[0].astype(jnp.bfloat16)


def whole_attention_kernel(place_ref, x_ref, own_ref, *refs):
    attention_kernel(place_ref, x_ref, own_ref, None, *refs[:-1], None, refs[-1])


def feed_kernel(
    place_ref, tags_ref, two_ref, res_ref, grad_ref, low_ref, *refs,
    devices, gathered, gate_rows, down_rows,
):
    cut = 1 if gathered else 2
    weight_refs, refs = refs[:cut], refs[cut:]
    attn_ref, gain_ref, out_ref, back_ref, att_ref, do_ref, dgain_ref, *refs = refs
    *grad_refs, sum_ref, inner_ref, coming_ref, hidden_ref = refs
    step = pl.program_id(0)
    length = two_ref.shape[0]
    size = min(256, length)
    core = place_ref[0, 0] & 1
    chunk = hidden_ref.shape[2]
    gate_blocks, down_blocks = chunk // gate_rows, chunk // down_rows
    count = jnp.sum(tags_ref[0:1] * tags_ref[1:2], axis=1, keepdims=True)
    weight = devices / (NUM_TAGS * count)
    if gathered:
        gate_ref, down_ref, first_row = weight_refs[0], weight_refs[0], gate_rows
    else:
        (gate_ref, down_ref), first_row = weight_refs, 0
    gate_spots = pl.ds(step * gate_blocks, gate_blocks)
    up_spots = pl.ds(FF // gate_rows + step * gate_blocks, gate_blocks)
    gate_w = gate_ref[gate_spots, :gate_rows].reshape(-1, D)
    up_w = gate_ref[up_spots, :gate_rows].reshape(-1, D)
    down_spots = pl.ds(step * down_blocks, down_blocks)
    down_w = down_ref[down_spots, first_row : first_row + down_rows].reshape(-1, D)
    o_w = attn_ref[-(attn_ref.shape[0] * HEADS // (2 * (HEADS + KV_HEADS))) :].reshape(-1, D)

    @pl.when(step == 0)
    def _():
        for start in range(0, length, size):
            rows = slice(start, start + size)
            grad = grad_ref[:, rows].astype(jnp.float32).T
            coming_ref[rows] = (grad * weight).astype(jnp.bfloat16)
        sum_ref[...] = jnp.zeros_like(sum_ref)
        inner_ref[...] = jnp.zeros_like(inner_ref)

    for start in range(0, length, 2 * size):
        rows = slice(start, min(start + 2 * size, length))
        two = two_ref[rows]
        gate = product(two, gate_w, 1, 1)
        up = product(two, up_w, 1, 1)
        sigmoid = 0.5 * jnp.tanh(0.5 * gate) + 0.5
        silu = gate * sigmoid
        activation = (silu * up).astype(jnp.bfloat16)
        act_grad = product(coming_ref[rows], down_w, 1, 1)
        gate_low = act_grad * up * (sigmoid * (1.0 + gate * (1.0 - sigmoid)))
        gate_low = gate_low.astype(jnp.bfloat16)
        up_low = (act_grad * silu).astype(jnp.bfloat16)
        sum_ref[rows] += product(activation, down_w, 1, 0)
        inner_ref[rows] += product(gate_low, gate_w, 1, 0) + product(up_low, up_w, 1, 0)
        for kind, value in enumerate((gate_low, up_low, activation)):
            hidden_ref[kind, rows] = value
    gate_grad = product(hidden_ref[0], two_ref[...], 0, 0)
    up_grad = product(hidden_ref[1], two_ref[...], 0, 0)
    down_grad = product(hidden_ref[2], coming_ref[...], 0, 0)
    if len(grad_refs) == 3:
        for ref, grad in zip(grad_refs, (gate_grad, up_grad, down_grad)):
            ref[...] = grad.reshape(ref.shape)
    else:
        first_held, first_sent, second_held, second_sent = grad_refs
        cut = first_held.shape[1]
        pairs = first_held.shape[0]
        for kind, grad in enumerate((gate_grad, up_grad, down_grad)):
            blocks, rows = (down_blocks, down_rows) if kind == 2 else (gate_blocks, gate_rows)
            grad = grad.reshape(blocks // 2, 2, rows, D)
            kept = jnp.where(core == 0, grad[:, 0], grad[:, 1])
            sent = jnp.where(core == 0, grad[:, 1], grad[:, 0]).astype(jnp.bfloat16)
            start = step * (blocks // 2) + (pairs // 2 if kind == 1 else 0)
            spot = pl.ds(start, blocks // 2)
            if kind == 2:
                second_held[spot, gate_rows - cut :, :] = kept
                second_sent[spot, gate_rows - cut :, :] = sent
            else:
                first_held[spot] = kept[:, :cut]
                first_sent[spot] = sent[:, :cut]
                second_held[spot, : rows - cut, :] = kept[:, cut:]
                second_sent[spot, : rows - cut, :] = sent[:, cut:]

    @pl.when(step == pl.num_programs(0) - 1)
    def _():
        dgain_ref[...] = jnp.zeros_like(dgain_ref)
        for start in range(0, length, size):
            rows = slice(start, start + size)
            residual = res_ref[rows]
            out_ref[:, rows] = (residual + sum_ref[rows]).T.astype(jnp.bfloat16)
            inner = inner_ref[rows]
            inverse = scaled_norm(residual, 1.0)[1]
            scaled = inner * gain_ref[1:2]
            dgain_ref[...] += jnp.sum(inner * residual * inverse, axis=0, keepdims=True)
            back = (
                grad_ref[:, rows].astype(jnp.float32).T * weight
                + inverse * scaled
                - residual
                * (inverse * inverse * inverse)
                * jnp.mean(scaled * residual, axis=-1, keepdims=True)
            )
            back_ref[rows] = back
            coming_ref[rows] = back.astype(jnp.bfloat16)
        do_ref[...] = product(low_ref[...], coming_ref[...], 0, 0)
        att_ref[...] = product(coming_ref[...], o_w, 1, 1).astype(jnp.bfloat16)


def heads_kernel(heads, *refs):
    outs = refs[8:-2]
    for index, head in enumerate(heads):
        head_kernel(head, *refs[:8], *outs[3 * index : 3 * index + 3], *refs[-2:])


def head_kernel(
    head, q_ref, k_ref, v_ref, grad_ref, peak_ref, total_ref, cos_ref, sin_ref,
    dq_ref, dk_ref, dv_ref, key_sum, value_sum,
):
    length = q_ref.shape[0]
    size = min(256, length)
    half_dim = HEAD_DIM // 2
    mask = causal_mask(size)
    group = HEADS // KV_HEADS
    shared = slice(head * HEAD_DIM, (head + 1) * HEAD_DIM)
    key_sum[...] = jnp.zeros_like(key_sum)
    value_sum[...] = jnp.zeros_like(value_sum)

    def turn_back(grad, columns):
        first, second = grad[:half_dim], grad[half_dim:]
        cosine, sine = cos_ref[:, columns], sin_ref[:, columns]
        turned = [first * cosine + second * sine, second * cosine - first * sine]
        return jnp.concatenate(turned, axis=0).T

    for member in range(group):
        row = head * group + member
        place = slice(row * HEAD_DIM, (row + 1) * HEAD_DIM)
        for start in range(0, length, size):
            end = start + size
            queries = q_ref[start:end, place] * jnp.bfloat16(SCORE_SCALE)
            grad = grad_ref[start:end, place]
            keys, values = k_ref[:end, shared], v_ref[:end, shared]
            scores = scores_by_key(keys, queries, mask)
            probs = (
                jnp.exp(scores - peak_ref[row, :, start:end])
                * total_ref[row, :, start:end]
            )
            moved = probs * product(values, grad, 1, 1)
            score_grad = (moved - probs * jnp.sum(moved, axis=0, keepdims=True)).astype(
                jnp.bfloat16
            )
            value_sum[:end] += product(probs.astype(jnp.bfloat16), grad, 1, 0)
            key_sum[:end] += product(score_grad, queries, 1, 0)
            back = turn_back(product(keys, score_grad, 0, 0) * SCORE_SCALE, slice(start, end))
            dq_ref[start:end, member * HEAD_DIM : (member + 1) * HEAD_DIM] = back.astype(
                jnp.bfloat16
            )
    dk_ref[...] = turn_back(key_sum[...].T, slice(0, length)).astype(jnp.bfloat16)
    dv_ref[...] = value_sum[...].astype(jnp.bfloat16)


def qkv_kernel(core_ref, *refs):
    parts, (normed_ref, o_ref, joined_ref), out_refs = refs[:9], refs[9:12], refs[12:]
    start = 0
    for part in parts:
        joined_ref[:, start : start + part.shape[1]] = part[...]
        start += part.shape[1]
    grad = product(joined_ref[...], normed_ref[...], 0, 0)
    if len(out_refs) == 1:
        out_refs[0][:start] = grad
        out_refs[0][start:] = o_ref[...]
        return
    held_ref, sent_ref = out_refs
    rows = held_ref.shape[1]
    spot = 0
    for value in (grad, o_ref[...]):
        value = value.reshape(-1, 2, rows, D)
        end = spot + value.shape[0]
        held_ref[spot:end] = jnp.where(core_ref[0, 0] == 0, value[:, 0], value[:, 1])
        sent = jnp.where(core_ref[0, 0] == 0, value[:, 1], value[:, 0])
        sent_ref[spot:end] = sent.astype(jnp.bfloat16)
        spot = end


def input_kernel(joined_ref, w_ref, x_ref, back_ref, gain_ref, out_ref, dgain_ref):
    length = x_ref.shape[0]
    size = min(256, length)
    count = joined_ref.shape[1]
    weights = w_ref[...].reshape(-1, D)[:count]
    dgain_ref[...] = jnp.zeros_like(dgain_ref)
    for start in range(0, length, size):
        rows = slice(start, start + size)
        inner = product(joined_ref[rows], weights, 1, 0)
        hidden = x_ref[rows]
        inverse = scaled_norm(hidden, 1.0)[1]
        scaled = inner * gain_ref[0:1]
        dgain_ref[...] += jnp.sum(inner * hidden * inverse, axis=0, keepdims=True)
        grad = (
            back_ref[rows]
            + inverse * scaled
            - hidden
            * (inverse * inverse * inverse)
            * jnp.mean(scaled * hidden, axis=-1, keepdims=True)
        )
        out_ref[:, rows] = grad.T.astype(jnp.bfloat16)


def ortho_sweeps(block, held_ref):
    size = min(block.shape)
    left = block.shape[0] < block.shape[1]
    block = block.astype(jnp.float32)
    held_ref[...] = block * (1.0 / (jnp.sqrt(jnp.sum(block * block)) + 1e-07))
    row = lax.broadcasted_iota(jnp.int32, (size, size), 0)
    diagonal = row == lax.broadcasted_iota(jnp.int32, (size, size), 1)

    def sweep(index, carry):
        held = held_ref[...]
        scaled = held.astype(jnp.bfloat16)
        side = 1 if left else 0
        gram = product(scaled, scaled, side, side)
        mean = jnp.sum(jnp.where(diagonal, gram, 0.0)) / size
        rest = jnp.where(diagonal, gram - mean, gram)
        rest_low = rest.astype(jnp.bfloat16)
        poly = (POLY_TWO + 2.0 * POLY_THREE * mean) * rest + POLY_THREE * product(
            rest_low, rest_low, 1, 0
        )
        poly_low = poly.astype(jnp.bfloat16)
        turned = product(poly_low, scaled, 1, 0) if left else product(scaled, poly_low, 1, 0)
        held_ref[...] = (POLY_ONE + POLY_TWO * mean + POLY_THREE * mean * mean) * held + turned
        return carry

    lax.fori_loop(0, ORTHO_STEPS, sweep, 0)
    return held_ref[...].astype(jnp.bfloat16)


def ortho_kernel(block_ref, out_ref, held_ref):
    out_ref[...] = ortho_sweeps(block_ref[...], held_ref)


def clip_factor(sums, limit):
    gains = sums[:2]
    squares = jnp.sum(gains * gains, axis=0, keepdims=True) + sums[2:3]
    norm = jnp.sqrt(jnp.sum(squares, axis=1, keepdims=True))
    return norm, jnp.minimum(1.0, limit / norm)


def solve_kernel(
    spot_ref, sums_ref, own_ref, other_ref, own_momentum, other_momentum,
    out_ref, block_ref, held_ref, *, limit,
):
    kind, place, start, count = [spot_ref[i] for i in range(4)]
    factor = clip_factor(sums_ref[...], limit)[1]
    lead, size = block_ref.shape[:2]
    rows = size // 2
    for index in range(lead):
        grad_ref = other_ref if index % 2 else own_ref
        momentum_ref = other_momentum if index % 2 else own_momentum
        momentum = momentum_ref[index // 2].astype(jnp.float32)
        mixed = MOMENTUM_DECAY * momentum + factor * grad_ref[index // 2].astype(jnp.float32)
        row = ((place & (lead - 1)) ^ index) * rows
        here = (kind < 2) | ((row >= start) & (row < start + count))
        block_ref[index, :rows] = jnp.where(here, mixed[:rows], 0.0).astype(jnp.bfloat16)
        block_ref[index, rows:] = jnp.where(kind < 2, mixed[rows:], 0.0).astype(jnp.bfloat16)
    done = ortho_sweeps(block_ref[...].reshape(lead * size, D), held_ref)
    block_ref[...] = done.reshape(lead, size, D)
    for flip in range(4):
        out_ref[flip] = block_ref[2 * flip]


def solve(spots, sums, grads, momenta, limit):
    half, size = grads[0].shape[:2]
    in_vmem = pl.BlockSpec(memory_space=pltpu.VMEM)
    in_smem = pl.BlockSpec(memory_space=pltpu.SMEM)
    return pl.pallas_call(
        partial(solve_kernel, limit=limit),
        out_shape=shape_of((4, size, D), jnp.bfloat16),
        in_specs=[in_smem] + [in_vmem] * 5,
        out_specs=in_vmem,
        scratch_shapes=[
            pltpu.VMEM((2 * half, size, D), jnp.bfloat16),
            pltpu.VMEM((2 * half * size, D), jnp.float32),
        ],
        compiler_params=pltpu.CompilerParams(vmem_limit_bytes=58 * 2**20),
    )(spots, sums, *grads, *momenta)


def orthogonalize(block):
    rows, columns = block.shape
    small, large = min(block.shape), max(block.shape)
    return call(
        ortho_kernel,
        shape_of(block.shape, jnp.bfloat16),
        (block,),
        2 * ORTHO_STEPS * small * small * (2 * large + small),
        32,
        scratch=(pltpu.VMEM((rows, columns), jnp.float32),),
    )


def block_list():
    q_rows = HEADS * HEAD_DIM
    kv_rows = KV_HEADS * HEAD_DIM
    return (
        (0, 0, q_rows),
        (0, q_rows, kv_rows),
        (0, q_rows + kv_rows, kv_rows),
        (0, q_rows + 2 * kv_rows, q_rows),
        (1, 0, FF),
        (1, FF, FF),
        (2, 0, FF),
    )


def row_scales(array_id):
    pieces = [
        jnp.full((row_count,), 0.2 * math.sqrt(max(row_count, D)), jnp.float32)
        for owner_id, row_start, row_count in block_list()
        if owner_id == array_id
    ]
    return jnp.concatenate(pieces, axis=0)


def split_rows(value):
    high = lax.reduce_precision(value, 8, 7)
    return jnp.concatenate([high.astype(jnp.bfloat16), (value - high).astype(jnp.bfloat16)], axis=0)


def joined_rows(rows):
    half = rows.shape[0] // 2
    return rows[:half].astype(jnp.float32) + rows[half:].astype(jnp.float32)


class Owners:
    def __init__(self, place, devices):
        self.place, self.devices = place, devices
        self.top_bit = devices.bit_length() - 2
        self.core, self.across, self.along = [bit_of(place, bit) for bit in range(3)]
        self.kind = 2 * self.along + self.across
        self.top = bit_of(place, self.top_bit)
        self.own = place & (devices // 2 - 1)

    def attn_span(self, large):
        q_rows, kv_rows = HEADS * HEAD_DIM, KV_HEADS * HEAD_DIM
        large_start = jnp.where(self.top == 0, 0, kv_rows)
        small_start = jnp.where(self.top == 0, q_rows, 0)
        return jnp.where(large, large_start, small_start), jnp.where(large, q_rows, kv_rows)

    def solve(self, sums, limit, grads, momenta, rows):
        lead = self.devices // 2
        start, count = self.attn_span(self.kind == 2)
        if rows % 16 == 0:
            spots = jnp.stack([self.kind, self.place, start, count])
            return solve(spots, sums, grads, momenta, limit)
        factor = clip_factor(sums, limit)[1]
        grads, momenta = [
            jnp.stack(pair, axis=1).reshape((lead,) + pair[0].shape[1:]).astype(jnp.float32)
            for pair in (grads, momenta)
        ]
        row = (jnp.arange(lead) ^ self.own) * rows
        here = ((row >= start) & (row < start + count))[:, None] & (jnp.arange(2 * rows) < rows)
        block = MOMENTUM_DECAY * momenta + factor * grads
        block = jnp.where((self.kind < 2) | here[..., None], block, 0.0).astype(jnp.bfloat16)
        return orthogonalize(block.reshape(-1, D)).reshape(lead, 2 * rows, D)[:8:2]

    def spread(self, result, rows):
        came = [result[0]]
        for flip in (1, 2, 3):
            came.append(exchange(result[flip], flip << 1, self.devices))

        def from_chip(chip, count):
            found = came[0][:count]
            for flip in (1, 2, 3):
                found = jnp.where(self.kind ^ flip == chip, came[flip][:count], found)
            return found

        start, count = self.attn_span(True)
        row = self.own * rows
        large = (row >= start) & (row < start + count)
        attn = jnp.where(large, from_chip(2, rows), from_chip(3, rows))
        return attn, from_chip(0, 2 * rows), from_chip(1, rows)


class Gather:
    def __init__(self, owners, gate_up, down, attn, sums=None):
        self.owners, self.sums = owners, sums
        parts = (gate_up, attn, down)
        self.gate_up, self.attn, self.down = [part.astype(jnp.bfloat16)[None] for part in parts]

    def send(self, parts, flip):
        flat = [part.reshape(-1, D) for part in parts]
        few = [] if self.sums is None else [split_rows(self.sums)]
        other = exchange(jnp.concatenate(flat + few, axis=0), flip, self.owners.devices)
        came, start = [], 0
        for part, rows in zip(parts, flat):
            came.append(other[start : start + rows.shape[0]].reshape(part.shape))
            start += rows.shape[0]
        return came, joined_rows(other[start:]) if few else 0.0

    def add(self, few):
        if self.sums is not None:
            self.sums = sum(few, self.sums)

    def widen(self, group):
        top = 1 << self.owners.top_bit
        gate_up, attn, down, few = [self.gate_up], [self.attn], [self.down], []
        for flip in flips_of(group):
            if flip & top:
                (more,), rest = self.send([self.down], flip)
            else:
                came, rest = self.send([self.gate_up, self.attn, self.down], flip)
                gate_up.append(came[0])
                attn.append(came[1])
                more = came[2]
            down.append(more)
            few.append(rest)
        joined = [jnp.concatenate(blocks, axis=0) for blocks in (gate_up, attn, down)]
        self.gate_up, self.attn, self.down = joined
        self.add(few)

    def route(self):
        kind = self.owners.kind
        gate_up = self.gate_up
        down = self.down.reshape(gate_up.shape)
        attn = jnp.pad(self.attn, ((0, 0), (0, self.attn.shape[1]), (0, 0)))
        wanted = lambda owner: jnp.where(owner == 0, gate_up, jnp.where(owner == 1, down, attn))
        blocks, few = [wanted(kind)], []
        for flip in (1, 2, 3):
            (came,), rest = self.send([wanted(kind ^ flip)], flip << 1)
            blocks.append(came)
            few.append(rest)
        self.add(few)
        self.blocks = jnp.stack(blocks, axis=1)

    def join(self):
        (self.other_blocks,), rest = self.send([self.blocks], 1)
        self.add([rest])

    def pair(self):
        shape = (-1,) + self.blocks.shape[2:]
        return self.blocks.reshape(shape), self.other_blocks.reshape(shape)


def per_device(
    inputs,
    out_grad,
    lang_tags,
    attn_master,
    gate_up_master,
    down_master,
    attn_momentum,
    gate_up_momentum,
    down_momentum,
    norm_gains,
    gain_first,
    gain_second,
):
    devices = lax.axis_size(("dp", "sub"))
    device_place = lax.axis_index(("dp", "sub"))
    q_rows = HEADS * HEAD_DIM
    kv_rows = KV_HEADS * HEAD_DIM
    qkv_rows = q_rows + 2 * kv_rows
    tag_hot = (lang_tags[:, None] == jnp.arange(NUM_TAGS, dtype=jnp.int32)[None, :]).astype(
        jnp.float32
    )
    masters = (attn_master, gate_up_master, down_master)
    attn_low = attn_master.astype(jnp.bfloat16)
    gate_up_low = gate_up_master.astype(jnp.bfloat16)
    down_low = down_master.astype(jnp.bfloat16)
    tag_row = jnp.pad(tag_hot[:1], ((0, 0), (0, D - NUM_TAGS)))
    ffn_low = jnp.concatenate([gate_up_low, down_low], axis=0)
    place = device_place
    groups = bit_groups(devices)
    ffn_blocks = lax.all_gather(ffn_low, AXES)
    owners = Owners(place, devices)
    momenta = Gather(owners, gate_up_momentum, down_momentum, attn_momentum, tag_row)
    early = (inputs.astype(jnp.float32), momenta.gate_up, momenta.attn, momenta.down)
    attn_blocks = gather_hop(attn_low[None], groups[-1], devices)
    attn_blocks, early = lax.optimization_barrier((attn_blocks, early))
    hidden_in, momenta.gate_up, momenta.attn, momenta.down = early
    for group in groups[-2:0:-1]:
        attn_blocks = gather_hop(attn_blocks, group, devices)
    for group in groups[2:]:
        momenta.widen(group)
    other_blocks = exchange(attn_blocks, 1, devices)
    momenta.route()
    attn_blocks, other_blocks, momenta.blocks, momenta.sums = lax.optimization_barrier(
        (attn_blocks, other_blocks, momenta.blocks, momenta.sums)
    )
    momenta.join()
    length = inputs.shape[0]
    wide_cos, wide_sin, tall_cos, tall_sin = [jnp.asarray(t) for t in rotary_rows(length)]
    low, single = jnp.bfloat16, jnp.float32
    spot = place[None, None]
    core = bit_of(place, 0)[None, None]
    in_smem = pl.BlockSpec(memory_space=pltpu.SMEM)
    in_vmem = pl.BlockSpec(memory_space=pltpu.VMEM)
    even = down_low.shape[0] % 16 == 0
    attn_outs = (
        shape_of((length, q_rows), low),
        shape_of((length, kv_rows), low),
        shape_of((length, kv_rows), low),
        shape_of((length, D), low),
        shape_of((length, q_rows), low),
        shape_of((HEADS, 1, length), single),
        shape_of((HEADS, 1, length), single),
        shape_of((length, D), single),
        shape_of((length, D), low),
    )
    if even:
        pieces = (attn_blocks, other_blocks)
        attn_outs += (shape_of((devices // 2, 2) + attn_low.shape, low),)
    else:
        whole_weights = in_order(jnp.stack([attn_blocks, other_blocks], 1).reshape(devices, -1), place)
        pieces = (whole_weights.reshape(16, 2, -1, D),)
    queries, keys, values, normed_one, attended_low, peaks, totals, residual, normed_two, *attn_w = call(
        attention_kernel if even else whole_attention_kernel,
        attn_outs,
        (spot, hidden_in, *pieces, norm_gains, wide_cos, wide_sin),
        2 * length * D * 3 * (qkv_rows + q_rows),
        58,
        in_specs=[in_smem] + [in_vmem] * (4 + len(pieces)),
        out_specs=(in_vmem,) * len(attn_outs),
        scratch=(pltpu.VMEM((HEADS + 2 * KV_HEADS, length, HEAD_DIM), low),),
    )
    attn_weights = attn_w[0] if even else pieces[0]
    normed_two, momenta.other_blocks, momenta.sums = lax.optimization_barrier(
        (normed_two, momenta.other_blocks, momenta.sums)
    )
    tags = jnp.concatenate([tag_row, momenta.sums], axis=0)
    gate_up_rows, down_rows = gate_up_low.shape[0], down_low.shape[0]
    if even:
        weights = (ffn_blocks,)
        weight_specs = [pl.BlockSpec(ffn_blocks.shape, lambda c: (0, 0, 0), pipeline_mode=pl.Buffered(1))]
    else:
        ffn_weights = ffn_blocks
        ffn_rows = gate_up_rows + down_rows
        gate_up_weights = ffn_weights[:, :gate_up_rows].reshape(32, -1, D)
        down_weights = ffn_weights[:, gate_up_rows:ffn_rows].reshape(32, -1, D)
        gate_up_rows, down_rows = gate_up_weights.shape[1], down_weights.shape[1]
        weights = (gate_up_weights, down_weights)
        weight_specs = [in_vmem] * 2
    chunk = 768 if even else 384
    steps = FF // chunk
    held_once = dict(pipeline_mode=pl.Buffered(1))
    whole = lambda *shape: pl.BlockSpec(shape, lambda c: (0,) * len(shape), **held_once)
    part = lambda rows: pl.BlockSpec((chunk // rows, rows, D), lambda c: (c, 0, 0))
    if even:
        cut = (gate_up_rows + down_rows) * 9 // 16 // 16 * 16
        other_cut = gate_up_rows + down_rows - cut
        pairs = devices // 2
        grad_outs = tuple(
            shape_of((pairs, size, D), kind) for size in (cut, other_cut) for kind in (single, low)
        )
        grad_specs = tuple(whole(*out.shape) for out in grad_outs)
    else:
        grad_outs = (
            shape_of((16, gate_up_rows, D), single),
            shape_of((16, gate_up_rows, D), single),
            shape_of((32, down_rows, D), single),
        )
        grad_specs = (part(gate_up_rows), part(gate_up_rows), part(down_rows))
    outputs, residual_grad, attended_grad, o_part, gain_two, *ffn_grads = call(
        partial(
            feed_kernel,
            devices=devices,
            gathered=even,
            gate_rows=gate_up_rows,
            down_rows=down_rows,
        ),
        (
            shape_of((D, length), low),
            shape_of((length, D), single),
            shape_of((length, q_rows), low),
            shape_of((q_rows, D), single),
            shape_of((1, D), single),
            *grad_outs,
        ),
        (
            spot,
            tags,
            normed_two,
            residual,
            out_grad.T,
            attended_low,
            *weights,
            attn_weights,
            norm_gains,
        ),
        2 * 3 * length * D * (3 * FF + q_rows),
        58,
        grid=(steps,),
        in_specs=[
            in_smem,
            whole(2, D),
            whole(length, D),
            whole(length, D),
            whole(D, length),
            whole(length, q_rows),
            *weight_specs,
            whole(*attn_weights.shape),
            whole(2, D),
        ],
        out_specs=(
            whole(D, length),
            whole(length, D),
            whole(length, q_rows),
            whole(q_rows, D),
            whole(1, D),
            *grad_specs,
        ),
        scratch=(
            pltpu.VMEM((length, D), single),
            pltpu.VMEM((length, D), single),
            pltpu.VMEM((length, D), low),
            pltpu.VMEM((3, length, chunk), low),
        ),
    )
    bits = range(devices.bit_length() - 1)
    if even:
        first_held, first_sent, second_held, second_sent = ffn_grads
        sums = [
            Sums(first_held, place, devices, bits[1:], [exchange(first_sent, 1, devices)]),
            Sums(second_held, place, devices, bits[1:], [exchange(second_sent, 1, devices)]),
        ]
    else:
        gate_up_part = jnp.concatenate([g.reshape(-1, D) for g in ffn_grads[:2]], axis=0)
        sums = [
            Sums(gate_up_part.reshape(devices, -1, D), place, devices, bits),
            Sums(ffn_grads[2].reshape(devices, -1, D), place, devices, bits),
        ]
        for s in sums:
            s.hop(0)
    head_outs = (
        shape_of((length, q_rows // KV_HEADS), low),
        shape_of((length, HEAD_DIM), low),
        shape_of((length, HEAD_DIM), low),
    )
    head_grads = []
    for heads in ((0,), (1, 2)):
        head_grads += call(
            partial(heads_kernel, heads),
            head_outs * len(heads),
            (queries, keys, values, attended_grad, peaks, totals, tall_cos, tall_sin),
            2 * 2 * length * length * q_rows * len(heads),
            58,
            scratch=(
                pltpu.VMEM((length, HEAD_DIM), single),
                pltpu.VMEM((length, HEAD_DIM), single),
            ),
        )
        if heads == (0,):
            attended_grad, head_grads = after((attended_grad, head_grads), sums)
            sums[0].hop(1)
            sums[1].hop(2)
    normed_one, head_grads = after((normed_one, head_grads), sums)
    proj_parts = [head_grads[3 * head + kind] for kind in range(3) for head in range(KV_HEADS)]
    sums[0].hop(2)
    sums[1].hop(1)
    if even:
        grad_outs = (
            shape_of((pairs, attn_low.shape[0], D), single),
            shape_of((pairs, attn_low.shape[0], D), low),
        )
    else:
        grad_outs = (shape_of((qkv_rows + q_rows, D), single),)
    joined, *attn_grads = call(
        qkv_kernel,
        (shape_of((length, qkv_rows), low), *grad_outs),
        (core, *proj_parts, normed_one, o_part),
        2 * length * D * qkv_rows,
        58,
        in_specs=[in_smem] + [in_vmem] * 11,
        out_specs=(in_vmem,) * (1 + len(grad_outs)),
    )
    if even:
        held, sent = attn_grads
        sent = after(sent, sums)
        late = Sums(held, place, devices, bits[1:], [exchange(sent, 1, devices)])
    else:
        late = Sums(attn_grads[0].reshape(devices, -1, D), place, devices, bits)
        late.hop(0)
    feed_rows = [s.shape[0] for s in sums]
    feed_sums = Sums(
        jnp.concatenate([s.total() for s in sums], axis=1), place, devices, bits[3:]
    )
    feed_sums.hop(*groups[2])
    residual_grad = after(residual_grad, [late])
    late.hop(*groups[1])
    input_grad, gain_one = call(
        input_kernel,
        (shape_of((D, length), low), shape_of((1, D), single)),
        (joined, attn_weights, hidden_in, residual_grad, norm_gains),
        2 * length * D * qkv_rows,
        58,
    )
    input_grad = after(input_grad, [late, feed_sums])
    for group in groups[3:]:
        feed_sums.hop(*group)
    feed_total = feed_sums.total()[0]
    if even:
        gate_up_sum = feed_total[:gate_up_rows]
        down_sum = feed_total[gate_up_rows:]
    else:
        gate_up_sum, down_sum = feed_total[: feed_rows[0]], feed_total[feed_rows[0] :]
    for group in groups[2:]:
        late.hop(*group)
    attn_sum = late.total()[0]
    squares = sum(
        jnp.sum(part * part, axis=0, keepdims=True) for part in (attn_sum, gate_up_sum, down_sum)
    )
    small_sums = jnp.concatenate([gain_one, gain_two, squares], axis=0)
    gather = Gather(owners, gate_up_sum, down_sum, attn_sum, small_sums)
    for group in groups[2:]:
        gather.widen(group)
    gather.route()
    gather.join()
    param_count = (qkv_rows + q_rows + 3 * FF) * D + 2 * D
    limit = CLIP_SCALE * math.sqrt(devices * length * param_count)
    down_count = down_low.shape[0]
    solved = owners.solve(gather.sums, limit, gather.pair(), momenta.pair(), down_count)
    small_sums, solved = lax.optimization_barrier((gather.sums, solved))
    gain_total = small_sums[:2]
    grad_norm, factor = [value[0, 0] for value in clip_factor(small_sums, limit)]
    attn_grad = attn_sum * factor
    gate_up_grad = gate_up_sum * factor
    down_grad = down_sum * factor
    gain_grad = gain_total * factor
    attn_moment = MOMENTUM_DECAY * attn_momentum + attn_grad
    gate_up_moment = MOMENTUM_DECAY * gate_up_momentum + gate_up_grad
    down_moment = MOMENTUM_DECAY * down_momentum + down_grad
    ortho_shards = owners.spread(solved, down_count)
    new_masters = []
    for array_id in range(3):
        shard_rows = masters[array_id].shape[0]
        scale_rows = lax.dynamic_slice_in_dim(
            row_scales(array_id), device_place * shard_rows, shard_rows, 0
        )
        new_masters.append(
            masters[array_id]
            - MATRIX_RATE
            * (scale_rows[:, None] * ortho_shards[array_id] + MATRIX_DECAY * masters[array_id])
        )
    first_new = BETA_FIRST * gain_first + (1.0 - BETA_FIRST) * gain_grad
    second_new = BETA_SECOND * gain_second + (1.0 - BETA_SECOND) * gain_grad * gain_grad
    gains_new = norm_gains - GAIN_RATE * (first_new / (1.0 - BETA_FIRST**STEP_NUMBER)) / (
        jnp.sqrt(second_new / (1.0 - BETA_SECOND**STEP_NUMBER)) + ADAM_EPS
    )
    return (
        outputs.T,
        input_grad.T,
        attn_grad,
        gate_up_grad,
        down_grad,
        grad_norm,
        attn_moment,
        gate_up_moment,
        down_moment,
        new_masters[0],
        new_masters[1],
        new_masters[2],
        gain_grad,
        first_new,
        second_new,
        gains_new,
    )


def solution(mesh):
    placed = (
        P(("dp", "sub"), None),
        P(("dp", "sub"), None),
        P(("dp", "sub")),
        P(("dp", "sub"), None),
        P(("dp", "sub"), None),
        P(("dp", "sub"), None),
        P(("dp", "sub"), None),
        P(("dp", "sub"), None),
        P(("dp", "sub"), None),
        P(),
        P(),
        P(),
    )
    return jax.shard_map(
        per_device,
        mesh=mesh,
        in_specs=placed,
        out_specs=(
            P(("dp", "sub"), None),
            P(("dp", "sub"), None),
            P(("dp", "sub"), None),
            P(("dp", "sub"), None),
            P(("dp", "sub"), None),
            P(),
            P(("dp", "sub"), None),
            P(("dp", "sub"), None),
            P(("dp", "sub"), None),
            P(("dp", "sub"), None),
            P(("dp", "sub"), None),
            P(("dp", "sub"), None),
            P(),
            P(),
            P(),
            P(),
        ),
        check_vma=False,
    )
```

```python
from functools import partial
import math

import jax
import jax.numpy as jnp
import numpy as np
from jax import lax
from jax.experimental import pallas as pl
from jax.experimental.pallas import tpu as pltpu
from jax.sharding import PartitionSpec as P

D = 576
HEADS = 9
KV_HEADS = 3
HEAD_DIM = 64
FF = 1536
NUM_TAGS = 8
ORTHO_STEPS = 5
STEP_NUMBER = 10


NORM_EPS = 1e-05
ROPE_BASE = 100000.0
POLY_ONE = 3.4445
POLY_TWO = -4.775
POLY_THREE = 2.0315
MOMENTUM_DECAY = 0.95
MATRIX_RATE = 0.2
MATRIX_DECAY = 0.1
GAIN_RATE = 1.0
BETA_FIRST = 0.9
BETA_SECOND = 0.95
ADAM_EPS = 1e-08
CLIP_SCALE = 0.002


AXES = ("dp", "sub")


def bit_of(place, bit):
    return (place >> bit) & 1


def exchange(array, flip, devices, source=None):
    pairs = [(i, i ^ flip) for i in range(devices) if source is None or source(i)]
    return lax.ppermute(array, AXES, pairs)


def bit_groups(devices):
    bits = devices.bit_length() - 1
    return [(0,)] + [tuple(range(bit, min(bit + 2, bits))) for bit in range(1, bits, 2)]


def flips_of(group):
    return [part << group[0] for part in range(1, 1 << len(group))]


def pick(array, axis, index):
    return lax.dynamic_index_in_dim(array, index, axis, keepdims=False)


def gather_hop(blocks, group, devices, front=False, source=None):
    came = [exchange(blocks, flip, devices, source) for flip in flips_of(group)]
    stacked = jnp.stack([blocks] + came, axis=0 if front else 1)
    return stacked.reshape((-1,) + blocks.shape[1:])


def in_order(blocks, place):
    return jnp.take(blocks, jnp.arange(blocks.shape[0]) ^ place, axis=0)


class Sums:
    def __init__(self, held, place, devices, bits, came=()):
        self.place, self.devices, self.bits = place, devices, list(bits)
        self.shape = held.shape[-2:]
        self.held, self.came = held, list(came)

    def hop(self, *group):
        low, width = self.bits.index(group[0]), len(group)
        high = len(self.bits) - low - width
        terms = [
            term.reshape((1 << high, 1 << width, 1 << low) + self.shape)
            for term in [self.held] + self.came
        ]
        mine = (self.place >> group[0]) & ((1 << width) - 1)

        def part(index):
            chosen = [pick(term, 1, index).astype(jnp.float32) for term in terms]
            return sum(chosen[1:], chosen[0]).reshape((-1,) + self.shape)

        sent = [part(mine ^ flip).astype(jnp.bfloat16) for flip in range(1, 1 << width)]
        self.held = part(mine)
        self.came = [exchange(s, f, self.devices) for s, f in zip(sent, flips_of(group))]
        for bit in group:
            self.bits.remove(bit)

    def total(self):
        return sum([term.astype(jnp.float32) for term in [self.held] + self.came])


def after(value, sums):
    value, came = lax.optimization_barrier((value, [s.came for s in sums]))
    for s, c in zip(sums, came):
        s.came = c
    return value


SCORE_SCALE = HEAD_DIM ** (-0.5)
MASKED = -1e30


def product(left, right, left_dim, right_dim):
    return lax.dot_general(
        left, right, (((left_dim,), (right_dim,)), ((), ())), preferred_element_type=jnp.float32
    )


def call(kernel, outs, args, flops, mib, grid=(), in_specs=None, out_specs=None, scratch=()):
    specs = {} if in_specs is None else dict(in_specs=in_specs, out_specs=out_specs)
    listed = tuple(outs) if isinstance(outs, (tuple, list)) else (outs,)
    moved = sum(math.prod(a.shape) * a.dtype.itemsize for a in tuple(args) + listed)
    return pl.pallas_call(
        kernel,
        out_shape=outs,
        grid=grid,
        scratch_shapes=scratch,
        compiler_params=pltpu.CompilerParams(vmem_limit_bytes=mib * 2**20),
        cost_estimate=pl.CostEstimate(flops=int(flops), bytes_accessed=moved, transcendentals=0),
        **specs,
    )(*args)


def shape_of(shape, dtype):
    return jax.ShapeDtypeStruct(shape, dtype)


def rotary_rows(length):
    half_dim = HEAD_DIM // 2
    frequency = np.float32(ROPE_BASE) ** (
        -(np.arange(half_dim, dtype=np.float32) * np.float32(2.0 / HEAD_DIM))
    )
    angles = np.arange(length, dtype=np.float32)[:, None] * frequency[None, :].astype(np.float32)
    cosine, sine = np.cos(angles), np.sin(angles)
    wide_cosine = np.concatenate([cosine] * 4, axis=1)
    wide_sine = np.concatenate([-sine, sine, -sine, sine], axis=1)
    return wide_cosine, wide_sine, cosine.T.copy(), sine.T.copy()


def causal_mask(size):
    key_pos = lax.broadcasted_iota(jnp.int32, (size, size), 0)
    query_pos = lax.broadcasted_iota(jnp.int32, (size, size), 1)
    return key_pos <= query_pos


def scores_by_key(keys, queries, mask):
    size = queries.shape[0]
    before = keys.shape[0] - size
    raw = product(keys, queries, 1, 1)
    last = jnp.where(mask, raw[before:], MASKED)
    return last if before == 0 else jnp.concatenate([raw[:before], last], axis=0)


def scaled_norm(values, gain):
    inverse = lax.rsqrt(jnp.mean(values * values, axis=-1, keepdims=True) + NORM_EPS)
    return values * inverse * gain, inverse


def attention_kernel(
    place_ref, x_ref, own_ref, other_ref, gain_ref, cos_ref, sin_ref,
    q_ref, k_ref, v_ref, normed_ref, low_ref, peak_ref, total_ref, res_ref, two_ref, joined_ref,
    heads_ref,
):
    length = x_ref.shape[0]
    q_rows = HEADS * HEAD_DIM
    kv_rows = KV_HEADS * HEAD_DIM
    turned = q_rows + kv_rows
    if other_ref is None:
        w_ref = own_ref
    else:
        core, pair = place_ref[0, 0] & 1, place_ref[0, 0] >> 1
        for index in range(own_ref.shape[0]):
            joined_ref[index ^ pair, core] = own_ref[index]
            joined_ref[index ^ pair, 1 - core] = other_ref[index]
        w_ref = joined_ref
    weights = w_ref[...].reshape(-1, D)
    size = min(256, length)
    lane = lax.broadcasted_iota(jnp.int32, (size, turned), 1)
    first = lane % HEAD_DIM < HEAD_DIM // 2
    for start in range(0, length, size):
        rows = slice(start, start + size)
        normed = scaled_norm(x_ref[rows], gain_ref[0:1])[0].astype(jnp.bfloat16)
        normed_ref[rows] = normed
        raw = product(normed, weights[: turned + kv_rows], 1, 1)
        both = raw[:, :turned]
        swapped = jnp.where(
            first,
            pltpu.roll(both, turned - HEAD_DIM // 2, 1),
            pltpu.roll(both, HEAD_DIM // 2, 1),
        )
        cosine = jnp.concatenate([cos_ref[rows]] * (turned // 128), axis=1)
        sine = jnp.concatenate([sin_ref[rows]] * (turned // 128), axis=1)
        both = both * cosine + swapped * sine
        q_ref[rows] = both[:, :q_rows].astype(jnp.bfloat16)
        k_ref[rows] = both[:, q_rows:].astype(jnp.bfloat16)
        v_ref[rows] = raw[:, turned:].astype(jnp.bfloat16)
    size = min(512, length)
    mask = causal_mask(size)
    group = HEADS // KV_HEADS
    span = lambda head: slice(head * HEAD_DIM, (head + 1) * HEAD_DIM)
    for head in range(HEADS):
        heads_ref[head] = q_ref[:, span(head)] * jnp.bfloat16(SCORE_SCALE)
    for head in range(KV_HEADS):
        heads_ref[HEADS + head] = k_ref[:, span(head)]
        heads_ref[HEADS + KV_HEADS + head] = v_ref[:, span(head)]

    def attend(head, carry):
        keys_at = HEADS + head // group
        for start in range(0, length, size):
            end = start + size
            queries = heads_ref[head, start:end]
            scores = scores_by_key(heads_ref[keys_at, :end], queries, mask)
            peak = jnp.max(scores, axis=0, keepdims=True)
            shifted = jnp.exp(scores - peak)
            inverse = 1.0 / jnp.sum(shifted, axis=0, keepdims=True)
            prob_low = (shifted * inverse).astype(jnp.bfloat16)
            out = product(heads_ref[keys_at + KV_HEADS, :end], prob_low, 0, 0)
            heads_ref[head, start:end] = out.T.astype(jnp.bfloat16)
            peak_ref[head, :, start:end] = peak
            total_ref[head, :, start:end] = inverse
        return carry

    lax.fori_loop(0, HEADS, attend, 0)
    low_ref[...] = jnp.concatenate([heads_ref[head] for head in range(HEADS)], axis=1)
    size = min(256, length)
    for start in range(0, length, size):
        rows = slice(start, start + size)
        residual = x_ref[rows] + product(low_ref[rows], weights[turned + kv_rows :], 1, 0)
        res_ref[rows] = residual
        two_ref[rows] = scaled_norm(residual, gain_ref[1:2])[0].astype(jnp.bfloat16)


def whole_attention_kernel(place_ref, x_ref, own_ref, *refs):
    attention_kernel(place_ref, x_ref, own_ref, None, *refs[:-1], None, refs[-1])


def feed_kernel(
    place_ref, tags_ref, two_ref, res_ref, grad_ref, low_ref, *refs,
    devices, gathered, gate_rows, down_rows,
):
    cut = 1 if gathered else 2
    weight_refs, refs = refs[:cut], refs[cut:]
    attn_ref, gain_ref, out_ref, back_ref, att_ref, do_ref, dgain_ref, *refs = refs
    if gathered:
        *refs, sems = refs
        refs, held_refs, grad_refs = refs[:-8], refs[-8:-4], refs[-4:]
        *grad_outs, sum_ref, inner_ref, coming_ref, hidden_ref = refs
    else:
        *grad_refs, sum_ref, inner_ref, coming_ref, hidden_ref = refs
    step = pl.program_id(0)
    length = two_ref.shape[0]
    size = min(256, length)
    core = place_ref[0, 0] & 1
    chunk = hidden_ref.shape[2]
    gate_blocks, down_blocks = chunk // gate_rows, chunk // down_rows
    count = jnp.sum(tags_ref[0:1] * tags_ref[1:2], axis=1, keepdims=True)
    weight = devices / (NUM_TAGS * count)
    if gathered:
        weights_ref, res_held, low_held, attn_held = held_refs
        later = [
            pltpu.make_async_copy(source, target, sems.at[at])
            for at, (source, target) in enumerate(
                ((res_ref, res_held), (low_ref, low_held), (attn_ref, attn_held))
            )
        ]
        leaving = [
            pltpu.make_async_copy(source, target, sems.at[3 + at])
            for at, (source, target) in enumerate(zip(grad_refs, grad_outs))
        ]

        def weight_copies(part):
            gates = pl.ds(part * gate_blocks, gate_blocks)
            ups = pl.ds(FF // gate_rows + part * gate_blocks, gate_blocks)
            downs = pl.ds(part * down_blocks, down_blocks)
            upper, lower = pl.ds(0, gate_rows), pl.ds(gate_rows, down_rows)
            return [
                pltpu.make_async_copy(
                    weight_refs[0].at[spot, rows],
                    weights_ref.at[spot, rows],
                    sems.at[7 + 3 * part + at],
                )
                for at, (spot, rows) in enumerate(((gates, upper), (ups, upper), (downs, lower)))
            ]

        @pl.when(step == 0)
        def _():
            for part in range(FF // chunk):
                for copy in weight_copies(part):
                    copy.start()
            for copy in later:
                copy.start()

        res_ref, low_ref, attn_ref = res_held, low_held, attn_held
        gate_ref, down_ref, first_row = weights_ref, weights_ref, gate_rows
    else:
        (gate_ref, down_ref), first_row = weight_refs, 0
    @pl.when(step == 0)
    def _():
        for start in range(0, length, size):
            rows = slice(start, start + size)
            grad = grad_ref[:, rows].astype(jnp.float32).T
            coming_ref[rows] = (grad * weight).astype(jnp.bfloat16)
        sum_ref[...] = jnp.zeros_like(sum_ref)
        inner_ref[...] = jnp.zeros_like(inner_ref)

    if gathered:
        for part in range(FF // chunk):

            @pl.when(step == part)
            def _(part=part):
                for copy in weight_copies(part):
                    copy.wait()

    gate_spots = pl.ds(step * gate_blocks, gate_blocks)
    up_spots = pl.ds(FF // gate_rows + step * gate_blocks, gate_blocks)
    gate_w = gate_ref[gate_spots, :gate_rows].reshape(-1, D)
    up_w = gate_ref[up_spots, :gate_rows].reshape(-1, D)
    down_spots = pl.ds(step * down_blocks, down_blocks)
    down_w = down_ref[down_spots, first_row : first_row + down_rows].reshape(-1, D)

    for start in range(0, length, 2 * size):
        rows = slice(start, min(start + 2 * size, length))
        two = two_ref[rows]
        gate = product(two, gate_w, 1, 1)
        up = product(two, up_w, 1, 1)
        sigmoid = 0.5 * jnp.tanh(0.5 * gate) + 0.5
        silu = gate * sigmoid
        activation = (silu * up).astype(jnp.bfloat16)
        act_grad = product(coming_ref[rows], down_w, 1, 1)
        gate_low = act_grad * up * (sigmoid * (1.0 + gate * (1.0 - sigmoid)))
        gate_low = gate_low.astype(jnp.bfloat16)
        up_low = (act_grad * silu).astype(jnp.bfloat16)
        sum_ref[rows] += product(activation, down_w, 1, 0)
        inner_ref[rows] += product(gate_low, gate_w, 1, 0) + product(up_low, up_w, 1, 0)
        for kind, value in enumerate((gate_low, up_low, activation)):
            hidden_ref[kind, rows] = value
    gate_grad = product(hidden_ref[0], two_ref[...], 0, 0)
    up_grad = product(hidden_ref[1], two_ref[...], 0, 0)
    down_grad = product(hidden_ref[2], coming_ref[...], 0, 0)
    if len(grad_refs) == 3:
        for ref, grad in zip(grad_refs, (gate_grad, up_grad, down_grad)):
            ref[...] = grad.reshape(ref.shape)
    else:
        first_held, first_sent, second_held, second_sent = grad_refs
        cut = first_held.shape[1]
        pairs = first_held.shape[0]
        for kind, grad in enumerate((gate_grad, up_grad, down_grad)):
            blocks, rows = (down_blocks, down_rows) if kind == 2 else (gate_blocks, gate_rows)
            grad = grad.reshape(blocks // 2, 2, rows, D)
            kept = jnp.where(core == 0, grad[:, 0], grad[:, 1]).astype(jnp.bfloat16)
            sent = jnp.where(core == 0, grad[:, 1], grad[:, 0]).astype(jnp.bfloat16)
            start = step * (blocks // 2) + (pairs // 2 if kind == 1 else 0)
            spot = pl.ds(start, blocks // 2)
            if kind == 2:
                second_held[spot, gate_rows - cut :, :] = kept
                second_sent[spot, gate_rows - cut :, :] = sent
            else:
                first_held[spot] = kept[:, :cut]
                first_sent[spot] = sent[:, :cut]
                second_held[spot, : rows - cut, :] = kept[:, cut:]
                second_sent[spot, : rows - cut, :] = sent[:, cut:]

    @pl.when(step == pl.num_programs(0) - 1)
    def _():
        if gathered:
            for copy in leaving:
                copy.start()
            for copy in later:
                copy.wait()
        o_w = attn_ref[-(attn_ref.shape[0] * HEADS // (2 * (HEADS + KV_HEADS))) :].reshape(-1, D)
        dgain_ref[...] = jnp.zeros_like(dgain_ref)
        for start in range(0, length, size):
            rows = slice(start, start + size)
            residual = res_ref[rows]
            out_ref[:, rows] = (residual + sum_ref[rows]).T.astype(jnp.bfloat16)
            inner = inner_ref[rows]
            inverse = scaled_norm(residual, 1.0)[1]
            scaled = inner * gain_ref[1:2]
            dgain_ref[...] += jnp.sum(inner * residual * inverse, axis=0, keepdims=True)
            back = (
                grad_ref[:, rows].astype(jnp.float32).T * weight
                + inverse * scaled
                - residual
                * (inverse * inverse * inverse)
                * jnp.mean(scaled * residual, axis=-1, keepdims=True)
            )
            back_ref[rows] = back
            coming_ref[rows] = back.astype(jnp.bfloat16)
        do_ref[...] = product(low_ref[...], coming_ref[...], 0, 0)
        att_ref[...] = product(coming_ref[...], o_w, 1, 1).astype(jnp.bfloat16)
        if gathered:
            for copy in leaving:
                copy.wait()


def heads_kernel(heads, *refs):
    outs = refs[8:-2]
    for index, head in enumerate(heads):
        head_kernel(head, *refs[:8], *outs[3 * index : 3 * index + 3], *refs[-2:])


def head_kernel(
    head, q_ref, k_ref, v_ref, grad_ref, peak_ref, total_ref, cos_ref, sin_ref,
    dq_ref, dk_ref, dv_ref, key_sum, value_sum,
):
    length = q_ref.shape[0]
    size = min(256, length)
    half_dim = HEAD_DIM // 2
    mask = causal_mask(size)
    group = HEADS // KV_HEADS
    shared = slice(head * HEAD_DIM, (head + 1) * HEAD_DIM)
    key_sum[...] = jnp.zeros_like(key_sum)
    value_sum[...] = jnp.zeros_like(value_sum)

    def turn_back(grad, columns):
        first, second = grad[:half_dim], grad[half_dim:]
        cosine, sine = cos_ref[:, columns], sin_ref[:, columns]
        turned = [first * cosine + second * sine, second * cosine - first * sine]
        return jnp.concatenate(turned, axis=0).T

    for member in range(group):
        row = head * group + member
        place = slice(row * HEAD_DIM, (row + 1) * HEAD_DIM)
        for start in range(0, length, size):
            end = start + size
            queries = q_ref[start:end, place] * jnp.bfloat16(SCORE_SCALE)
            grad = grad_ref[start:end, place]
            keys, values = k_ref[:end, shared], v_ref[:end, shared]
            scores = scores_by_key(keys, queries, mask)
            probs = (
                jnp.exp(scores - peak_ref[row, :, start:end])
                * total_ref[row, :, start:end]
            )
            moved = probs * product(values, grad, 1, 1)
            score_grad = (moved - probs * jnp.sum(moved, axis=0, keepdims=True)).astype(
                jnp.bfloat16
            )
            value_sum[:end] += product(probs.astype(jnp.bfloat16), grad, 1, 0)
            key_sum[:end] += product(score_grad, queries, 1, 0)
            back = turn_back(product(keys, score_grad, 0, 0) * SCORE_SCALE, slice(start, end))
            dq_ref[start:end, member * HEAD_DIM : (member + 1) * HEAD_DIM] = back.astype(
                jnp.bfloat16
            )
    dk_ref[...] = turn_back(key_sum[...].T, slice(0, length)).astype(jnp.bfloat16)
    dv_ref[...] = value_sum[...].astype(jnp.bfloat16)


def qkv_kernel(core_ref, *refs):
    parts, (normed_ref, o_ref, joined_ref), out_refs = refs[:9], refs[9:12], refs[12:]
    start = 0
    for part in parts:
        joined_ref[:, start : start + part.shape[1]] = part[...]
        start += part.shape[1]
    grad = product(joined_ref[...], normed_ref[...], 0, 0)
    if len(out_refs) == 1:
        out_refs[0][:start] = grad
        out_refs[0][start:] = o_ref[...]
        return
    held_ref, sent_ref = out_refs
    rows = held_ref.shape[1]
    spot = 0
    for value in (grad, o_ref[...]):
        value = value.reshape(-1, 2, rows, D)
        end = spot + value.shape[0]
        held = jnp.where(core_ref[0, 0] == 0, value[:, 0], value[:, 1])
        held_ref[spot:end] = held.astype(jnp.bfloat16)
        sent = jnp.where(core_ref[0, 0] == 0, value[:, 1], value[:, 0])
        sent_ref[spot:end] = sent.astype(jnp.bfloat16)
        spot = end


def input_kernel(joined_ref, w_ref, x_ref, back_ref, gain_ref, out_ref, dgain_ref):
    length = x_ref.shape[0]
    size = min(256, length)
    count = joined_ref.shape[1]
    weights = w_ref[...].reshape(-1, D)[:count]
    dgain_ref[...] = jnp.zeros_like(dgain_ref)
    for start in range(0, length, size):
        rows = slice(start, start + size)
        inner = product(joined_ref[rows], weights, 1, 0)
        hidden = x_ref[rows]
        inverse = scaled_norm(hidden, 1.0)[1]
        scaled = inner * gain_ref[0:1]
        dgain_ref[...] += jnp.sum(inner * hidden * inverse, axis=0, keepdims=True)
        grad = (
            back_ref[rows]
            + inverse * scaled
            - hidden
            * (inverse * inverse * inverse)
            * jnp.mean(scaled * hidden, axis=-1, keepdims=True)
        )
        out_ref[:, rows] = grad.T.astype(jnp.bfloat16)


def ortho_sweeps(block, held_ref):
    size = min(block.shape)
    left = block.shape[0] < block.shape[1]
    block = block.astype(jnp.float32)
    held_ref[...] = block * (1.0 / (jnp.sqrt(jnp.sum(block * block)) + 1e-07))
    row = lax.broadcasted_iota(jnp.int32, (size, size), 0)
    diagonal = row == lax.broadcasted_iota(jnp.int32, (size, size), 1)

    def sweep(index, carry):
        held = held_ref[...]
        scaled = held.astype(jnp.bfloat16)
        side = 1 if left else 0
        gram = product(scaled, scaled, side, side)
        mean = jnp.sum(jnp.where(diagonal, gram, 0.0)) / size
        rest = jnp.where(diagonal, gram - mean, gram)
        rest_low = rest.astype(jnp.bfloat16)
        poly = (POLY_TWO + 2.0 * POLY_THREE * mean) * rest + POLY_THREE * product(
            rest_low, rest_low, 1, 0
        )
        poly_low = poly.astype(jnp.bfloat16)
        turned = product(poly_low, scaled, 1, 0) if left else product(scaled, poly_low, 1, 0)
        held_ref[...] = (POLY_ONE + POLY_TWO * mean + POLY_THREE * mean * mean) * held + turned
        return carry

    lax.fori_loop(0, ORTHO_STEPS, sweep, 0)
    return held_ref[...].astype(jnp.bfloat16)


def ortho_kernel(block_ref, out_ref, held_ref):
    out_ref[...] = ortho_sweeps(block_ref[...], held_ref)


def clip_factor(sums, limit):
    gains = sums[:2]
    squares = jnp.sum(gains * gains, axis=0, keepdims=True) + sums[2:3]
    norm = jnp.sqrt(jnp.sum(squares, axis=1, keepdims=True))
    return norm, jnp.minimum(1.0, limit / norm)


def solve_kernel(
    spot_ref, own_sums_ref, own_ref, other_ref, own_momentum, other_momentum, *refs, limit
):
    parts, out_refs, (gain_ref, norm_ref), refs = refs[:6], refs[6:10], refs[10:12], refs[12:]
    new_refs, (block_ref, held_ref) = refs[:6], refs[6:]
    kind, place, start, count = [spot_ref[i] for i in range(4)]
    lead, size = block_ref.shape[:2]
    rows = size // 2
    last = lead // 2 * size
    sums = own_sums_ref[...] + joined_rows(other_ref[last:])
    norm, factor = clip_factor(sums, limit)
    norm_ref[...] = norm
    gain_ref[...] = sums[:2] * factor
    for part in range(3):
        grad = parts[part][...] * factor
        new_refs[part][...] = grad
        new_refs[3 + part][...] = MOMENTUM_DECAY * parts[3 + part][...] + grad
    for index in range(lead):
        spot = slice(index // 2 * size, (index // 2 + 1) * size)
        if index % 2:
            momentum, grad = other_momentum[spot], other_ref[spot]
        else:
            momentum, grad = own_momentum[index // 2], own_ref[index // 2]
        mixed = MOMENTUM_DECAY * momentum.astype(jnp.float32) + factor * grad.astype(jnp.float32)
        row = ((place & (lead - 1)) ^ index) * rows
        here = (kind < 2) | ((row >= start) & (row < start + count))
        block_ref[index, :rows] = jnp.where(here, mixed[:rows], 0.0).astype(jnp.bfloat16)
        block_ref[index, rows:] = jnp.where(kind < 2, mixed[rows:], 0.0).astype(jnp.bfloat16)
    done = ortho_sweeps(block_ref[...].reshape(lead * size, D), held_ref)
    block_ref[...] = done.reshape(lead, size, D)
    for flip in range(4):
        out_refs[flip][...] = block_ref[2 * flip]


def solve(spots, sums, own, other, own_momentum, other_momentum, parts, limit):
    half, size = own.shape[:2]
    in_vmem = pl.BlockSpec(memory_space=pltpu.VMEM)
    in_smem = pl.BlockSpec(memory_space=pltpu.SMEM)
    outs = (shape_of((size, D), jnp.bfloat16),) * 4
    outs += (shape_of((2, D), jnp.float32), shape_of((1, 1), jnp.float32))
    outs += tuple(shape_of(part.shape, jnp.float32) for part in parts)
    return pl.pallas_call(
        partial(solve_kernel, limit=limit),
        out_shape=outs,
        in_specs=[in_smem] + [in_vmem] * 11,
        out_specs=(in_vmem,) * len(outs),
        scratch_shapes=[
            pltpu.VMEM((2 * half, size, D), jnp.bfloat16),
            pltpu.VMEM((2 * half * size, D), jnp.float32),
        ],
        compiler_params=pltpu.CompilerParams(vmem_limit_bytes=58 * 2**20),
    )(spots, sums, own, other, own_momentum, other_momentum, *parts)


def orthogonalize(block):
    rows, columns = block.shape
    small, large = min(block.shape), max(block.shape)
    return call(
        ortho_kernel,
        shape_of(block.shape, jnp.bfloat16),
        (block,),
        2 * ORTHO_STEPS * small * small * (2 * large + small),
        32,
        scratch=(pltpu.VMEM((rows, columns), jnp.float32),),
    )


def block_list():
    q_rows = HEADS * HEAD_DIM
    kv_rows = KV_HEADS * HEAD_DIM
    return (
        (0, 0, q_rows),
        (0, q_rows, kv_rows),
        (0, q_rows + kv_rows, kv_rows),
        (0, q_rows + 2 * kv_rows, q_rows),
        (1, 0, FF),
        (1, FF, FF),
        (2, 0, FF),
    )


def step_rates():
    rates = [set(), set(), set()]
    for owner_id, _, row_count in block_list():
        rates[owner_id].add(0.2 * math.sqrt(max(row_count, D)))
    return [rate for (rate,) in rates]


def from_chip(came, kind, chip, rows):
    found = came[0][:rows].astype(jnp.float32)
    for flip in (1, 2, 3):
        found = jnp.where(kind ^ flip == chip, came[flip][:rows].astype(jnp.float32), found)
    return found


def updated(master, rows, rate):
    return master - MATRIX_RATE * (rate * rows + MATRIX_DECAY * master)


def finish_kernel(spot_ref, *refs):
    came, masters, outs = refs[:4], refs[4:7], refs[7:]
    chips = (spot_ref[1], 0, 1)
    for master, out, chip, rate in zip(masters, outs, chips, step_rates()):
        rows = from_chip(came, spot_ref[0], chip, master.shape[0])
        out[...] = updated(master[...], rows, rate)


def split_rows(value):
    high = lax.reduce_precision(value, 8, 7)
    return jnp.concatenate([high.astype(jnp.bfloat16), (value - high).astype(jnp.bfloat16)], axis=0)


def joined_rows(rows):
    half = rows.shape[0] // 2
    return rows[:half].astype(jnp.float32) + rows[half:].astype(jnp.float32)


class Owners:
    def __init__(self, place, devices):
        self.place, self.devices = place, devices
        self.top_bit = devices.bit_length() - 2
        self.core, self.across, self.along = [bit_of(place, bit) for bit in range(3)]
        self.kind = 2 * self.along + self.across
        self.top = bit_of(place, self.top_bit)
        self.own = place & (devices // 2 - 1)

    def attn_span(self, large):
        q_rows, kv_rows = HEADS * HEAD_DIM, KV_HEADS * HEAD_DIM
        large_start = jnp.where(self.top == 0, 0, kv_rows)
        small_start = jnp.where(self.top == 0, q_rows, 0)
        return jnp.where(large, large_start, small_start), jnp.where(large, q_rows, kv_rows)

    def solve(self, gather, momenta, parts, limit, rows):
        lead = self.devices // 2
        start, count = self.attn_span(self.kind == 2)
        own, own_momentum = gather.flat(), momenta.flat()
        if rows % 16 == 0:
            spots = jnp.stack([self.kind, self.place, start, count])
            return solve(
                spots, gather.sums, own, gather.message, own_momentum, momenta.message, parts, limit
            )
        last = lead // 2 * 2 * rows
        sums = gather.sums + joined_rows(gather.message[last:])
        norm, factor = clip_factor(sums, limit)
        new = [part * factor for part in parts[:3]]
        new += [MOMENTUM_DECAY * part + grad for part, grad in zip(parts[3:], new)]
        grads, momenta = [
            jnp.stack([mine, message[:last].reshape(mine.shape)], axis=1)
            .reshape((lead,) + mine.shape[1:])
            .astype(jnp.float32)
            for mine, message in ((own, gather.message), (own_momentum, momenta.message))
        ]
        row = (jnp.arange(lead) ^ self.own) * rows
        here = ((row >= start) & (row < start + count))[:, None] & (jnp.arange(2 * rows) < rows)
        block = MOMENTUM_DECAY * momenta + factor * grads
        block = jnp.where((self.kind < 2) | here[..., None], block, 0.0).astype(jnp.bfloat16)
        result = orthogonalize(block.reshape(-1, D)).reshape(lead, 2 * rows, D)[:8:2]
        return (*result, sums[:2] * factor, norm, *new)

    def spread(self, result, masters):
        came = [result[0]]
        for flip in (1, 2, 3):
            came.append(exchange(result[flip], flip << 1, self.devices))
        rows = masters[0].shape[0]
        start, count = self.attn_span(True)
        row = self.own * rows
        large = (row >= start) & (row < start + count)
        attn_chip = jnp.where(large, 2, 3)
        if rows % 16 == 0:
            in_smem = pl.BlockSpec(memory_space=pltpu.SMEM)
            in_vmem = pl.BlockSpec(memory_space=pltpu.VMEM)
            return call(
                finish_kernel,
                tuple(shape_of(master.shape, jnp.float32) for master in masters),
                (jnp.stack([self.kind, attn_chip]), *came, *masters),
                0,
                16,
                in_specs=[in_smem] + [in_vmem] * 7,
                out_specs=(in_vmem,) * 3,
            )
        return [
            updated(master, from_chip(came, self.kind, chip, master.shape[0]), rate)
            for master, chip, rate in zip(masters, (attn_chip, 0, 1), step_rates())
        ]


class Gather:
    def __init__(self, owners, gate_up, down, attn, sums=None):
        self.owners, self.sums = owners, sums
        parts = (gate_up, attn, down)
        self.gate_up, self.attn, self.down = [part.astype(jnp.bfloat16)[None] for part in parts]

    def send(self, parts, flip):
        flat = [part.reshape(-1, D) for part in parts]
        few = [] if self.sums is None else [split_rows(self.sums)]
        other = exchange(jnp.concatenate(flat + few, axis=0), flip, self.owners.devices)
        came, start = [], 0
        for part, rows in zip(parts, flat):
            came.append(other[start : start + rows.shape[0]].reshape(part.shape))
            start += rows.shape[0]
        return came, joined_rows(other[start:]) if few else 0.0

    def add(self, few):
        if self.sums is not None:
            self.sums = sum(few, self.sums)

    def widen(self, group):
        top = 1 << self.owners.top_bit
        gate_up, attn, down, few = [self.gate_up], [self.attn], [self.down], []
        for flip in flips_of(group):
            if flip & top:
                (more,), rest = self.send([self.down], flip)
            else:
                came, rest = self.send([self.gate_up, self.attn, self.down], flip)
                gate_up.append(came[0])
                attn.append(came[1])
                more = came[2]
            down.append(more)
            few.append(rest)
        joined = [jnp.concatenate(blocks, axis=0) for blocks in (gate_up, attn, down)]
        self.gate_up, self.attn, self.down = joined
        self.add(few)

    def route(self):
        kind = self.owners.kind
        gate_up = self.gate_up
        down = self.down.reshape(gate_up.shape)
        attn = jnp.pad(self.attn, ((0, 0), (0, self.attn.shape[1]), (0, 0)))
        wanted = lambda owner: jnp.where(owner == 0, gate_up, jnp.where(owner == 1, down, attn))
        blocks, few = [wanted(kind)], []
        for flip in (1, 2, 3):
            (came,), rest = self.send([wanted(kind ^ flip)], flip << 1)
            blocks.append(came)
            few.append(rest)
        self.add(few)
        self.blocks = jnp.stack(blocks, axis=1)

    def join(self):
        few = [split_rows(self.sums)]
        message = jnp.concatenate([self.blocks.reshape(-1, D)] + few, axis=0)
        self.message = exchange(message, 1, self.owners.devices)

    def flat(self):
        return self.blocks.reshape((-1,) + self.blocks.shape[2:])


def per_device(
    inputs,
    out_grad,
    lang_tags,
    attn_master,
    gate_up_master,
    down_master,
    attn_momentum,
    gate_up_momentum,
    down_momentum,
    norm_gains,
    gain_first,
    gain_second,
):
    devices = lax.axis_size(("dp", "sub"))
    device_place = lax.axis_index(("dp", "sub"))
    q_rows = HEADS * HEAD_DIM
    kv_rows = KV_HEADS * HEAD_DIM
    qkv_rows = q_rows + 2 * kv_rows
    tag_hot = (lang_tags[:, None] == jnp.arange(NUM_TAGS, dtype=jnp.int32)[None, :]).astype(
        jnp.float32
    )
    masters = (attn_master, gate_up_master, down_master)
    attn_low = attn_master.astype(jnp.bfloat16)
    gate_up_low = gate_up_master.astype(jnp.bfloat16)
    down_low = down_master.astype(jnp.bfloat16)
    tag_row = jnp.pad(tag_hot[:1], ((0, 0), (0, D - NUM_TAGS)))
    ffn_low = jnp.concatenate([gate_up_low, down_low], axis=0)
    place = device_place
    groups = bit_groups(devices)
    ffn_blocks = lax.all_gather(ffn_low, AXES)
    owners = Owners(place, devices)
    momenta = Gather(owners, gate_up_momentum, down_momentum, attn_momentum, tag_row)
    early = (inputs.astype(jnp.float32), momenta.gate_up, momenta.attn, momenta.down)
    attn_blocks = gather_hop(attn_low[None], groups[-1], devices)
    attn_blocks, early = lax.optimization_barrier((attn_blocks, early))
    hidden_in, momenta.gate_up, momenta.attn, momenta.down = early
    for group in groups[-2:0:-1]:
        attn_blocks = gather_hop(attn_blocks, group, devices)
    for group in groups[2:]:
        momenta.widen(group)
    other_blocks = exchange(attn_blocks, 1, devices)
    momenta.route()
    attn_blocks, other_blocks, momenta.blocks, momenta.sums = lax.optimization_barrier(
        (attn_blocks, other_blocks, momenta.blocks, momenta.sums)
    )
    momenta.join()
    length = inputs.shape[0]
    wide_cos, wide_sin, tall_cos, tall_sin = [jnp.asarray(t) for t in rotary_rows(length)]
    low, single = jnp.bfloat16, jnp.float32
    spot = place[None, None]
    core = bit_of(place, 0)[None, None]
    in_smem = pl.BlockSpec(memory_space=pltpu.SMEM)
    in_vmem = pl.BlockSpec(memory_space=pltpu.VMEM)
    even = down_low.shape[0] % 16 == 0
    attn_outs = (
        shape_of((length, q_rows), low),
        shape_of((length, kv_rows), low),
        shape_of((length, kv_rows), low),
        shape_of((length, D), low),
        shape_of((length, q_rows), low),
        shape_of((HEADS, 1, length), single),
        shape_of((HEADS, 1, length), single),
        shape_of((length, D), single),
        shape_of((length, D), low),
    )
    if even:
        pieces = (attn_blocks, other_blocks)
        attn_outs += (shape_of((devices // 2, 2) + attn_low.shape, low),)
    else:
        whole_weights = in_order(jnp.stack([attn_blocks, other_blocks], 1).reshape(devices, -1), place)
        pieces = (whole_weights.reshape(16, 2, -1, D),)
    queries, keys, values, normed_one, attended_low, peaks, totals, residual, normed_two, *attn_w = call(
        attention_kernel if even else whole_attention_kernel,
        attn_outs,
        (spot, hidden_in, *pieces, norm_gains, wide_cos, wide_sin),
        2 * length * D * 3 * (qkv_rows + q_rows),
        58,
        in_specs=[in_smem] + [in_vmem] * (4 + len(pieces)),
        out_specs=(in_vmem,) * len(attn_outs),
        scratch=(pltpu.VMEM((HEADS + 2 * KV_HEADS, length, HEAD_DIM), low),),
    )
    attn_weights = attn_w[0] if even else pieces[0]
    tag_count = momenta.sums + joined_rows(momenta.message[-2:])
    tags = jnp.concatenate([tag_row, tag_count], axis=0)
    gate_up_rows, down_rows = gate_up_low.shape[0], down_low.shape[0]
    if even:
        weights = (ffn_blocks,)
        weight_specs = [pl.BlockSpec(memory_space=pl.ANY)]
    else:
        ffn_weights = ffn_blocks
        ffn_rows = gate_up_rows + down_rows
        gate_up_weights = ffn_weights[:, :gate_up_rows].reshape(32, -1, D)
        down_weights = ffn_weights[:, gate_up_rows:ffn_rows].reshape(32, -1, D)
        gate_up_rows, down_rows = gate_up_weights.shape[1], down_weights.shape[1]
        weights = (gate_up_weights, down_weights)
        weight_specs = [in_vmem] * 2
    chunk = 768 if even else 384
    steps = FF // chunk
    held_once = dict(pipeline_mode=pl.Buffered(1))
    whole = lambda *shape: pl.BlockSpec(shape, lambda c: (0,) * len(shape), **held_once)
    part = lambda rows: pl.BlockSpec((chunk // rows, rows, D), lambda c: (c, 0, 0))
    if even:
        cut = (gate_up_rows + down_rows) * 9 // 16 // 16 * 16
        other_cut = gate_up_rows + down_rows - cut
        pairs = devices // 2
        grad_outs = tuple(
            shape_of((pairs, size, D), low) for size in (cut, other_cut) for _ in range(2)
        )
        grad_specs = (pl.BlockSpec(memory_space=pl.ANY),) * len(grad_outs)
        lazy = lambda *shape: pl.BlockSpec(memory_space=pl.ANY)
        held_scratch = (
            pltpu.VMEM(ffn_blocks.shape, low),
            pltpu.VMEM((length, D), single),
            pltpu.VMEM((length, q_rows), low),
            pltpu.VMEM(attn_weights.shape, low),
            *[pltpu.VMEM(out.shape, out.dtype) for out in grad_outs],
            pltpu.SemaphoreType.DMA((7 + 3 * steps,)),
        )
    else:
        grad_outs = (
            shape_of((16, gate_up_rows, D), single),
            shape_of((16, gate_up_rows, D), single),
            shape_of((32, down_rows, D), single),
        )
        grad_specs = (part(gate_up_rows), part(gate_up_rows), part(down_rows))
        lazy, held_scratch = whole, ()
    outputs, residual_grad, attended_grad, o_part, gain_two, *ffn_grads = call(
        partial(
            feed_kernel,
            devices=devices,
            gathered=even,
            gate_rows=gate_up_rows,
            down_rows=down_rows,
        ),
        (
            shape_of((D, length), low),
            shape_of((length, D), single),
            shape_of((length, q_rows), low),
            shape_of((q_rows, D), single),
            shape_of((1, D), single),
            *grad_outs,
        ),
        (
            spot,
            tags,
            normed_two,
            residual,
            out_grad.T,
            attended_low,
            *weights,
            attn_weights,
            norm_gains,
        ),
        2 * 3 * length * D * (3 * FF + q_rows),
        58,
        grid=(steps,),
        in_specs=[
            in_smem,
            whole(2, D),
            whole(length, D),
            lazy(length, D),
            whole(D, length),
            lazy(length, q_rows),
            *weight_specs,
            lazy(*attn_weights.shape),
            whole(2, D),
        ],
        out_specs=(
            whole(D, length),
            whole(length, D),
            whole(length, q_rows),
            whole(q_rows, D),
            whole(1, D),
            *grad_specs,
        ),
        scratch=(
            pltpu.VMEM((length, D), single),
            pltpu.VMEM((length, D), single),
            pltpu.VMEM((length, D), low),
            pltpu.VMEM((3, length, chunk), low),
        )
        + held_scratch,
    )
    bits = range(devices.bit_length() - 1)
    if even:
        first_held, first_sent, second_held, second_sent = ffn_grads
        sums = [
            Sums(first_held, place, devices, bits[1:], [exchange(first_sent, 1, devices)]),
            Sums(second_held, place, devices, bits[1:], [exchange(second_sent, 1, devices)]),
        ]
    else:
        gate_up_part = jnp.concatenate([g.reshape(-1, D) for g in ffn_grads[:2]], axis=0)
        sums = [
            Sums(gate_up_part.reshape(devices, -1, D), place, devices, bits),
            Sums(ffn_grads[2].reshape(devices, -1, D), place, devices, bits),
        ]
        for s in sums:
            s.hop(0)
    head_outs = (
        shape_of((length, q_rows // KV_HEADS), low),
        shape_of((length, HEAD_DIM), low),
        shape_of((length, HEAD_DIM), low),
    )
    head_grads = []
    for heads in ((0,), (1, 2)):
        head_grads += call(
            partial(heads_kernel, heads),
            head_outs * len(heads),
            (queries, keys, values, attended_grad, peaks, totals, tall_cos, tall_sin),
            2 * 2 * length * length * q_rows * len(heads),
            58,
            scratch=(
                pltpu.VMEM((length, HEAD_DIM), single),
                pltpu.VMEM((length, HEAD_DIM), single),
            ),
        )
        if heads == (0,):
            attended_grad, head_grads = after((attended_grad, head_grads), sums)
            sums[0].hop(1)
            sums[1].hop(2)
    normed_one, head_grads = after((normed_one, head_grads), sums)
    proj_parts = [head_grads[3 * head + kind] for kind in range(3) for head in range(KV_HEADS)]
    sums[0].hop(2)
    sums[1].hop(1)
    if even:
        grad_outs = (
            shape_of((pairs, attn_low.shape[0], D), low),
            shape_of((pairs, attn_low.shape[0], D), low),
        )
    else:
        grad_outs = (shape_of((qkv_rows + q_rows, D), single),)
    joined, *attn_grads = call(
        qkv_kernel,
        (shape_of((length, qkv_rows), low), *grad_outs),
        (core, *proj_parts, normed_one, o_part),
        2 * length * D * qkv_rows,
        58,
        in_specs=[in_smem] + [in_vmem] * 11,
        out_specs=(in_vmem,) * (1 + len(grad_outs)),
    )
    joined, attn_grads = after((joined, attn_grads), sums)
    if even:
        held, sent = attn_grads
        late = Sums(held, place, devices, bits[1:], [exchange(sent, 1, devices)])
    else:
        late = Sums(attn_grads[0].reshape(devices, -1, D), place, devices, bits)
        late.hop(0)
    feed_rows = [s.shape[0] for s in sums]
    feed_sums = Sums(
        jnp.concatenate([s.total() for s in sums], axis=1), place, devices, bits[3:]
    )
    feed_sums.hop(*groups[2])
    residual_grad = after(residual_grad, [late])
    late.hop(*groups[1])
    input_grad, gain_one = call(
        input_kernel,
        (shape_of((D, length), low), shape_of((1, D), single)),
        (joined, attn_weights, hidden_in, residual_grad, norm_gains),
        2 * length * D * qkv_rows,
        58,
    )
    input_grad = after(input_grad, [late, feed_sums])
    for group in groups[3:]:
        feed_sums.hop(*group)
    feed_total = feed_sums.total()[0]
    if even:
        gate_up_sum = feed_total[:gate_up_rows]
        down_sum = feed_total[gate_up_rows:]
    else:
        gate_up_sum, down_sum = feed_total[: feed_rows[0]], feed_total[feed_rows[0] :]
    for group in groups[2:]:
        late.hop(*group)
    attn_sum = late.total()[0]
    squares = sum(
        jnp.sum(part * part, axis=0, keepdims=True) for part in (attn_sum, gate_up_sum, down_sum)
    )
    small_sums = jnp.concatenate([gain_one, gain_two, squares], axis=0)
    gather = Gather(owners, gate_up_sum, down_sum, attn_sum, small_sums)
    for group in groups[2:]:
        gather.widen(group)
    gather.route()
    gather.join()
    param_count = (qkv_rows + q_rows + 3 * FF) * D + 2 * D
    limit = CLIP_SCALE * math.sqrt(devices * length * param_count)
    down_count = down_low.shape[0]
    parts = (attn_sum, gate_up_sum, down_sum, attn_momentum, gate_up_momentum, down_momentum)
    solved = owners.solve(gather, momenta, parts, limit, down_count)
    solved, (gain_grad, grad_norm, *new) = solved[:4], solved[4:]
    attn_grad, gate_up_grad, down_grad, attn_moment, gate_up_moment, down_moment = new
    grad_norm = grad_norm[0, 0]
    new_masters = owners.spread(solved, masters)
    first_new = BETA_FIRST * gain_first + (1.0 - BETA_FIRST) * gain_grad
    second_new = BETA_SECOND * gain_second + (1.0 - BETA_SECOND) * gain_grad * gain_grad
    gains_new = norm_gains - GAIN_RATE * (first_new / (1.0 - BETA_FIRST**STEP_NUMBER)) / (
        jnp.sqrt(second_new / (1.0 - BETA_SECOND**STEP_NUMBER)) + ADAM_EPS
    )
    return (
        outputs.T,
        input_grad.T,
        attn_grad,
        gate_up_grad,
        down_grad,
        grad_norm,
        attn_moment,
        gate_up_moment,
        down_moment,
        new_masters[0],
        new_masters[1],
        new_masters[2],
        gain_grad,
        first_new,
        second_new,
        gains_new,
    )


def solution(mesh):
    placed = (
        P(("dp", "sub"), None),
        P(("dp", "sub"), None),
        P(("dp", "sub")),
        P(("dp", "sub"), None),
        P(("dp", "sub"), None),
        P(("dp", "sub"), None),
        P(("dp", "sub"), None),
        P(("dp", "sub"), None),
        P(("dp", "sub"), None),
        P(),
        P(),
        P(),
    )
    return jax.shard_map(
        per_device,
        mesh=mesh,
        in_specs=placed,
        out_specs=(
            P(("dp", "sub"), None),
            P(("dp", "sub"), None),
            P(("dp", "sub"), None),
            P(("dp", "sub"), None),
            P(("dp", "sub"), None),
            P(),
            P(("dp", "sub"), None),
            P(("dp", "sub"), None),
            P(("dp", "sub"), None),
            P(("dp", "sub"), None),
            P(("dp", "sub"), None),
            P(("dp", "sub"), None),
            P(),
            P(),
            P(),
            P(),
        ),
        check_vma=False,
    )
```

```python
from functools import partial
import math

import jax
import jax.numpy as jnp
import numpy as np
from jax import lax
from jax.experimental import pallas as pl
from jax.experimental.pallas import tpu as pltpu
from jax.sharding import PartitionSpec as P

D = 576
HEADS = 9
KV_HEADS = 3
HEAD_DIM = 64
FF = 1536
NUM_TAGS = 8
ORTHO_STEPS = 5
STEP_NUMBER = 10


NORM_EPS = 1e-05
ROPE_BASE = 100000.0
POLY_ONE = 3.4445
POLY_TWO = -4.775
POLY_THREE = 2.0315
MOMENTUM_DECAY = 0.95
MATRIX_RATE = 0.2
MATRIX_DECAY = 0.1
GAIN_RATE = 1.0
BETA_FIRST = 0.9
BETA_SECOND = 0.95
ADAM_EPS = 1e-08
CLIP_SCALE = 0.002


AXES = ("dp", "sub")


def bit_of(place, bit):
    return (place >> bit) & 1


def exchange(array, flip, devices, source=None):
    pairs = [(i, i ^ flip) for i in range(devices) if source is None or source(i)]
    return lax.ppermute(array, AXES, pairs)


def bit_groups(devices):
    bits = devices.bit_length() - 1
    return [(0,)] + [tuple(range(bit, min(bit + 2, bits))) for bit in range(1, bits, 2)]


def flips_of(group):
    return [part << group[0] for part in range(1, 1 << len(group))]


def pick(array, axis, index):
    return lax.dynamic_index_in_dim(array, index, axis, keepdims=False)


def gather_hop(blocks, group, devices, front=False, source=None):
    came = [exchange(blocks, flip, devices, source) for flip in flips_of(group)]
    stacked = jnp.stack([blocks] + came, axis=0 if front else 1)
    return stacked.reshape((-1,) + blocks.shape[1:])


def in_order(blocks, place):
    return jnp.take(blocks, jnp.arange(blocks.shape[0]) ^ place, axis=0)


class Sums:
    def __init__(self, held, place, devices, bits, came=()):
        self.place, self.devices, self.bits = place, devices, list(bits)
        self.shape = held.shape[-2:]
        self.held, self.came = held, list(came)

    def hop(self, *group):
        low, width = self.bits.index(group[0]), len(group)
        high = len(self.bits) - low - width
        terms = [
            term.reshape((1 << high, 1 << width, 1 << low) + self.shape)
            for term in [self.held] + self.came
        ]
        mine = (self.place >> group[0]) & ((1 << width) - 1)

        def part(index):
            chosen = [pick(term, 1, index).astype(jnp.float32) for term in terms]
            return sum(chosen[1:], chosen[0]).reshape((-1,) + self.shape)

        sent = [part(mine ^ flip).astype(jnp.bfloat16) for flip in range(1, 1 << width)]
        self.held = part(mine)
        self.came = [exchange(s, f, self.devices) for s, f in zip(sent, flips_of(group))]
        for bit in group:
            self.bits.remove(bit)

    def total(self):
        return sum([term.astype(jnp.float32) for term in [self.held] + self.came])


def after(value, sums):
    value, came = lax.optimization_barrier((value, [s.came for s in sums]))
    for s, c in zip(sums, came):
        s.came = c
    return value


SCORE_SCALE = HEAD_DIM ** (-0.5)
MASKED = -1e30


def product(left, right, left_dim, right_dim):
    return lax.dot_general(
        left, right, (((left_dim,), (right_dim,)), ((), ())), preferred_element_type=jnp.float32
    )


def call(kernel, outs, args, flops, mib, grid=(), in_specs=None, out_specs=None, scratch=()):
    specs = {} if in_specs is None else dict(in_specs=in_specs, out_specs=out_specs)
    listed = tuple(outs) if isinstance(outs, (tuple, list)) else (outs,)
    moved = sum(math.prod(a.shape) * a.dtype.itemsize for a in tuple(args) + listed)
    return pl.pallas_call(
        kernel,
        out_shape=outs,
        grid=grid,
        scratch_shapes=scratch,
        compiler_params=pltpu.CompilerParams(vmem_limit_bytes=mib * 2**20),
        cost_estimate=pl.CostEstimate(flops=int(flops), bytes_accessed=moved, transcendentals=0),
        **specs,
    )(*args)


def shape_of(shape, dtype):
    return jax.ShapeDtypeStruct(shape, dtype)


def rotary_rows(length):
    half_dim = HEAD_DIM // 2
    frequency = np.float32(ROPE_BASE) ** (
        -(np.arange(half_dim, dtype=np.float32) * np.float32(2.0 / HEAD_DIM))
    )
    angles = np.arange(length, dtype=np.float32)[:, None] * frequency[None, :].astype(np.float32)
    cosine, sine = np.cos(angles), np.sin(angles)
    wide_cosine = np.concatenate([cosine] * 4, axis=1)
    wide_sine = np.concatenate([-sine, sine, -sine, sine], axis=1)
    return wide_cosine, wide_sine, cosine.T.copy(), sine.T.copy()


def causal_mask(size):
    key_pos = lax.broadcasted_iota(jnp.int32, (size, size), 0)
    query_pos = lax.broadcasted_iota(jnp.int32, (size, size), 1)
    return key_pos <= query_pos


def scores_by_key(keys, queries, mask):
    size = queries.shape[0]
    before = keys.shape[0] - size
    raw = product(keys, queries, 1, 1)
    last = jnp.where(mask, raw[before:], MASKED)
    return last if before == 0 else jnp.concatenate([raw[:before], last], axis=0)


def scaled_norm(values, gain):
    inverse = lax.rsqrt(jnp.mean(values * values, axis=-1, keepdims=True) + NORM_EPS)
    return values * inverse * gain, inverse


def attention_kernel(
    place_ref, x_ref, own_ref, other_ref, gain_ref, cos_ref, sin_ref,
    q_ref, k_ref, v_ref, normed_ref, low_ref, peak_ref, total_ref, res_ref, two_ref, joined_ref,
    heads_ref,
):
    length = x_ref.shape[0]
    q_rows = HEADS * HEAD_DIM
    kv_rows = KV_HEADS * HEAD_DIM
    turned = q_rows + kv_rows
    if other_ref is None:
        w_ref = own_ref
    else:
        core, pair = place_ref[0, 0] & 1, place_ref[0, 0] >> 1
        for index in range(own_ref.shape[0]):
            joined_ref[index ^ pair, core] = own_ref[index]
            joined_ref[index ^ pair, 1 - core] = other_ref[index]
        w_ref = joined_ref
    weights = w_ref[...].reshape(-1, D)
    size = min(256, length)
    lane = lax.broadcasted_iota(jnp.int32, (size, turned), 1)
    first = lane % HEAD_DIM < HEAD_DIM // 2
    for start in range(0, length, size):
        rows = slice(start, start + size)
        normed = scaled_norm(x_ref[rows], gain_ref[0:1])[0].astype(jnp.bfloat16)
        normed_ref[rows] = normed
        raw = product(normed, weights[: turned + kv_rows], 1, 1)
        both = raw[:, :turned]
        swapped = jnp.where(
            first,
            pltpu.roll(both, turned - HEAD_DIM // 2, 1),
            pltpu.roll(both, HEAD_DIM // 2, 1),
        )
        cosine = jnp.concatenate([cos_ref[rows]] * (turned // 128), axis=1)
        sine = jnp.concatenate([sin_ref[rows]] * (turned // 128), axis=1)
        both = both * cosine + swapped * sine
        q_ref[rows] = both[:, :q_rows].astype(jnp.bfloat16)
        k_ref[rows] = both[:, q_rows:].astype(jnp.bfloat16)
        v_ref[rows] = raw[:, turned:].astype(jnp.bfloat16)
    size = min(512, length)
    mask = causal_mask(size)
    group = HEADS // KV_HEADS
    span = lambda head: slice(head * HEAD_DIM, (head + 1) * HEAD_DIM)
    for head in range(HEADS):
        heads_ref[head] = q_ref[:, span(head)] * jnp.bfloat16(SCORE_SCALE)
    for head in range(KV_HEADS):
        heads_ref[HEADS + head] = k_ref[:, span(head)]
        heads_ref[HEADS + KV_HEADS + head] = v_ref[:, span(head)]

    def attend(head, carry):
        keys_at = HEADS + head // group
        for start in range(0, length, size):
            end = start + size
            queries = heads_ref[head, start:end]
            scores = scores_by_key(heads_ref[keys_at, :end], queries, mask)
            peak = jnp.max(scores, axis=0, keepdims=True)
            shifted = jnp.exp(scores - peak)
            inverse = 1.0 / jnp.sum(shifted, axis=0, keepdims=True)
            prob_low = (shifted * inverse).astype(jnp.bfloat16)
            out = product(heads_ref[keys_at + KV_HEADS, :end], prob_low, 0, 0)
            heads_ref[head, start:end] = out.T.astype(jnp.bfloat16)
            peak_ref[head, :, start:end] = peak
            total_ref[head, :, start:end] = inverse
        return carry

    lax.fori_loop(0, HEADS, attend, 0)
    low_ref[...] = jnp.concatenate([heads_ref[head] for head in range(HEADS)], axis=1)
    size = min(256, length)
    for start in range(0, length, size):
        rows = slice(start, start + size)
        residual = x_ref[rows] + product(low_ref[rows], weights[turned + kv_rows :], 1, 0)
        res_ref[rows] = residual
        two_ref[rows] = scaled_norm(residual, gain_ref[1:2])[0].astype(jnp.bfloat16)


def whole_attention_kernel(place_ref, x_ref, own_ref, *refs):
    attention_kernel(place_ref, x_ref, own_ref, None, *refs[:-1], None, refs[-1])


def feed_kernel(
    place_ref, tags_ref, two_ref, res_ref, grad_ref, low_ref, *refs,
    devices, gathered, gate_rows, down_rows,
):
    cut = 1 if gathered else 2
    weight_refs, refs = refs[:cut], refs[cut:]
    attn_ref, gain_ref, out_ref, back_ref, att_ref, do_ref, dgain_ref, *refs = refs
    if gathered:
        *refs, sems = refs
        refs, held_refs, grad_refs = refs[:-8], refs[-8:-4], refs[-4:]
        *grad_outs, sum_ref, inner_ref, coming_ref, hidden_ref = refs
    else:
        *grad_refs, sum_ref, inner_ref, coming_ref, hidden_ref = refs
    step = pl.program_id(0)
    length = two_ref.shape[0]
    size = min(256, length)
    core = place_ref[0, 0] & 1
    chunk = hidden_ref.shape[2]
    gate_blocks, down_blocks = chunk // gate_rows, chunk // down_rows
    count = jnp.sum(tags_ref[0:1] * tags_ref[1:2], axis=1, keepdims=True)
    weight = devices / (NUM_TAGS * count)
    if gathered:
        weights_ref, res_held, low_held, attn_held = held_refs
        later = [
            pltpu.make_async_copy(source, target, sems.at[at])
            for at, (source, target) in enumerate(
                ((res_ref, res_held), (low_ref, low_held), (attn_ref, attn_held))
            )
        ]
        leaving = [
            pltpu.make_async_copy(source, target, sems.at[3 + at])
            for at, (source, target) in enumerate(zip(grad_refs, grad_outs))
        ]

        def weight_copies(part):
            gates = pl.ds(part * gate_blocks, gate_blocks)
            ups = pl.ds(FF // gate_rows + part * gate_blocks, gate_blocks)
            downs = pl.ds(part * down_blocks, down_blocks)
            upper, lower = pl.ds(0, gate_rows), pl.ds(gate_rows, down_rows)
            return [
                pltpu.make_async_copy(
                    weight_refs[0].at[spot, rows],
                    weights_ref.at[spot, rows],
                    sems.at[7 + 3 * part + at],
                )
                for at, (spot, rows) in enumerate(((gates, upper), (ups, upper), (downs, lower)))
            ]

        @pl.when(step == 0)
        def _():
            for part in range(FF // chunk):
                for copy in weight_copies(part):
                    copy.start()
            for copy in later:
                copy.start()

        res_ref, low_ref, attn_ref = res_held, low_held, attn_held
        gate_ref, down_ref, first_row = weights_ref, weights_ref, gate_rows
    else:
        (gate_ref, down_ref), first_row = weight_refs, 0
    @pl.when(step == 0)
    def _():
        for start in range(0, length, size):
            rows = slice(start, start + size)
            grad = grad_ref[:, rows].astype(jnp.float32).T
            coming_ref[rows] = (grad * weight).astype(jnp.bfloat16)
        sum_ref[...] = jnp.zeros_like(sum_ref)
        inner_ref[...] = jnp.zeros_like(inner_ref)

    if gathered:
        for part in range(FF // chunk):

            @pl.when(step == part)
            def _(part=part):
                for copy in weight_copies(part):
                    copy.wait()

    gate_spots = pl.ds(step * gate_blocks, gate_blocks)
    up_spots = pl.ds(FF // gate_rows + step * gate_blocks, gate_blocks)
    gate_w = gate_ref[gate_spots, :gate_rows].reshape(-1, D)
    up_w = gate_ref[up_spots, :gate_rows].reshape(-1, D)
    down_spots = pl.ds(step * down_blocks, down_blocks)
    down_w = down_ref[down_spots, first_row : first_row + down_rows].reshape(-1, D)

    tile = min(512, length)

    def feed_tile(index, carry):
        rows = pl.ds(pl.multiple_of(index * tile, tile), tile)
        two = two_ref[rows]
        gate = product(two, gate_w, 1, 1)
        up = product(two, up_w, 1, 1)
        sigmoid = 0.5 * jnp.tanh(0.5 * gate) + 0.5
        silu = gate * sigmoid
        activation = (silu * up).astype(jnp.bfloat16)
        act_grad = product(coming_ref[rows], down_w, 1, 1)
        gate_low = act_grad * up * (sigmoid * (1.0 + gate * (1.0 - sigmoid)))
        gate_low = gate_low.astype(jnp.bfloat16)
        up_low = (act_grad * silu).astype(jnp.bfloat16)
        sum_ref[rows] += product(activation, down_w, 1, 0)
        inner_ref[rows] += product(gate_low, gate_w, 1, 0) + product(up_low, up_w, 1, 0)
        for kind, value in enumerate((gate_low, up_low, activation)):
            hidden_ref[kind, rows] = value
        return carry

    lax.fori_loop(0, length // tile, feed_tile, 0)
    gate_grad = product(hidden_ref[0], two_ref[...], 0, 0)
    up_grad = product(hidden_ref[1], two_ref[...], 0, 0)
    down_grad = product(hidden_ref[2], coming_ref[...], 0, 0)
    if len(grad_refs) == 3:
        for ref, grad in zip(grad_refs, (gate_grad, up_grad, down_grad)):
            ref[...] = grad.reshape(ref.shape)
    else:
        first_held, first_sent, second_held, second_sent = grad_refs
        cut = first_held.shape[1]
        pairs = first_held.shape[0]
        for kind, grad in enumerate((gate_grad, up_grad, down_grad)):
            blocks, rows = (down_blocks, down_rows) if kind == 2 else (gate_blocks, gate_rows)
            grad = grad.reshape(blocks // 2, 2, rows, D)
            kept = jnp.where(core == 0, grad[:, 0], grad[:, 1]).astype(jnp.bfloat16)
            sent = jnp.where(core == 0, grad[:, 1], grad[:, 0]).astype(jnp.bfloat16)
            start = step * (blocks // 2) + (pairs // 2 if kind == 1 else 0)
            spot = pl.ds(start, blocks // 2)
            if kind == 2:
                second_held[spot, gate_rows - cut :, :] = kept
                second_sent[spot, gate_rows - cut :, :] = sent
            else:
                first_held[spot] = kept[:, :cut]
                first_sent[spot] = sent[:, :cut]
                second_held[spot, : rows - cut, :] = kept[:, cut:]
                second_sent[spot, : rows - cut, :] = sent[:, cut:]

    @pl.when(step == pl.num_programs(0) - 1)
    def _():
        if gathered:
            for copy in leaving:
                copy.start()
            for copy in later:
                copy.wait()
        o_w = attn_ref[-(attn_ref.shape[0] * HEADS // (2 * (HEADS + KV_HEADS))) :].reshape(-1, D)
        dgain_ref[...] = jnp.zeros_like(dgain_ref)
        for start in range(0, length, size):
            rows = slice(start, start + size)
            residual = res_ref[rows]
            out_ref[:, rows] = (residual + sum_ref[rows]).T.astype(jnp.bfloat16)
            inner = inner_ref[rows]
            inverse = scaled_norm(residual, 1.0)[1]
            scaled = inner * gain_ref[1:2]
            dgain_ref[...] += jnp.sum(inner * residual * inverse, axis=0, keepdims=True)
            back = (
                grad_ref[:, rows].astype(jnp.float32).T * weight
                + inverse * scaled
                - residual
                * (inverse * inverse * inverse)
                * jnp.mean(scaled * residual, axis=-1, keepdims=True)
            )
            back_ref[rows] = back
            coming_ref[rows] = back.astype(jnp.bfloat16)
        do_ref[...] = product(low_ref[...], coming_ref[...], 0, 0)
        att_ref[...] = product(coming_ref[...], o_w, 1, 1).astype(jnp.bfloat16)
        if gathered:
            for copy in leaving:
                copy.wait()


def heads_kernel(heads, *refs):
    outs = refs[8:-2]
    for index, head in enumerate(heads):
        head_kernel(head, *refs[:8], *outs[3 * index : 3 * index + 3], *refs[-2:])


def head_kernel(
    head, q_ref, k_ref, v_ref, grad_ref, peak_ref, total_ref, cos_ref, sin_ref,
    dq_ref, dk_ref, dv_ref, key_sum, value_sum,
):
    length = q_ref.shape[0]
    size = min(256, length)
    half_dim = HEAD_DIM // 2
    mask = causal_mask(size)
    group = HEADS // KV_HEADS
    shared = slice(head * HEAD_DIM, (head + 1) * HEAD_DIM)
    key_sum[...] = jnp.zeros_like(key_sum)
    value_sum[...] = jnp.zeros_like(value_sum)

    def turn_back(grad, columns):
        first, second = grad[:half_dim], grad[half_dim:]
        cosine, sine = cos_ref[:, columns], sin_ref[:, columns]
        turned = [first * cosine + second * sine, second * cosine - first * sine]
        return jnp.concatenate(turned, axis=0).T

    for member in range(group):
        row = head * group + member
        place = slice(row * HEAD_DIM, (row + 1) * HEAD_DIM)
        for start in range(0, length, size):
            end = start + size
            queries = q_ref[start:end, place] * jnp.bfloat16(SCORE_SCALE)
            grad = grad_ref[start:end, place]
            keys, values = k_ref[:end, shared], v_ref[:end, shared]
            scores = scores_by_key(keys, queries, mask)
            probs = (
                jnp.exp(scores - peak_ref[row, :, start:end])
                * total_ref[row, :, start:end]
            )
            moved = probs * product(values, grad, 1, 1)
            score_grad = (moved - probs * jnp.sum(moved, axis=0, keepdims=True)).astype(
                jnp.bfloat16
            )
            value_sum[:end] += product(probs.astype(jnp.bfloat16), grad, 1, 0)
            key_sum[:end] += product(score_grad, queries, 1, 0)
            back = turn_back(product(keys, score_grad, 0, 0) * SCORE_SCALE, slice(start, end))
            dq_ref[start:end, member * HEAD_DIM : (member + 1) * HEAD_DIM] = back.astype(
                jnp.bfloat16
            )
    dk_ref[...] = turn_back(key_sum[...].T, slice(0, length)).astype(jnp.bfloat16)
    dv_ref[...] = value_sum[...].astype(jnp.bfloat16)


def qkv_kernel(core_ref, *refs):
    parts, (normed_ref, o_ref, joined_ref), out_refs = refs[:9], refs[9:12], refs[12:]
    start = 0
    for part in parts:
        joined_ref[:, start : start + part.shape[1]] = part[...]
        start += part.shape[1]
    grad = product(joined_ref[...], normed_ref[...], 0, 0)
    if len(out_refs) == 1:
        out_refs[0][:start] = grad
        out_refs[0][start:] = o_ref[...]
        return
    held_ref, sent_ref = out_refs
    rows = held_ref.shape[1]
    spot = 0
    for value in (grad, o_ref[...]):
        value = value.reshape(-1, 2, rows, D)
        end = spot + value.shape[0]
        held = jnp.where(core_ref[0, 0] == 0, value[:, 0], value[:, 1])
        held_ref[spot:end] = held.astype(jnp.bfloat16)
        sent = jnp.where(core_ref[0, 0] == 0, value[:, 1], value[:, 0])
        sent_ref[spot:end] = sent.astype(jnp.bfloat16)
        spot = end


def input_kernel(joined_ref, w_ref, x_ref, back_ref, gain_ref, out_ref, dgain_ref):
    length = x_ref.shape[0]
    size = min(256, length)
    count = joined_ref.shape[1]
    weights = w_ref[...].reshape(-1, D)[:count]
    dgain_ref[...] = jnp.zeros_like(dgain_ref)
    for start in range(0, length, size):
        rows = slice(start, start + size)
        inner = product(joined_ref[rows], weights, 1, 0)
        hidden = x_ref[rows]
        inverse = scaled_norm(hidden, 1.0)[1]
        scaled = inner * gain_ref[0:1]
        dgain_ref[...] += jnp.sum(inner * hidden * inverse, axis=0, keepdims=True)
        grad = (
            back_ref[rows]
            + inverse * scaled
            - hidden
            * (inverse * inverse * inverse)
            * jnp.mean(scaled * hidden, axis=-1, keepdims=True)
        )
        out_ref[:, rows] = grad.T.astype(jnp.bfloat16)


def symmetric_product(left, right, left_dim):
    size = right.shape[1]
    cut = size // 256 * 256
    if cut == 0 or cut == size or left_dim == 1 and left.shape[0] != size:
        return product(left, right, left_dim, 0)
    first = product(left, right[:, :cut], left_dim, 0)
    rest = left[:, cut:] if left_dim == 0 else left[cut:]
    corner = product(rest, right[:, cut:], left_dim, 0)
    second = jnp.concatenate([first[cut:].T, corner], axis=0)
    return jnp.concatenate([first, second], axis=1)


def ortho_sweeps(block, held_ref):
    size = min(block.shape)
    left = block.shape[0] < block.shape[1]
    block = block.astype(jnp.float32)
    held_ref[...] = block * (1.0 / (jnp.sqrt(jnp.sum(block * block)) + 1e-07))
    row = lax.broadcasted_iota(jnp.int32, (size, size), 0)
    diagonal = row == lax.broadcasted_iota(jnp.int32, (size, size), 1)

    def sweep(index, carry):
        held = held_ref[...]
        scaled = held.astype(jnp.bfloat16)
        gram = product(scaled, scaled, 1, 1) if left else symmetric_product(scaled, scaled, 0)
        mean = jnp.sum(jnp.where(diagonal, gram, 0.0)) / size
        rest = jnp.where(diagonal, gram - mean, gram)
        rest_low = rest.astype(jnp.bfloat16)
        square = symmetric_product(rest_low, rest_low, 1)
        poly = (POLY_TWO + 2.0 * POLY_THREE * mean) * rest + POLY_THREE * square
        poly_low = poly.astype(jnp.bfloat16)
        turned = product(poly_low, scaled, 1, 0) if left else product(scaled, poly_low, 1, 0)
        held_ref[...] = (POLY_ONE + POLY_TWO * mean + POLY_THREE * mean * mean) * held + turned
        return carry

    lax.fori_loop(0, ORTHO_STEPS, sweep, 0)
    return held_ref[...].astype(jnp.bfloat16)


def ortho_kernel(block_ref, out_ref, held_ref):
    out_ref[...] = ortho_sweeps(block_ref[...], held_ref)


def clip_factor(sums, limit):
    gains = sums[:2]
    squares = jnp.sum(gains * gains, axis=0, keepdims=True) + sums[2:3]
    norm = jnp.sqrt(jnp.sum(squares, axis=1, keepdims=True))
    return norm, jnp.minimum(1.0, limit / norm)


def solve_kernel(
    spot_ref, own_sums_ref, own_ref, other_ref, own_momentum, other_momentum, *refs, limit
):
    parts, out_refs, (gain_ref, norm_ref), refs = refs[:6], refs[6:10], refs[10:12], refs[12:]
    new_refs, (block_ref, held_ref) = refs[:6], refs[6:]
    kind, place, start, count = [spot_ref[i] for i in range(4)]
    lead, size = block_ref.shape[:2]
    rows = size // 2
    last = lead // 2 * size
    sums = own_sums_ref[...] + joined_rows(other_ref[last:])
    norm, factor = clip_factor(sums, limit)
    norm_ref[...] = norm
    gain_ref[...] = sums[:2] * factor
    for part in range(3):
        grad = parts[part][...] * factor
        new_refs[part][...] = grad
        new_refs[3 + part][...] = MOMENTUM_DECAY * parts[3 + part][...] + grad
    for index in range(lead):
        spot = slice(index // 2 * size, (index // 2 + 1) * size)
        if index % 2:
            momentum, grad = other_momentum[spot], other_ref[spot]
        else:
            momentum, grad = own_momentum[index // 2], own_ref[index // 2]
        mixed = MOMENTUM_DECAY * momentum.astype(jnp.float32) + factor * grad.astype(jnp.float32)
        row = ((place & (lead - 1)) ^ index) * rows
        here = (kind < 2) | ((row >= start) & (row < start + count))
        block_ref[index, :rows] = jnp.where(here, mixed[:rows], 0.0).astype(jnp.bfloat16)
        block_ref[index, rows:] = jnp.where(kind < 2, mixed[rows:], 0.0).astype(jnp.bfloat16)
    done = ortho_sweeps(block_ref[...].reshape(lead * size, D), held_ref)
    block_ref[...] = done.reshape(lead, size, D)
    for flip in range(4):
        out_refs[flip][...] = block_ref[2 * flip]


def solve(spots, sums, own, other, own_momentum, other_momentum, parts, limit):
    half, size = own.shape[:2]
    in_vmem = pl.BlockSpec(memory_space=pltpu.VMEM)
    in_smem = pl.BlockSpec(memory_space=pltpu.SMEM)
    outs = (shape_of((size, D), jnp.bfloat16),) * 4
    outs += (shape_of((2, D), jnp.float32), shape_of((1, 1), jnp.float32))
    outs += tuple(shape_of(part.shape, jnp.float32) for part in parts)
    return pl.pallas_call(
        partial(solve_kernel, limit=limit),
        out_shape=outs,
        in_specs=[in_smem] + [in_vmem] * 11,
        out_specs=(in_vmem,) * len(outs),
        scratch_shapes=[
            pltpu.VMEM((2 * half, size, D), jnp.bfloat16),
            pltpu.VMEM((2 * half * size, D), jnp.float32),
        ],
        compiler_params=pltpu.CompilerParams(vmem_limit_bytes=58 * 2**20),
    )(spots, sums, own, other, own_momentum, other_momentum, *parts)


def orthogonalize(block):
    rows, columns = block.shape
    small, large = min(block.shape), max(block.shape)
    return call(
        ortho_kernel,
        shape_of(block.shape, jnp.bfloat16),
        (block,),
        2 * ORTHO_STEPS * small * small * (2 * large + small),
        32,
        scratch=(pltpu.VMEM((rows, columns), jnp.float32),),
    )


def block_list():
    q_rows = HEADS * HEAD_DIM
    kv_rows = KV_HEADS * HEAD_DIM
    return (
        (0, 0, q_rows),
        (0, q_rows, kv_rows),
        (0, q_rows + kv_rows, kv_rows),
        (0, q_rows + 2 * kv_rows, q_rows),
        (1, 0, FF),
        (1, FF, FF),
        (2, 0, FF),
    )


def step_rates():
    rates = [set(), set(), set()]
    for owner_id, _, row_count in block_list():
        rates[owner_id].add(0.2 * math.sqrt(max(row_count, D)))
    return [rate for (rate,) in rates]


def from_chip(came, kind, chip, rows):
    found = came[0][:rows].astype(jnp.float32)
    for flip in (1, 2, 3):
        found = jnp.where(kind ^ flip == chip, came[flip][:rows].astype(jnp.float32), found)
    return found


def updated(master, rows, rate):
    return master - MATRIX_RATE * (rate * rows + MATRIX_DECAY * master)


def finish_kernel(spot_ref, *refs):
    came, masters, outs = refs[:4], refs[4:7], refs[7:]
    chips = (spot_ref[1], 0, 1)
    for master, out, chip, rate in zip(masters, outs, chips, step_rates()):
        rows = from_chip(came, spot_ref[0], chip, master.shape[0])
        out[...] = updated(master[...], rows, rate)


def split_rows(value):
    high = lax.reduce_precision(value, 8, 7)
    return jnp.concatenate([high.astype(jnp.bfloat16), (value - high).astype(jnp.bfloat16)], axis=0)


def joined_rows(rows):
    half = rows.shape[0] // 2
    return rows[:half].astype(jnp.float32) + rows[half:].astype(jnp.float32)


class Owners:
    def __init__(self, place, devices):
        self.place, self.devices = place, devices
        self.top_bit = devices.bit_length() - 2
        self.core, self.across, self.along = [bit_of(place, bit) for bit in range(3)]
        self.kind = 2 * self.along + self.across
        self.top = bit_of(place, self.top_bit)
        self.own = place & (devices // 2 - 1)

    def attn_span(self, large):
        q_rows, kv_rows = HEADS * HEAD_DIM, KV_HEADS * HEAD_DIM
        large_start = jnp.where(self.top == 0, 0, kv_rows)
        small_start = jnp.where(self.top == 0, q_rows, 0)
        return jnp.where(large, large_start, small_start), jnp.where(large, q_rows, kv_rows)

    def solve(self, gather, momenta, parts, limit, rows):
        lead = self.devices // 2
        start, count = self.attn_span(self.kind == 2)
        own, own_momentum = gather.flat(), momenta.flat()
        if rows % 16 == 0:
            spots = jnp.stack([self.kind, self.place, start, count])
            return solve(
                spots, gather.sums, own, gather.message, own_momentum, momenta.message, parts, limit
            )
        last = lead // 2 * 2 * rows
        sums = gather.sums + joined_rows(gather.message[last:])
        norm, factor = clip_factor(sums, limit)
        new = [part * factor for part in parts[:3]]
        new += [MOMENTUM_DECAY * part + grad for part, grad in zip(parts[3:], new)]
        grads, momenta = [
            jnp.stack([mine, message[:last].reshape(mine.shape)], axis=1)
            .reshape((lead,) + mine.shape[1:])
            .astype(jnp.float32)
            for mine, message in ((own, gather.message), (own_momentum, momenta.message))
        ]
        row = (jnp.arange(lead) ^ self.own) * rows
        here = ((row >= start) & (row < start + count))[:, None] & (jnp.arange(2 * rows) < rows)
        block = MOMENTUM_DECAY * momenta + factor * grads
        block = jnp.where((self.kind < 2) | here[..., None], block, 0.0).astype(jnp.bfloat16)
        result = orthogonalize(block.reshape(-1, D)).reshape(lead, 2 * rows, D)[:8:2]
        return (*result, sums[:2] * factor, norm, *new)

    def spread(self, result, masters):
        came = [result[0]]
        for flip in (1, 2, 3):
            came.append(exchange(result[flip], flip << 1, self.devices))
        rows = masters[0].shape[0]
        start, count = self.attn_span(True)
        row = self.own * rows
        large = (row >= start) & (row < start + count)
        attn_chip = jnp.where(large, 2, 3)
        if rows % 16 == 0:
            in_smem = pl.BlockSpec(memory_space=pltpu.SMEM)
            in_vmem = pl.BlockSpec(memory_space=pltpu.VMEM)
            return call(
                finish_kernel,
                tuple(shape_of(master.shape, jnp.float32) for master in masters),
                (jnp.stack([self.kind, attn_chip]), *came, *masters),
                0,
                16,
                in_specs=[in_smem] + [in_vmem] * 7,
                out_specs=(in_vmem,) * 3,
            )
        return [
            updated(master, from_chip(came, self.kind, chip, master.shape[0]), rate)
            for master, chip, rate in zip(masters, (attn_chip, 0, 1), step_rates())
        ]


class Gather:
    def __init__(self, owners, gate_up, down, attn, sums=None):
        self.owners, self.sums = owners, sums
        parts = (gate_up, attn, down)
        self.gate_up, self.attn, self.down = [part.astype(jnp.bfloat16)[None] for part in parts]

    def send(self, parts, flip):
        flat = [part.reshape(-1, D) for part in parts]
        few = [] if self.sums is None else [split_rows(self.sums)]
        other = exchange(jnp.concatenate(flat + few, axis=0), flip, self.owners.devices)
        came, start = [], 0
        for part, rows in zip(parts, flat):
            came.append(other[start : start + rows.shape[0]].reshape(part.shape))
            start += rows.shape[0]
        return came, joined_rows(other[start:]) if few else 0.0

    def add(self, few):
        if self.sums is not None:
            self.sums = sum(few, self.sums)

    def widen(self, group):
        top = 1 << self.owners.top_bit
        gate_up, attn, down, few = [self.gate_up], [self.attn], [self.down], []
        for flip in flips_of(group):
            if flip & top:
                (more,), rest = self.send([self.down], flip)
            else:
                came, rest = self.send([self.gate_up, self.attn, self.down], flip)
                gate_up.append(came[0])
                attn.append(came[1])
                more = came[2]
            down.append(more)
            few.append(rest)
        joined = [jnp.concatenate(blocks, axis=0) for blocks in (gate_up, attn, down)]
        self.gate_up, self.attn, self.down = joined
        self.add(few)

    def route(self):
        kind = self.owners.kind
        gate_up = self.gate_up
        down = self.down.reshape(gate_up.shape)
        attn = jnp.pad(self.attn, ((0, 0), (0, self.attn.shape[1]), (0, 0)))
        wanted = lambda owner: jnp.where(owner == 0, gate_up, jnp.where(owner == 1, down, attn))
        blocks, few = [wanted(kind)], []
        for flip in (1, 2, 3):
            (came,), rest = self.send([wanted(kind ^ flip)], flip << 1)
            blocks.append(came)
            few.append(rest)
        self.add(few)
        self.blocks = jnp.stack(blocks, axis=1)

    def join(self):
        few = [split_rows(self.sums)]
        message = jnp.concatenate([self.blocks.reshape(-1, D)] + few, axis=0)
        self.message = exchange(message, 1, self.owners.devices)

    def flat(self):
        return self.blocks.reshape((-1,) + self.blocks.shape[2:])


def per_device(
    inputs,
    out_grad,
    lang_tags,
    attn_master,
    gate_up_master,
    down_master,
    attn_momentum,
    gate_up_momentum,
    down_momentum,
    norm_gains,
    gain_first,
    gain_second,
):
    devices = lax.axis_size(("dp", "sub"))
    device_place = lax.axis_index(("dp", "sub"))
    q_rows = HEADS * HEAD_DIM
    kv_rows = KV_HEADS * HEAD_DIM
    qkv_rows = q_rows + 2 * kv_rows
    tag_hot = (lang_tags[:, None] == jnp.arange(NUM_TAGS, dtype=jnp.int32)[None, :]).astype(
        jnp.float32
    )
    masters = (attn_master, gate_up_master, down_master)
    attn_low = attn_master.astype(jnp.bfloat16)
    gate_up_low = gate_up_master.astype(jnp.bfloat16)
    down_low = down_master.astype(jnp.bfloat16)
    tag_row = jnp.pad(tag_hot[:1], ((0, 0), (0, D - NUM_TAGS)))
    ffn_low = jnp.concatenate([gate_up_low, down_low], axis=0)
    place = device_place
    groups = bit_groups(devices)
    ffn_blocks = lax.all_gather(ffn_low, AXES)
    owners = Owners(place, devices)
    momenta = Gather(owners, gate_up_momentum, down_momentum, attn_momentum, tag_row)
    early = (inputs.astype(jnp.float32), momenta.gate_up, momenta.attn, momenta.down)
    attn_blocks = gather_hop(attn_low[None], groups[-1], devices)
    attn_blocks, early = lax.optimization_barrier((attn_blocks, early))
    hidden_in, momenta.gate_up, momenta.attn, momenta.down = early
    for group in groups[-2:0:-1]:
        attn_blocks = gather_hop(attn_blocks, group, devices)
    for group in groups[2:]:
        momenta.widen(group)
    other_blocks = exchange(attn_blocks, 1, devices)
    momenta.route()
    attn_blocks, other_blocks, momenta.blocks, momenta.sums = lax.optimization_barrier(
        (attn_blocks, other_blocks, momenta.blocks, momenta.sums)
    )
    momenta.join()
    length = inputs.shape[0]
    wide_cos, wide_sin, tall_cos, tall_sin = [jnp.asarray(t) for t in rotary_rows(length)]
    low, single = jnp.bfloat16, jnp.float32
    spot = place[None, None]
    core = bit_of(place, 0)[None, None]
    in_smem = pl.BlockSpec(memory_space=pltpu.SMEM)
    in_vmem = pl.BlockSpec(memory_space=pltpu.VMEM)
    even = down_low.shape[0] % 16 == 0
    attn_outs = (
        shape_of((length, q_rows), low),
        shape_of((length, kv_rows), low),
        shape_of((length, kv_rows), low),
        shape_of((length, D), low),
        shape_of((length, q_rows), low),
        shape_of((HEADS, 1, length), single),
        shape_of((HEADS, 1, length), single),
        shape_of((length, D), single),
        shape_of((length, D), low),
    )
    if even:
        pieces = (attn_blocks, other_blocks)
        attn_outs += (shape_of((devices // 2, 2) + attn_low.shape, low),)
    else:
        whole_weights = in_order(jnp.stack([attn_blocks, other_blocks], 1).reshape(devices, -1), place)
        pieces = (whole_weights.reshape(16, 2, -1, D),)
    queries, keys, values, normed_one, attended_low, peaks, totals, residual, normed_two, *attn_w = call(
        attention_kernel if even else whole_attention_kernel,
        attn_outs,
        (spot, hidden_in, *pieces, norm_gains, wide_cos, wide_sin),
        2 * length * D * 3 * (qkv_rows + q_rows),
        58,
        in_specs=[in_smem] + [in_vmem] * (4 + len(pieces)),
        out_specs=(in_vmem,) * len(attn_outs),
        scratch=(pltpu.VMEM((HEADS + 2 * KV_HEADS, length, HEAD_DIM), low),),
    )
    attn_weights = attn_w[0] if even else pieces[0]
    tag_count = momenta.sums + joined_rows(momenta.message[-2:])
    tags = jnp.concatenate([tag_row, tag_count], axis=0)
    gate_up_rows, down_rows = gate_up_low.shape[0], down_low.shape[0]
    if even:
        weights = (ffn_blocks,)
        weight_specs = [pl.BlockSpec(memory_space=pl.ANY)]
    else:
        ffn_weights = ffn_blocks
        ffn_rows = gate_up_rows + down_rows
        gate_up_weights = ffn_weights[:, :gate_up_rows].reshape(32, -1, D)
        down_weights = ffn_weights[:, gate_up_rows:ffn_rows].reshape(32, -1, D)
        gate_up_rows, down_rows = gate_up_weights.shape[1], down_weights.shape[1]
        weights = (gate_up_weights, down_weights)
        weight_specs = [in_vmem] * 2
    chunk = 768 if even else 384
    steps = FF // chunk
    held_once = dict(pipeline_mode=pl.Buffered(1))
    whole = lambda *shape: pl.BlockSpec(shape, lambda c: (0,) * len(shape), **held_once)
    part = lambda rows: pl.BlockSpec((chunk // rows, rows, D), lambda c: (c, 0, 0))
    if even:
        cut = (gate_up_rows + down_rows) * 9 // 16 // 16 * 16
        other_cut = gate_up_rows + down_rows - cut
        pairs = devices // 2
        grad_outs = tuple(
            shape_of((pairs, size, D), low) for size in (cut, other_cut) for _ in range(2)
        )
        grad_specs = (pl.BlockSpec(memory_space=pl.ANY),) * len(grad_outs)
        lazy = lambda *shape: pl.BlockSpec(memory_space=pl.ANY)
        held_scratch = (
            pltpu.VMEM(ffn_blocks.shape, low),
            pltpu.VMEM((length, D), single),
            pltpu.VMEM((length, q_rows), low),
            pltpu.VMEM(attn_weights.shape, low),
            *[pltpu.VMEM(out.shape, out.dtype) for out in grad_outs],
            pltpu.SemaphoreType.DMA((7 + 3 * steps,)),
        )
    else:
        grad_outs = (
            shape_of((16, gate_up_rows, D), single),
            shape_of((16, gate_up_rows, D), single),
            shape_of((32, down_rows, D), single),
        )
        grad_specs = (part(gate_up_rows), part(gate_up_rows), part(down_rows))
        lazy, held_scratch = whole, ()
    outputs, residual_grad, attended_grad, o_part, gain_two, *ffn_grads = call(
        partial(
            feed_kernel,
            devices=devices,
            gathered=even,
            gate_rows=gate_up_rows,
            down_rows=down_rows,
        ),
        (
            shape_of((D, length), low),
            shape_of((length, D), single),
            shape_of((length, q_rows), low),
            shape_of((q_rows, D), single),
            shape_of((1, D), single),
            *grad_outs,
        ),
        (
            spot,
            tags,
            normed_two,
            residual,
            out_grad.T,
            attended_low,
            *weights,
            attn_weights,
            norm_gains,
        ),
        2 * 3 * length * D * (3 * FF + q_rows),
        58,
        grid=(steps,),
        in_specs=[
            in_smem,
            whole(2, D),
            whole(length, D),
            lazy(length, D),
            whole(D, length),
            lazy(length, q_rows),
            *weight_specs,
            lazy(*attn_weights.shape),
            whole(2, D),
        ],
        out_specs=(
            whole(D, length),
            whole(length, D),
            whole(length, q_rows),
            whole(q_rows, D),
            whole(1, D),
            *grad_specs,
        ),
        scratch=(
            pltpu.VMEM((length, D), single),
            pltpu.VMEM((length, D), single),
            pltpu.VMEM((length, D), low),
            pltpu.VMEM((3, length, chunk), low),
        )
        + held_scratch,
    )
    bits = range(devices.bit_length() - 1)
    if even:
        first_held, first_sent, second_held, second_sent = ffn_grads
        sums = [
            Sums(first_held, place, devices, bits[1:], [exchange(first_sent, 1, devices)]),
            Sums(second_held, place, devices, bits[1:], [exchange(second_sent, 1, devices)]),
        ]
    else:
        gate_up_part = jnp.concatenate([g.reshape(-1, D) for g in ffn_grads[:2]], axis=0)
        sums = [
            Sums(gate_up_part.reshape(devices, -1, D), place, devices, bits),
            Sums(ffn_grads[2].reshape(devices, -1, D), place, devices, bits),
        ]
        for s in sums:
            s.hop(0)
    head_outs = (
        shape_of((length, q_rows // KV_HEADS), low),
        shape_of((length, HEAD_DIM), low),
        shape_of((length, HEAD_DIM), low),
    )
    head_grads = []
    for heads in ((0,), (1, 2)):
        head_grads += call(
            partial(heads_kernel, heads),
            head_outs * len(heads),
            (queries, keys, values, attended_grad, peaks, totals, tall_cos, tall_sin),
            2 * 2 * length * length * q_rows * len(heads),
            58,
            scratch=(
                pltpu.VMEM((length, HEAD_DIM), single),
                pltpu.VMEM((length, HEAD_DIM), single),
            ),
        )
        if heads == (0,):
            attended_grad, head_grads = after((attended_grad, head_grads), sums)
            sums[0].hop(1)
            sums[1].hop(2)
    normed_one, head_grads = after((normed_one, head_grads), sums)
    proj_parts = [head_grads[3 * head + kind] for kind in range(3) for head in range(KV_HEADS)]
    sums[0].hop(2)
    sums[1].hop(1)
    if even:
        grad_outs = (
            shape_of((pairs, attn_low.shape[0], D), low),
            shape_of((pairs, attn_low.shape[0], D), low),
        )
    else:
        grad_outs = (shape_of((qkv_rows + q_rows, D), single),)
    joined, *attn_grads = call(
        qkv_kernel,
        (shape_of((length, qkv_rows), low), *grad_outs),
        (core, *proj_parts, normed_one, o_part),
        2 * length * D * qkv_rows,
        58,
        in_specs=[in_smem] + [in_vmem] * 11,
        out_specs=(in_vmem,) * (1 + len(grad_outs)),
    )
    joined, attn_grads = after((joined, attn_grads), sums)
    if even:
        held, sent = attn_grads
        late = Sums(held, place, devices, bits[1:], [exchange(sent, 1, devices)])
    else:
        late = Sums(attn_grads[0].reshape(devices, -1, D), place, devices, bits)
        late.hop(0)
    feed_rows = [s.shape[0] for s in sums]
    feed_sums = Sums(
        jnp.concatenate([s.total() for s in sums], axis=1), place, devices, bits[3:]
    )
    feed_sums.hop(*groups[2])
    residual_grad = after(residual_grad, [late])
    late.hop(*groups[1])
    input_grad, gain_one = call(
        input_kernel,
        (shape_of((D, length), low), shape_of((1, D), single)),
        (joined, attn_weights, hidden_in, residual_grad, norm_gains),
        2 * length * D * qkv_rows,
        58,
    )
    input_grad = after(input_grad, [late, feed_sums])
    for group in groups[3:]:
        feed_sums.hop(*group)
    feed_total = feed_sums.total()[0]
    if even:
        gate_up_sum = feed_total[:gate_up_rows]
        down_sum = feed_total[gate_up_rows:]
    else:
        gate_up_sum, down_sum = feed_total[: feed_rows[0]], feed_total[feed_rows[0] :]
    for group in groups[2:]:
        late.hop(*group)
    attn_sum = late.total()[0]
    squares = sum(
        jnp.sum(part * part, axis=0, keepdims=True) for part in (attn_sum, gate_up_sum, down_sum)
    )
    small_sums = jnp.concatenate([gain_one, gain_two, squares], axis=0)
    gather = Gather(owners, gate_up_sum, down_sum, attn_sum, small_sums)
    for group in groups[2:]:
        gather.widen(group)
    gather.route()
    gather.join()
    param_count = (qkv_rows + q_rows + 3 * FF) * D + 2 * D
    limit = CLIP_SCALE * math.sqrt(devices * length * param_count)
    down_count = down_low.shape[0]
    parts = (attn_sum, gate_up_sum, down_sum, attn_momentum, gate_up_momentum, down_momentum)
    solved = owners.solve(gather, momenta, parts, limit, down_count)
    solved, (gain_grad, grad_norm, *new) = solved[:4], solved[4:]
    attn_grad, gate_up_grad, down_grad, attn_moment, gate_up_moment, down_moment = new
    grad_norm = grad_norm[0, 0]
    new_masters = owners.spread(solved, masters)
    first_new = BETA_FIRST * gain_first + (1.0 - BETA_FIRST) * gain_grad
    second_new = BETA_SECOND * gain_second + (1.0 - BETA_SECOND) * gain_grad * gain_grad
    gains_new = norm_gains - GAIN_RATE * (first_new / (1.0 - BETA_FIRST**STEP_NUMBER)) / (
        jnp.sqrt(second_new / (1.0 - BETA_SECOND**STEP_NUMBER)) + ADAM_EPS
    )
    return (
        outputs.T,
        input_grad.T,
        attn_grad,
        gate_up_grad,
        down_grad,
        grad_norm,
        attn_moment,
        gate_up_moment,
        down_moment,
        new_masters[0],
        new_masters[1],
        new_masters[2],
        gain_grad,
        first_new,
        second_new,
        gains_new,
    )


def solution(mesh):
    placed = (
        P(("dp", "sub"), None),
        P(("dp", "sub"), None),
        P(("dp", "sub")),
        P(("dp", "sub"), None),
        P(("dp", "sub"), None),
        P(("dp", "sub"), None),
        P(("dp", "sub"), None),
        P(("dp", "sub"), None),
        P(("dp", "sub"), None),
        P(),
        P(),
        P(),
    )
    return jax.shard_map(
        per_device,
        mesh=mesh,
        in_specs=placed,
        out_specs=(
            P(("dp", "sub"), None),
            P(("dp", "sub"), None),
            P(("dp", "sub"), None),
            P(("dp", "sub"), None),
            P(("dp", "sub"), None),
            P(),
            P(("dp", "sub"), None),
            P(("dp", "sub"), None),
            P(("dp", "sub"), None),
            P(("dp", "sub"), None),
            P(("dp", "sub"), None),
            P(("dp", "sub"), None),
            P(),
            P(),
            P(),
            P(),
        ),
        check_vma=False,
    )
```

```python
from functools import partial
import math

import jax
import jax.numpy as jnp
import numpy as np
from jax import lax
from jax.experimental import pallas as pl
from jax.experimental.pallas import tpu as pltpu
from jax.sharding import PartitionSpec as P

D = 576
HEADS = 9
KV_HEADS = 3
HEAD_DIM = 64
FF = 1536
NUM_TAGS = 8
ORTHO_STEPS = 5
STEP_NUMBER = 10


NORM_EPS = 1e-05
ROPE_BASE = 100000.0
POLY_ONE = 3.4445
POLY_TWO = -4.775
POLY_THREE = 2.0315
MOMENTUM_DECAY = 0.95
MATRIX_RATE = 0.2
MATRIX_DECAY = 0.1
GAIN_RATE = 1.0
BETA_FIRST = 0.9
BETA_SECOND = 0.95
ADAM_EPS = 1e-08
CLIP_SCALE = 0.002


AXES = ("dp", "sub")


def bit_of(place, bit):
    return (place >> bit) & 1


def exchange(array, flip, devices, source=None):
    pairs = [(i, i ^ flip) for i in range(devices) if source is None or source(i)]
    return lax.ppermute(array, AXES, pairs)


def bit_groups(devices):
    bits = devices.bit_length() - 1
    return [(0,)] + [tuple(range(bit, min(bit + 2, bits))) for bit in range(1, bits, 2)]


def flips_of(group):
    return [part << group[0] for part in range(1, 1 << len(group))]


def pick(array, axis, index):
    return lax.dynamic_index_in_dim(array, index, axis, keepdims=False)


def gather_hop(blocks, group, devices, front=False, source=None):
    came = [exchange(blocks, flip, devices, source) for flip in flips_of(group)]
    stacked = jnp.stack([blocks] + came, axis=0 if front else 1)
    return stacked.reshape((-1,) + blocks.shape[1:])


def in_order(blocks, place):
    return jnp.take(blocks, jnp.arange(blocks.shape[0]) ^ place, axis=0)


class Sums:
    def __init__(self, held, place, devices, bits, came=()):
        self.place, self.devices, self.bits = place, devices, list(bits)
        self.shape = held.shape[-2:]
        self.held, self.came = held, list(came)

    def hop(self, *group):
        low, width = self.bits.index(group[0]), len(group)
        high = len(self.bits) - low - width
        terms = [
            term.reshape((1 << high, 1 << width, 1 << low) + self.shape)
            for term in [self.held] + self.came
        ]
        mine = (self.place >> group[0]) & ((1 << width) - 1)

        def part(index):
            chosen = [pick(term, 1, index).astype(jnp.float32) for term in terms]
            return sum(chosen[1:], chosen[0]).reshape((-1,) + self.shape)

        sent = [part(mine ^ flip).astype(jnp.bfloat16) for flip in range(1, 1 << width)]
        self.held = part(mine)
        self.came = [exchange(s, f, self.devices) for s, f in zip(sent, flips_of(group))]
        for bit in group:
            self.bits.remove(bit)

    def total(self):
        return sum([term.astype(jnp.float32) for term in [self.held] + self.came])


def after(value, sums):
    value, came = lax.optimization_barrier((value, [s.came for s in sums]))
    for s, c in zip(sums, came):
        s.came = c
    return value


SCORE_SCALE = HEAD_DIM ** (-0.5)
MASKED = -1e30


def product(left, right, left_dim, right_dim):
    return lax.dot_general(
        left, right, (((left_dim,), (right_dim,)), ((), ())), preferred_element_type=jnp.float32
    )


def call(kernel, outs, args, flops, mib, grid=(), in_specs=None, out_specs=None, scratch=()):
    specs = {} if in_specs is None else dict(in_specs=in_specs, out_specs=out_specs)
    listed = tuple(outs) if isinstance(outs, (tuple, list)) else (outs,)
    moved = sum(math.prod(a.shape) * a.dtype.itemsize for a in tuple(args) + listed)
    return pl.pallas_call(
        kernel,
        out_shape=outs,
        grid=grid,
        scratch_shapes=scratch,
        compiler_params=pltpu.CompilerParams(vmem_limit_bytes=mib * 2**20),
        cost_estimate=pl.CostEstimate(flops=int(flops), bytes_accessed=moved, transcendentals=0),
        **specs,
    )(*args)


def shape_of(shape, dtype):
    return jax.ShapeDtypeStruct(shape, dtype)


def rotary_rows(length):
    half_dim = HEAD_DIM // 2
    frequency = np.float32(ROPE_BASE) ** (
        -(np.arange(half_dim, dtype=np.float32) * np.float32(2.0 / HEAD_DIM))
    )
    angles = np.arange(length, dtype=np.float32)[:, None] * frequency[None, :].astype(np.float32)
    cosine, sine = np.cos(angles), np.sin(angles)
    wide_cosine = np.concatenate([cosine] * 4, axis=1)
    wide_sine = np.concatenate([-sine, sine, -sine, sine], axis=1)
    return wide_cosine, wide_sine, cosine.T.copy(), sine.T.copy()


def causal_mask(size):
    key_pos = lax.broadcasted_iota(jnp.int32, (size, size), 0)
    query_pos = lax.broadcasted_iota(jnp.int32, (size, size), 1)
    return key_pos <= query_pos


def scores_by_key(keys, queries, mask):
    size = queries.shape[0]
    before = keys.shape[0] - size
    raw = product(keys, queries, 1, 1)
    last = jnp.where(mask, raw[before:], MASKED)
    return last if before == 0 else jnp.concatenate([raw[:before], last], axis=0)


def scaled_norm(values, gain):
    inverse = lax.rsqrt(jnp.mean(values * values, axis=-1, keepdims=True) + NORM_EPS)
    return values * inverse * gain, inverse


def attention_kernel(
    place_ref, x_ref, own_ref, other_ref, gain_ref, cos_ref, sin_ref,
    q_ref, k_ref, v_ref, normed_ref, low_ref, peak_ref, total_ref, res_ref, two_ref, joined_ref,
    heads_ref,
):
    length = x_ref.shape[0]
    q_rows = HEADS * HEAD_DIM
    kv_rows = KV_HEADS * HEAD_DIM
    turned = q_rows + kv_rows
    if other_ref is None:
        w_ref = own_ref
    else:
        core, pair = place_ref[0, 0] & 1, place_ref[0, 0] >> 1
        for index in range(own_ref.shape[0]):
            joined_ref[index ^ pair, core] = own_ref[index]
            joined_ref[index ^ pair, 1 - core] = other_ref[index]
        w_ref = joined_ref
    weights = w_ref[...].reshape(-1, D)
    size = min(256, length)
    lane = lax.broadcasted_iota(jnp.int32, (size, turned), 1)
    first = lane % HEAD_DIM < HEAD_DIM // 2
    for start in range(0, length, size):
        rows = slice(start, start + size)
        normed = scaled_norm(x_ref[rows], gain_ref[0:1])[0].astype(jnp.bfloat16)
        normed_ref[rows] = normed
        raw = product(normed, weights[: turned + kv_rows], 1, 1)
        both = raw[:, :turned]
        swapped = jnp.where(
            first,
            pltpu.roll(both, turned - HEAD_DIM // 2, 1),
            pltpu.roll(both, HEAD_DIM // 2, 1),
        )
        cosine = jnp.concatenate([cos_ref[rows]] * (turned // 128), axis=1)
        sine = jnp.concatenate([sin_ref[rows]] * (turned // 128), axis=1)
        both = both * cosine + swapped * sine
        q_ref[rows] = both[:, :q_rows].astype(jnp.bfloat16)
        k_ref[rows] = both[:, q_rows:].astype(jnp.bfloat16)
        v_ref[rows] = raw[:, turned:].astype(jnp.bfloat16)
    size = min(512, length)
    mask = causal_mask(size)
    group = HEADS // KV_HEADS
    span = lambda head: slice(head * HEAD_DIM, (head + 1) * HEAD_DIM)
    for head in range(HEADS):
        heads_ref[head] = q_ref[:, span(head)] * jnp.bfloat16(SCORE_SCALE)
    for head in range(KV_HEADS):
        heads_ref[HEADS + head] = k_ref[:, span(head)]
        heads_ref[HEADS + KV_HEADS + head] = v_ref[:, span(head)]

    def attend(head, carry):
        keys_at = HEADS + head // group
        for start in range(0, length, size):
            end = start + size
            queries = heads_ref[head, start:end]
            scores = scores_by_key(heads_ref[keys_at, :end], queries, mask)
            peak = jnp.max(scores, axis=0, keepdims=True)
            shifted = jnp.exp(scores - peak)
            inverse = 1.0 / jnp.sum(shifted, axis=0, keepdims=True)
            prob_low = (shifted * inverse).astype(jnp.bfloat16)
            out = product(heads_ref[keys_at + KV_HEADS, :end], prob_low, 0, 0)
            heads_ref[head, start:end] = out.T.astype(jnp.bfloat16)
            peak_ref[head, :, start:end] = peak
            total_ref[head, :, start:end] = inverse
        return carry

    lax.fori_loop(0, HEADS, attend, 0)
    low_ref[...] = jnp.concatenate([heads_ref[head] for head in range(HEADS)], axis=1)
    size = min(256, length)
    for start in range(0, length, size):
        rows = slice(start, start + size)
        residual = x_ref[rows] + product(low_ref[rows], weights[turned + kv_rows :], 1, 0)
        res_ref[rows] = residual
        two_ref[rows] = scaled_norm(residual, gain_ref[1:2])[0].astype(jnp.bfloat16)


def whole_attention_kernel(place_ref, x_ref, own_ref, *refs):
    attention_kernel(place_ref, x_ref, own_ref, None, *refs[:-1], None, refs[-1])


def feed_kernel(
    place_ref, tags_ref, two_ref, res_ref, grad_ref, low_ref, *refs,
    devices, gathered, gate_rows, down_rows,
):
    cut = 1 if gathered else 2
    weight_refs, refs = refs[:cut], refs[cut:]
    attn_ref, gain_ref, out_ref, back_ref, att_ref, do_ref, dgain_ref, *refs = refs
    if gathered:
        *refs, sems = refs
        out_any, back_any = out_ref, back_ref
        out_ref, back_ref = refs[-2:]
        refs, held_refs, grad_refs = refs[:-10], refs[-10:-6], refs[-6:-2]
        *grad_outs, sum_ref, inner_ref, coming_ref, hidden_ref = refs
    else:
        *grad_refs, sum_ref, inner_ref, coming_ref, hidden_ref = refs
    step = pl.program_id(0)
    length = two_ref.shape[0]
    size = min(256, length)
    core = place_ref[0, 0] & 1
    chunk = hidden_ref.shape[2]
    gate_blocks, down_blocks = chunk // gate_rows, chunk // down_rows
    count = jnp.sum(tags_ref[0:1] * tags_ref[1:2], axis=1, keepdims=True)
    weight = devices / (NUM_TAGS * count)
    if gathered:
        weights_ref, res_held, low_held, attn_held = held_refs
        later = [
            pltpu.make_async_copy(source, target, sems.at[at])
            for at, (source, target) in enumerate(
                ((res_ref, res_held), (low_ref, low_held), (attn_ref, attn_held))
            )
        ]
        leaving = [
            pltpu.make_async_copy(source, target, sems.at[3 + at])
            for at, (source, target) in enumerate(zip(grad_refs, grad_outs))
        ]

        results = [
            pltpu.make_async_copy(out_ref, out_any, sems.at[sems.shape[0] - 2]),
            pltpu.make_async_copy(back_ref, back_any, sems.at[sems.shape[0] - 1]),
        ]

        def weight_copies(part):
            gates = pl.ds(part * gate_blocks, gate_blocks)
            ups = pl.ds(FF // gate_rows + part * gate_blocks, gate_blocks)
            downs = pl.ds(part * down_blocks, down_blocks)
            upper, lower = pl.ds(0, gate_rows), pl.ds(gate_rows, down_rows)
            return [
                pltpu.make_async_copy(
                    weight_refs[0].at[spot, rows],
                    weights_ref.at[spot, rows],
                    sems.at[7 + 3 * part + at],
                )
                for at, (spot, rows) in enumerate(((gates, upper), (ups, upper), (downs, lower)))
            ]

        @pl.when(step == 0)
        def _():
            for part in range(FF // chunk):
                for copy in weight_copies(part):
                    copy.start()
            for copy in later:
                copy.start()

        res_ref, low_ref, attn_ref = res_held, low_held, attn_held
        gate_ref, down_ref, first_row = weights_ref, weights_ref, gate_rows
    else:
        (gate_ref, down_ref), first_row = weight_refs, 0
    @pl.when(step == 0)
    def _():
        for start in range(0, length, size):
            rows = slice(start, start + size)
            grad = grad_ref[:, rows].astype(jnp.float32).T
            coming_ref[rows] = (grad * weight).astype(jnp.bfloat16)
        sum_ref[...] = jnp.zeros_like(sum_ref)
        inner_ref[...] = jnp.zeros_like(inner_ref)

    if gathered:
        for part in range(FF // chunk):

            @pl.when(step == part)
            def _(part=part):
                for copy in weight_copies(part):
                    copy.wait()

    gate_spots = pl.ds(step * gate_blocks, gate_blocks)
    up_spots = pl.ds(FF // gate_rows + step * gate_blocks, gate_blocks)
    gate_w = gate_ref[gate_spots, :gate_rows].reshape(-1, D)
    up_w = gate_ref[up_spots, :gate_rows].reshape(-1, D)
    down_spots = pl.ds(step * down_blocks, down_blocks)
    down_w = down_ref[down_spots, first_row : first_row + down_rows].reshape(-1, D)

    tile = min(512, length)

    def feed_tile(index, carry):
        rows = pl.ds(pl.multiple_of(index * tile, tile), tile)
        two = two_ref[rows]
        gate = product(two, gate_w, 1, 1)
        up = product(two, up_w, 1, 1)
        sigmoid = 0.5 * jnp.tanh(0.5 * gate) + 0.5
        silu = gate * sigmoid
        activation = (silu * up).astype(jnp.bfloat16)
        act_grad = product(coming_ref[rows], down_w, 1, 1)
        gate_low = act_grad * up * (sigmoid * (1.0 + gate * (1.0 - sigmoid)))
        gate_low = gate_low.astype(jnp.bfloat16)
        up_low = (act_grad * silu).astype(jnp.bfloat16)
        sum_ref[rows] += product(activation, down_w, 1, 0)
        inner_ref[rows] += product(gate_low, gate_w, 1, 0) + product(up_low, up_w, 1, 0)
        for kind, value in enumerate((gate_low, up_low, activation)):
            hidden_ref[kind, rows] = value
        return carry

    lax.fori_loop(0, length // tile, feed_tile, 0)
    gate_grad = product(two_ref[...], hidden_ref[0], 0, 0).T
    up_grad = product(two_ref[...], hidden_ref[1], 0, 0).T
    down_grad = product(coming_ref[...], hidden_ref[2], 0, 0).T
    if len(grad_refs) == 3:
        for ref, grad in zip(grad_refs, (gate_grad, up_grad, down_grad)):
            ref[...] = grad.reshape(ref.shape)
    else:
        first_held, first_sent, second_held, second_sent = grad_refs
        cut = first_held.shape[1]
        pairs = first_held.shape[0]
        for kind, grad in enumerate((gate_grad, up_grad, down_grad)):
            blocks, rows = (down_blocks, down_rows) if kind == 2 else (gate_blocks, gate_rows)
            grad = grad.reshape(blocks // 2, 2, rows, D)
            kept = jnp.where(core == 0, grad[:, 0], grad[:, 1]).astype(jnp.bfloat16)
            sent = jnp.where(core == 0, grad[:, 1], grad[:, 0]).astype(jnp.bfloat16)
            start = step * (blocks // 2) + (pairs // 2 if kind == 1 else 0)
            spot = pl.ds(start, blocks // 2)
            if kind == 2:
                second_held[spot, gate_rows - cut :, :] = kept
                second_sent[spot, gate_rows - cut :, :] = sent
            else:
                first_held[spot] = kept[:, :cut]
                first_sent[spot] = sent[:, :cut]
                second_held[spot, : rows - cut, :] = kept[:, cut:]
                second_sent[spot, : rows - cut, :] = sent[:, cut:]

    @pl.when(step == pl.num_programs(0) - 1)
    def _():
        if gathered:
            for copy in leaving:
                copy.start()
            for copy in later:
                copy.wait()
        o_w = attn_ref[-(attn_ref.shape[0] * HEADS // (2 * (HEADS + KV_HEADS))) :].reshape(-1, D)
        dgain_ref[...] = jnp.zeros_like(dgain_ref)
        for start in range(0, length, size):
            rows = slice(start, start + size)
            residual = res_ref[rows]
            out_ref[:, rows] = (residual + sum_ref[rows]).T.astype(jnp.bfloat16)
            inner = inner_ref[rows]
            inverse = scaled_norm(residual, 1.0)[1]
            scaled = inner * gain_ref[1:2]
            dgain_ref[...] += jnp.sum(inner * residual * inverse, axis=0, keepdims=True)
            back = (
                grad_ref[:, rows].astype(jnp.float32).T * weight
                + inverse * scaled
                - residual
                * (inverse * inverse * inverse)
                * jnp.mean(scaled * residual, axis=-1, keepdims=True)
            )
            back_ref[rows] = back
            coming_ref[rows] = back.astype(jnp.bfloat16)
        if gathered:
            for copy in results:
                copy.start()
        do_ref[...] = product(low_ref[...], coming_ref[...], 0, 0)
        att_ref[...] = product(coming_ref[...], o_w, 1, 1).astype(jnp.bfloat16)
        if gathered:
            for copy in leaving + results:
                copy.wait()


def heads_kernel(heads, *refs):
    outs = refs[8:-2]
    for index, head in enumerate(heads):
        head_kernel(head, *refs[:8], *outs[3 * index : 3 * index + 3], *refs[-2:])


def head_kernel(
    head, q_ref, k_ref, v_ref, grad_ref, peak_ref, total_ref, cos_ref, sin_ref,
    dq_ref, dk_ref, dv_ref, key_sum, value_sum,
):
    length = q_ref.shape[0]
    size = min(256, length)
    half_dim = HEAD_DIM // 2
    mask = causal_mask(size)
    group = HEADS // KV_HEADS
    shared = slice(head * HEAD_DIM, (head + 1) * HEAD_DIM)
    key_sum[...] = jnp.zeros_like(key_sum)
    value_sum[...] = jnp.zeros_like(value_sum)

    def turn_back(grad, columns):
        first, second = grad[:half_dim], grad[half_dim:]
        cosine, sine = cos_ref[:, columns], sin_ref[:, columns]
        turned = [first * cosine + second * sine, second * cosine - first * sine]
        return jnp.concatenate(turned, axis=0).T

    for member in range(group):
        row = head * group + member
        place = slice(row * HEAD_DIM, (row + 1) * HEAD_DIM)
        for start in range(0, length, size):
            end = start + size
            queries = q_ref[start:end, place] * jnp.bfloat16(SCORE_SCALE)
            grad = grad_ref[start:end, place]
            keys, values = k_ref[:end, shared], v_ref[:end, shared]
            scores = scores_by_key(keys, queries, mask)
            probs = (
                jnp.exp(scores - peak_ref[row, :, start:end])
                * total_ref[row, :, start:end]
            )
            moved = probs * product(values, grad, 1, 1)
            score_grad = (moved - probs * jnp.sum(moved, axis=0, keepdims=True)).astype(
                jnp.bfloat16
            )
            value_sum[:end] += product(probs.astype(jnp.bfloat16), grad, 1, 0)
            key_sum[:end] += product(score_grad, queries, 1, 0)
            back = turn_back(product(keys, score_grad, 0, 0) * SCORE_SCALE, slice(start, end))
            dq_ref[start:end, member * HEAD_DIM : (member + 1) * HEAD_DIM] = back.astype(
                jnp.bfloat16
            )
    dk_ref[...] = turn_back(key_sum[...].T, slice(0, length)).astype(jnp.bfloat16)
    dv_ref[...] = value_sum[...].astype(jnp.bfloat16)


def qkv_kernel(core_ref, *refs):
    parts, (normed_ref, o_ref, joined_ref), out_refs = refs[:9], refs[9:12], refs[12:]
    start = 0
    for part in parts:
        joined_ref[:, start : start + part.shape[1]] = part[...]
        start += part.shape[1]
    grad = product(joined_ref[...], normed_ref[...], 0, 0)
    if len(out_refs) == 1:
        out_refs[0][:start] = grad
        out_refs[0][start:] = o_ref[...]
        return
    held_ref, sent_ref = out_refs
    rows = held_ref.shape[1]
    spot = 0
    for value in (grad, o_ref[...]):
        value = value.reshape(-1, 2, rows, D)
        end = spot + value.shape[0]
        held = jnp.where(core_ref[0, 0] == 0, value[:, 0], value[:, 1])
        held_ref[spot:end] = held.astype(jnp.bfloat16)
        sent = jnp.where(core_ref[0, 0] == 0, value[:, 1], value[:, 0])
        sent_ref[spot:end] = sent.astype(jnp.bfloat16)
        spot = end


def input_kernel(joined_ref, w_ref, x_ref, back_ref, gain_ref, out_ref, dgain_ref):
    length = x_ref.shape[0]
    size = min(256, length)
    count = joined_ref.shape[1]
    weights = w_ref[...].reshape(-1, D)[:count]
    dgain_ref[...] = jnp.zeros_like(dgain_ref)
    for start in range(0, length, size):
        rows = slice(start, start + size)
        inner = product(joined_ref[rows], weights, 1, 0)
        hidden = x_ref[rows]
        inverse = scaled_norm(hidden, 1.0)[1]
        scaled = inner * gain_ref[0:1]
        dgain_ref[...] += jnp.sum(inner * hidden * inverse, axis=0, keepdims=True)
        grad = (
            back_ref[rows]
            + inverse * scaled
            - hidden
            * (inverse * inverse * inverse)
            * jnp.mean(scaled * hidden, axis=-1, keepdims=True)
        )
        out_ref[:, rows] = grad.T.astype(jnp.bfloat16)


def symmetric_product(left, right, left_dim):
    size = right.shape[1]
    cut = size // 256 * 256
    if cut == 0 or cut == size or left_dim == 1 and left.shape[0] != size:
        return product(left, right, left_dim, 0)
    first = product(left, right[:, :cut], left_dim, 0)
    rest = left[:, cut:] if left_dim == 0 else left[cut:]
    corner = product(rest, right[:, cut:], left_dim, 0)
    second = jnp.concatenate([first[cut:].T, corner], axis=0)
    return jnp.concatenate([first, second], axis=1)


def ortho_sweeps(block, held_ref):
    size = min(block.shape)
    left = block.shape[0] < block.shape[1]
    block = block.astype(jnp.float32)
    held_ref[...] = block * (1.0 / (jnp.sqrt(jnp.sum(block * block)) + 1e-07))
    row = lax.broadcasted_iota(jnp.int32, (size, size), 0)
    diagonal = row == lax.broadcasted_iota(jnp.int32, (size, size), 1)

    def sweep(index, carry):
        held = held_ref[...]
        scaled = held.astype(jnp.bfloat16)
        gram = product(scaled, scaled, 1, 1) if left else symmetric_product(scaled, scaled, 0)
        mean = jnp.sum(jnp.where(diagonal, gram, 0.0)) / size
        rest = jnp.where(diagonal, gram - mean, gram)
        rest_low = rest.astype(jnp.bfloat16)
        square = symmetric_product(rest_low, rest_low, 1)
        poly = (POLY_TWO + 2.0 * POLY_THREE * mean) * rest + POLY_THREE * square
        poly_low = poly.astype(jnp.bfloat16)
        turned = product(poly_low, scaled, 1, 0) if left else product(scaled, poly_low, 1, 0)
        held_ref[...] = (POLY_ONE + POLY_TWO * mean + POLY_THREE * mean * mean) * held + turned
        return carry

    lax.fori_loop(0, ORTHO_STEPS, sweep, 0)
    return held_ref[...].astype(jnp.bfloat16)


def ortho_kernel(block_ref, out_ref, held_ref):
    out_ref[...] = ortho_sweeps(block_ref[...], held_ref)


def clip_factor(sums, limit):
    gains = sums[:2]
    squares = jnp.sum(gains * gains, axis=0, keepdims=True) + sums[2:3]
    norm = jnp.sqrt(jnp.sum(squares, axis=1, keepdims=True))
    return norm, jnp.minimum(1.0, limit / norm)


def solve_kernel(
    spot_ref, own_sums_ref, own_ref, other_ref, own_momentum, other_momentum, *refs, limit
):
    parts, out_refs, (gain_ref, norm_ref), refs = refs[:6], refs[6:10], refs[10:12], refs[12:]
    new_refs, (block_ref, held_ref) = refs[:6], refs[6:]
    kind, place, start, count = [spot_ref[i] for i in range(4)]
    lead, size = block_ref.shape[:2]
    rows = size // 2
    last = lead // 2 * size
    sums = own_sums_ref[...] + joined_rows(other_ref[last:])
    norm, factor = clip_factor(sums, limit)
    norm_ref[...] = norm
    gain_ref[...] = sums[:2] * factor
    for part in range(3):
        grad = parts[part][...] * factor
        new_refs[part][...] = grad
        new_refs[3 + part][...] = MOMENTUM_DECAY * parts[3 + part][...] + grad
    for index in range(lead):
        spot = slice(index // 2 * size, (index // 2 + 1) * size)
        if index % 2:
            momentum, grad = other_momentum[spot], other_ref[spot]
        else:
            momentum, grad = own_momentum[index // 2], own_ref[index // 2]
        mixed = MOMENTUM_DECAY * momentum.astype(jnp.float32) + factor * grad.astype(jnp.float32)
        row = ((place & (lead - 1)) ^ index) * rows
        here = (kind < 2) | ((row >= start) & (row < start + count))
        block_ref[index, :rows] = jnp.where(here, mixed[:rows], 0.0).astype(jnp.bfloat16)
        block_ref[index, rows:] = jnp.where(kind < 2, mixed[rows:], 0.0).astype(jnp.bfloat16)
    done = ortho_sweeps(block_ref[...].reshape(lead * size, D), held_ref)
    block_ref[...] = done.reshape(lead, size, D)
    for flip in range(4):
        out_refs[flip][...] = block_ref[2 * flip]


def solve(spots, sums, own, other, own_momentum, other_momentum, parts, limit):
    half, size = own.shape[:2]
    in_vmem = pl.BlockSpec(memory_space=pltpu.VMEM)
    in_smem = pl.BlockSpec(memory_space=pltpu.SMEM)
    outs = (shape_of((size, D), jnp.bfloat16),) * 4
    outs += (shape_of((2, D), jnp.float32), shape_of((1, 1), jnp.float32))
    outs += tuple(shape_of(part.shape, jnp.float32) for part in parts)
    return pl.pallas_call(
        partial(solve_kernel, limit=limit),
        out_shape=outs,
        in_specs=[in_smem] + [in_vmem] * 11,
        out_specs=(in_vmem,) * len(outs),
        scratch_shapes=[
            pltpu.VMEM((2 * half, size, D), jnp.bfloat16),
            pltpu.VMEM((2 * half * size, D), jnp.float32),
        ],
        compiler_params=pltpu.CompilerParams(vmem_limit_bytes=58 * 2**20),
    )(spots, sums, own, other, own_momentum, other_momentum, *parts)


def orthogonalize(block):
    rows, columns = block.shape
    small, large = min(block.shape), max(block.shape)
    return call(
        ortho_kernel,
        shape_of(block.shape, jnp.bfloat16),
        (block,),
        2 * ORTHO_STEPS * small * small * (2 * large + small),
        32,
        scratch=(pltpu.VMEM((rows, columns), jnp.float32),),
    )


def block_list():
    q_rows = HEADS * HEAD_DIM
    kv_rows = KV_HEADS * HEAD_DIM
    return (
        (0, 0, q_rows),
        (0, q_rows, kv_rows),
        (0, q_rows + kv_rows, kv_rows),
        (0, q_rows + 2 * kv_rows, q_rows),
        (1, 0, FF),
        (1, FF, FF),
        (2, 0, FF),
    )


def step_rates():
    rates = [set(), set(), set()]
    for owner_id, _, row_count in block_list():
        rates[owner_id].add(0.2 * math.sqrt(max(row_count, D)))
    return [rate for (rate,) in rates]


def from_chip(came, kind, chip, rows):
    found = came[0][:rows].astype(jnp.float32)
    for flip in (1, 2, 3):
        found = jnp.where(kind ^ flip == chip, came[flip][:rows].astype(jnp.float32), found)
    return found


def updated(master, rows, rate):
    return master - MATRIX_RATE * (rate * rows + MATRIX_DECAY * master)


def finish_kernel(spot_ref, *refs):
    came, masters, outs = refs[:4], refs[4:7], refs[7:]
    chips = (spot_ref[1], 0, 1)
    for master, out, chip, rate in zip(masters, outs, chips, step_rates()):
        rows = from_chip(came, spot_ref[0], chip, master.shape[0])
        out[...] = updated(master[...], rows, rate)


def split_rows(value):
    high = lax.reduce_precision(value, 8, 7)
    return jnp.concatenate([high.astype(jnp.bfloat16), (value - high).astype(jnp.bfloat16)], axis=0)


def joined_rows(rows):
    half = rows.shape[0] // 2
    return rows[:half].astype(jnp.float32) + rows[half:].astype(jnp.float32)


class Owners:
    def __init__(self, place, devices):
        self.place, self.devices = place, devices
        self.top_bit = devices.bit_length() - 2
        self.core, self.across, self.along = [bit_of(place, bit) for bit in range(3)]
        self.kind = 2 * self.along + self.across
        self.top = bit_of(place, self.top_bit)
        self.own = place & (devices // 2 - 1)

    def attn_span(self, large):
        q_rows, kv_rows = HEADS * HEAD_DIM, KV_HEADS * HEAD_DIM
        large_start = jnp.where(self.top == 0, 0, kv_rows)
        small_start = jnp.where(self.top == 0, q_rows, 0)
        return jnp.where(large, large_start, small_start), jnp.where(large, q_rows, kv_rows)

    def solve(self, gather, momenta, parts, limit, rows):
        lead = self.devices // 2
        start, count = self.attn_span(self.kind == 2)
        own, own_momentum = gather.flat(), momenta.flat()
        if rows % 16 == 0:
            spots = jnp.stack([self.kind, self.place, start, count])
            return solve(
                spots, gather.sums, own, gather.message, own_momentum, momenta.message, parts, limit
            )
        last = lead // 2 * 2 * rows
        sums = gather.sums + joined_rows(gather.message[last:])
        norm, factor = clip_factor(sums, limit)
        new = [part * factor for part in parts[:3]]
        new += [MOMENTUM_DECAY * part + grad for part, grad in zip(parts[3:], new)]
        grads, momenta = [
            jnp.stack([mine, message[:last].reshape(mine.shape)], axis=1)
            .reshape((lead,) + mine.shape[1:])
            .astype(jnp.float32)
            for mine, message in ((own, gather.message), (own_momentum, momenta.message))
        ]
        row = (jnp.arange(lead) ^ self.own) * rows
        here = ((row >= start) & (row < start + count))[:, None] & (jnp.arange(2 * rows) < rows)
        block = MOMENTUM_DECAY * momenta + factor * grads
        block = jnp.where((self.kind < 2) | here[..., None], block, 0.0).astype(jnp.bfloat16)
        result = orthogonalize(block.reshape(-1, D)).reshape(lead, 2 * rows, D)[:8:2]
        return (*result, sums[:2] * factor, norm, *new)

    def spread(self, result, masters):
        came = [result[0]]
        for flip in (1, 2, 3):
            came.append(exchange(result[flip], flip << 1, self.devices))
        rows = masters[0].shape[0]
        start, count = self.attn_span(True)
        row = self.own * rows
        large = (row >= start) & (row < start + count)
        attn_chip = jnp.where(large, 2, 3)
        if rows % 16 == 0:
            in_smem = pl.BlockSpec(memory_space=pltpu.SMEM)
            in_vmem = pl.BlockSpec(memory_space=pltpu.VMEM)
            return call(
                finish_kernel,
                tuple(shape_of(master.shape, jnp.float32) for master in masters),
                (jnp.stack([self.kind, attn_chip]), *came, *masters),
                0,
                16,
                in_specs=[in_smem] + [in_vmem] * 7,
                out_specs=(in_vmem,) * 3,
            )
        return [
            updated(master, from_chip(came, self.kind, chip, master.shape[0]), rate)
            for master, chip, rate in zip(masters, (attn_chip, 0, 1), step_rates())
        ]


class Gather:
    def __init__(self, owners, gate_up, down, attn, sums=None):
        self.owners, self.sums = owners, sums
        parts = (gate_up, attn, down)
        self.gate_up, self.attn, self.down = [part.astype(jnp.bfloat16)[None] for part in parts]

    def send(self, parts, flip):
        flat = [part.reshape(-1, D) for part in parts]
        few = [] if self.sums is None else [split_rows(self.sums)]
        other = exchange(jnp.concatenate(flat + few, axis=0), flip, self.owners.devices)
        came, start = [], 0
        for part, rows in zip(parts, flat):
            came.append(other[start : start + rows.shape[0]].reshape(part.shape))
            start += rows.shape[0]
        return came, joined_rows(other[start:]) if few else 0.0

    def add(self, few):
        if self.sums is not None:
            self.sums = sum(few, self.sums)

    def widen(self, group):
        top = 1 << self.owners.top_bit
        gate_up, attn, down, few = [self.gate_up], [self.attn], [self.down], []
        for flip in flips_of(group):
            if flip & top:
                (more,), rest = self.send([self.down], flip)
            else:
                came, rest = self.send([self.gate_up, self.attn, self.down], flip)
                gate_up.append(came[0])
                attn.append(came[1])
                more = came[2]
            down.append(more)
            few.append(rest)
        joined = [jnp.concatenate(blocks, axis=0) for blocks in (gate_up, attn, down)]
        self.gate_up, self.attn, self.down = joined
        self.add(few)

    def route(self):
        kind = self.owners.kind
        gate_up = self.gate_up
        down = self.down.reshape(gate_up.shape)
        attn = jnp.pad(self.attn, ((0, 0), (0, self.attn.shape[1]), (0, 0)))
        wanted = lambda owner: jnp.where(owner == 0, gate_up, jnp.where(owner == 1, down, attn))
        blocks, few = [wanted(kind)], []
        for flip in (1, 2, 3):
            (came,), rest = self.send([wanted(kind ^ flip)], flip << 1)
            blocks.append(came)
            few.append(rest)
        self.add(few)
        self.blocks = jnp.stack(blocks, axis=1)

    def join(self):
        few = [split_rows(self.sums)]
        message = jnp.concatenate([self.blocks.reshape(-1, D)] + few, axis=0)
        self.message = exchange(message, 1, self.owners.devices)

    def flat(self):
        return self.blocks.reshape((-1,) + self.blocks.shape[2:])


def per_device(
    inputs,
    out_grad,
    lang_tags,
    attn_master,
    gate_up_master,
    down_master,
    attn_momentum,
    gate_up_momentum,
    down_momentum,
    norm_gains,
    gain_first,
    gain_second,
):
    devices = lax.axis_size(("dp", "sub"))
    device_place = lax.axis_index(("dp", "sub"))
    q_rows = HEADS * HEAD_DIM
    kv_rows = KV_HEADS * HEAD_DIM
    qkv_rows = q_rows + 2 * kv_rows
    tag_hot = (lang_tags[:, None] == jnp.arange(NUM_TAGS, dtype=jnp.int32)[None, :]).astype(
        jnp.float32
    )
    masters = (attn_master, gate_up_master, down_master)
    attn_low = attn_master.astype(jnp.bfloat16)
    gate_up_low = gate_up_master.astype(jnp.bfloat16)
    down_low = down_master.astype(jnp.bfloat16)
    tag_row = jnp.pad(tag_hot[:1], ((0, 0), (0, D - NUM_TAGS)))
    ffn_low = jnp.concatenate([gate_up_low, down_low], axis=0)
    place = device_place
    groups = bit_groups(devices)
    ffn_blocks = lax.all_gather(ffn_low, AXES)
    owners = Owners(place, devices)
    momenta = Gather(owners, gate_up_momentum, down_momentum, attn_momentum, tag_row)
    early = (inputs.astype(jnp.float32), momenta.gate_up, momenta.attn, momenta.down)
    attn_blocks = gather_hop(attn_low[None], groups[-1], devices)
    attn_blocks, early = lax.optimization_barrier((attn_blocks, early))
    hidden_in, momenta.gate_up, momenta.attn, momenta.down = early
    for group in groups[-2:0:-1]:
        attn_blocks = gather_hop(attn_blocks, group, devices)
    for group in groups[2:]:
        momenta.widen(group)
    other_blocks = exchange(attn_blocks, 1, devices)
    momenta.route()
    attn_blocks, other_blocks, momenta.blocks, momenta.sums = lax.optimization_barrier(
        (attn_blocks, other_blocks, momenta.blocks, momenta.sums)
    )
    momenta.join()
    length = inputs.shape[0]
    wide_cos, wide_sin, tall_cos, tall_sin = [jnp.asarray(t) for t in rotary_rows(length)]
    low, single = jnp.bfloat16, jnp.float32
    spot = place[None, None]
    core = bit_of(place, 0)[None, None]
    in_smem = pl.BlockSpec(memory_space=pltpu.SMEM)
    in_vmem = pl.BlockSpec(memory_space=pltpu.VMEM)
    even = down_low.shape[0] % 16 == 0
    attn_outs = (
        shape_of((length, q_rows), low),
        shape_of((length, kv_rows), low),
        shape_of((length, kv_rows), low),
        shape_of((length, D), low),
        shape_of((length, q_rows), low),
        shape_of((HEADS, 1, length), single),
        shape_of((HEADS, 1, length), single),
        shape_of((length, D), single),
        shape_of((length, D), low),
    )
    if even:
        pieces = (attn_blocks, other_blocks)
        attn_outs += (shape_of((devices // 2, 2) + attn_low.shape, low),)
    else:
        whole_weights = in_order(jnp.stack([attn_blocks, other_blocks], 1).reshape(devices, -1), place)
        pieces = (whole_weights.reshape(16, 2, -1, D),)
    queries, keys, values, normed_one, attended_low, peaks, totals, residual, normed_two, *attn_w = call(
        attention_kernel if even else whole_attention_kernel,
        attn_outs,
        (spot, hidden_in, *pieces, norm_gains, wide_cos, wide_sin),
        2 * length * D * 3 * (qkv_rows + q_rows),
        58,
        in_specs=[in_smem] + [in_vmem] * (4 + len(pieces)),
        out_specs=(in_vmem,) * len(attn_outs),
        scratch=(pltpu.VMEM((HEADS + 2 * KV_HEADS, length, HEAD_DIM), low),),
    )
    attn_weights = attn_w[0] if even else pieces[0]
    tag_count = momenta.sums + joined_rows(momenta.message[-2:])
    tags = jnp.concatenate([tag_row, tag_count], axis=0)
    gate_up_rows, down_rows = gate_up_low.shape[0], down_low.shape[0]
    if even:
        weights = (ffn_blocks,)
        weight_specs = [pl.BlockSpec(memory_space=pl.ANY)]
    else:
        ffn_weights = ffn_blocks
        ffn_rows = gate_up_rows + down_rows
        gate_up_weights = ffn_weights[:, :gate_up_rows].reshape(32, -1, D)
        down_weights = ffn_weights[:, gate_up_rows:ffn_rows].reshape(32, -1, D)
        gate_up_rows, down_rows = gate_up_weights.shape[1], down_weights.shape[1]
        weights = (gate_up_weights, down_weights)
        weight_specs = [in_vmem] * 2
    chunk = 768 if even else 384
    steps = FF // chunk
    held_once = dict(pipeline_mode=pl.Buffered(1))
    whole = lambda *shape: pl.BlockSpec(shape, lambda c: (0,) * len(shape), **held_once)
    part = lambda rows: pl.BlockSpec((chunk // rows, rows, D), lambda c: (c, 0, 0))
    if even:
        cut = (gate_up_rows + down_rows) * 9 // 16 // 16 * 16
        other_cut = gate_up_rows + down_rows - cut
        pairs = devices // 2
        grad_outs = tuple(
            shape_of((pairs, size, D), low) for size in (cut, other_cut) for _ in range(2)
        )
        grad_specs = (pl.BlockSpec(memory_space=pl.ANY),) * len(grad_outs)
        lazy = lambda *shape: pl.BlockSpec(memory_space=pl.ANY)
        held_scratch = (
            pltpu.VMEM(ffn_blocks.shape, low),
            pltpu.VMEM((length, D), single),
            pltpu.VMEM((length, q_rows), low),
            pltpu.VMEM(attn_weights.shape, low),
            *[pltpu.VMEM(out.shape, out.dtype) for out in grad_outs],
            pltpu.VMEM((D, length), low),
            pltpu.VMEM((length, D), single),
            pltpu.SemaphoreType.DMA((9 + 3 * steps,)),
        )
    else:
        grad_outs = (
            shape_of((16, gate_up_rows, D), single),
            shape_of((16, gate_up_rows, D), single),
            shape_of((32, down_rows, D), single),
        )
        grad_specs = (part(gate_up_rows), part(gate_up_rows), part(down_rows))
        lazy, held_scratch = whole, ()
    outputs, residual_grad, attended_grad, o_part, gain_two, *ffn_grads = call(
        partial(
            feed_kernel,
            devices=devices,
            gathered=even,
            gate_rows=gate_up_rows,
            down_rows=down_rows,
        ),
        (
            shape_of((D, length), low),
            shape_of((length, D), single),
            shape_of((length, q_rows), low),
            shape_of((q_rows, D), single),
            shape_of((1, D), single),
            *grad_outs,
        ),
        (
            spot,
            tags,
            normed_two,
            residual,
            out_grad.T,
            attended_low,
            *weights,
            attn_weights,
            norm_gains,
        ),
        2 * 3 * length * D * (3 * FF + q_rows),
        58,
        grid=(steps,),
        in_specs=[
            in_smem,
            whole(2, D),
            whole(length, D),
            lazy(length, D),
            whole(D, length),
            lazy(length, q_rows),
            *weight_specs,
            lazy(*attn_weights.shape),
            whole(2, D),
        ],
        out_specs=(
            lazy(D, length),
            lazy(length, D),
            whole(length, q_rows),
            whole(q_rows, D),
            whole(1, D),
            *grad_specs,
        ),
        scratch=(
            pltpu.VMEM((length, D), single),
            pltpu.VMEM((length, D), single),
            pltpu.VMEM((length, D), low),
            pltpu.VMEM((3, length, chunk), low),
        )
        + held_scratch,
    )
    bits = range(devices.bit_length() - 1)
    if even:
        first_held, first_sent, second_held, second_sent = ffn_grads
        sums = [
            Sums(first_held, place, devices, bits[1:], [exchange(first_sent, 1, devices)]),
            Sums(second_held, place, devices, bits[1:], [exchange(second_sent, 1, devices)]),
        ]
    else:
        gate_up_part = jnp.concatenate([g.reshape(-1, D) for g in ffn_grads[:2]], axis=0)
        sums = [
            Sums(gate_up_part.reshape(devices, -1, D), place, devices, bits),
            Sums(ffn_grads[2].reshape(devices, -1, D), place, devices, bits),
        ]
        for s in sums:
            s.hop(0)
    head_outs = (
        shape_of((length, q_rows // KV_HEADS), low),
        shape_of((length, HEAD_DIM), low),
        shape_of((length, HEAD_DIM), low),
    )
    head_grads = []
    for heads in ((0,), (1, 2)):
        head_grads += call(
            partial(heads_kernel, heads),
            head_outs * len(heads),
            (queries, keys, values, attended_grad, peaks, totals, tall_cos, tall_sin),
            2 * 2 * length * length * q_rows * len(heads),
            58,
            scratch=(
                pltpu.VMEM((length, HEAD_DIM), single),
                pltpu.VMEM((length, HEAD_DIM), single),
            ),
        )
        if heads == (0,):
            attended_grad, head_grads = after((attended_grad, head_grads), sums)
            sums[0].hop(1)
            sums[1].hop(2)
    normed_one, head_grads = after((normed_one, head_grads), sums)
    proj_parts = [head_grads[3 * head + kind] for kind in range(3) for head in range(KV_HEADS)]
    sums[0].hop(2)
    sums[1].hop(1)
    if even:
        grad_outs = (
            shape_of((pairs, attn_low.shape[0], D), low),
            shape_of((pairs, attn_low.shape[0], D), low),
        )
    else:
        grad_outs = (shape_of((qkv_rows + q_rows, D), single),)
    joined, *attn_grads = call(
        qkv_kernel,
        (shape_of((length, qkv_rows), low), *grad_outs),
        (core, *proj_parts, normed_one, o_part),
        2 * length * D * qkv_rows,
        58,
        in_specs=[in_smem] + [in_vmem] * 11,
        out_specs=(in_vmem,) * (1 + len(grad_outs)),
    )
    joined, attn_grads = after((joined, attn_grads), sums)
    if even:
        held, sent = attn_grads
        late = Sums(held, place, devices, bits[1:], [exchange(sent, 1, devices)])
    else:
        late = Sums(attn_grads[0].reshape(devices, -1, D), place, devices, bits)
        late.hop(0)
    feed_rows = [s.shape[0] for s in sums]
    feed_sums = Sums(
        jnp.concatenate([s.total() for s in sums], axis=1), place, devices, bits[3:]
    )
    feed_sums.hop(*groups[2])
    residual_grad = after(residual_grad, [late])
    late.hop(*groups[1])
    input_grad, gain_one = call(
        input_kernel,
        (shape_of((D, length), low), shape_of((1, D), single)),
        (joined, attn_weights, hidden_in, residual_grad, norm_gains),
        2 * length * D * qkv_rows,
        58,
    )
    input_grad = after(input_grad, [late, feed_sums])
    for group in groups[3:]:
        feed_sums.hop(*group)
    feed_total = feed_sums.total()[0]
    if even:
        gate_up_sum = feed_total[:gate_up_rows]
        down_sum = feed_total[gate_up_rows:]
    else:
        gate_up_sum, down_sum = feed_total[: feed_rows[0]], feed_total[feed_rows[0] :]
    for group in groups[2:]:
        late.hop(*group)
    attn_sum = late.total()[0]
    squares = sum(
        jnp.sum(part * part, axis=0, keepdims=True) for part in (attn_sum, gate_up_sum, down_sum)
    )
    small_sums = jnp.concatenate([gain_one, gain_two, squares], axis=0)
    gather = Gather(owners, gate_up_sum, down_sum, attn_sum, small_sums)
    for group in groups[2:]:
        gather.widen(group)
    gather.route()
    gather.join()
    param_count = (qkv_rows + q_rows + 3 * FF) * D + 2 * D
    limit = CLIP_SCALE * math.sqrt(devices * length * param_count)
    down_count = down_low.shape[0]
    parts = (attn_sum, gate_up_sum, down_sum, attn_momentum, gate_up_momentum, down_momentum)
    solved = owners.solve(gather, momenta, parts, limit, down_count)
    solved, (gain_grad, grad_norm, *new) = solved[:4], solved[4:]
    attn_grad, gate_up_grad, down_grad, attn_moment, gate_up_moment, down_moment = new
    grad_norm = grad_norm[0, 0]
    new_masters = owners.spread(solved, masters)
    first_new = BETA_FIRST * gain_first + (1.0 - BETA_FIRST) * gain_grad
    second_new = BETA_SECOND * gain_second + (1.0 - BETA_SECOND) * gain_grad * gain_grad
    gains_new = norm_gains - GAIN_RATE * (first_new / (1.0 - BETA_FIRST**STEP_NUMBER)) / (
        jnp.sqrt(second_new / (1.0 - BETA_SECOND**STEP_NUMBER)) + ADAM_EPS
    )
    return (
        outputs.T,
        input_grad.T,
        attn_grad,
        gate_up_grad,
        down_grad,
        grad_norm,
        attn_moment,
        gate_up_moment,
        down_moment,
        new_masters[0],
        new_masters[1],
        new_masters[2],
        gain_grad,
        first_new,
        second_new,
        gains_new,
    )


def solution(mesh):
    placed = (
        P(("dp", "sub"), None),
        P(("dp", "sub"), None),
        P(("dp", "sub")),
        P(("dp", "sub"), None),
        P(("dp", "sub"), None),
        P(("dp", "sub"), None),
        P(("dp", "sub"), None),
        P(("dp", "sub"), None),
        P(("dp", "sub"), None),
        P(),
        P(),
        P(),
    )
    return jax.shard_map(
        per_device,
        mesh=mesh,
        in_specs=placed,
        out_specs=(
            P(("dp", "sub"), None),
            P(("dp", "sub"), None),
            P(("dp", "sub"), None),
            P(("dp", "sub"), None),
            P(("dp", "sub"), None),
            P(),
            P(("dp", "sub"), None),
            P(("dp", "sub"), None),
            P(("dp", "sub"), None),
            P(("dp", "sub"), None),
            P(("dp", "sub"), None),
            P(("dp", "sub"), None),
            P(),
            P(),
            P(),
            P(),
        ),
        check_vma=False,
    )
```
